512 devices in a mesh: grid: 2 (over core), lat: 8 (over z_lo), lon: 32 (over x, y, z_hi).
Axes of the slice: x: 4, y: 4, z: 16 (z_hi: 2, z_lo: 8; z = z_hi * 8 + z_lo), core: 2. Of those that a mesh axis runs over, the one named last changes fastest.
Arguments:
- velocity: float32 [2, 3, 8, 1024, 1024], P('grid', None, None, 'lon', 'lat'), may hold values from -6 to 6
- magnetic: float32 [2, 3, 8, 1024, 1024], P('grid', None, None, 'lon', 'lat'), may hold values from -6 to 6
- pair_rows: int32 [2, 8, 32, 32], P('grid', 'lat', 'lon'), may hold values from 0 to 16, as said below
- send_cell: int32 [2, 8, 32, 512], P('grid', 'lat', 'lon'), may hold values from 0 to 4095
- send_weight: float32 [2, 8, 32, 512], P('grid', 'lat', 'lon'), may hold values from 0.25 to 1
- cycle_slot: int32 [2, 8, 32, 512], P('grid', 'lat', 'lon'), may hold values from 0 to 127
Outputs:
- new_velocity: float32 [2, 3, 8, 1024, 1024], P('grid', None, None, 'lon', 'lat')
- new_magnetic: float32 [2, 3, 8, 1024, 1024], P('grid', None, None, 'lon', 'lat')
- cycle_values: float32 [2, 8, 32, 48, 128], P('grid', 'lat', 'lon')
The draws below stay inside these ranges and needn't reach their ends.
Inputs may be any that keep to these rules, and one draw needn't show every extreme that they name: `pair_rows`: at most 16 rows go from one donor block to one longitude block; the first and the last longitude block receive exactly 16 from every donor block. `send_cell`: A cell of the donor block.
All inputs are finite; a program needn't handle non-finite values.
Results may differ from the reference program's by a relative error of at most 0.0001.
Values sent between devices are 32-bit elements; how exact they have to be, the bound alone decides.
No kernel may reach another device: no remote copies, remote signals or barrier semaphores. Data moves between devices by JAX's collectives and lax.ppermute only.
A program may use at most 64 MiB of HBM per device.

```python
import math
import jax
import jax.numpy as jnp
from jax import lax

R = 8
CT = 128
CP = 32
CAP = 16
CYCLE = 128
LAT_BLOCKS = 8
LON_BLOCKS = 32
NT = 1024
NP = 1024
SEND = 512


def draw_pair_rows(key, part):
    key = jax.random.fold_in(key, 7)
    base = jax.random.randint(key, (2, LAT_BLOCKS, LON_BLOCKS, LON_BLOCKS), CAP // 2, CAP + 1)
    target = jnp.arange(LON_BLOCKS, dtype=jnp.int32)[None, None, None, :]
    edge = (target == 0) | (target == LON_BLOCKS - 1)
    return jnp.where(edge, CAP, base).astype(jnp.int32)


def set_ends(entries, own_key, smallest, top_value):
    longest = entries.shape.index(max(entries.shape))
    spots = []
    for shift in (0, 1):
        where = [jax.random.randint(jax.random.fold_in(own_key, axis), (), 0, length) for axis, length in enumerate(entries.shape)]
        where[longest] = (where[longest] + shift) % entries.shape[longest]
        spots.append(tuple(where))
    return entries.at[spots[0]].set(smallest).at[spots[1]].set(top_value)


def block_scale(key, dims, cuts, least, largest):
    factor_of = 1.0
    for position, blocks in cuts:
        heights = jax.random.uniform(jax.random.fold_in(jax.random.fold_in(key, 6), position), (blocks,), jnp.float32, least / len(cuts), largest / len(cuts))
        factor_of = factor_of * jnp.repeat(jnp.exp(heights), dims[position] // blocks).reshape((-1,) + (1,) * (len(dims) - 1 - position))
    return factor_of


def noise(own_key, extent, scale, reach, pieces=(), held_as=jnp.bfloat16):
    level = block_scale(own_key, extent, pieces, -0.22, 0.18) if pieces else 1.0
    array = jax.random.normal(own_key, extent, jnp.float32) * scale * level
    return jnp.minimum(jnp.maximum(array, -reach), reach).astype(held_as)


def setup_inputs(seed: int = 0) -> dict:
    keys = jax.random.split(jax.random.key(seed), 7)
    velocity = noise(keys[0], (2, 3, R, NP, NT), 1.0, 6.0, ((0, 2), (3, 32), (4, 8)), jnp.float32)
    magnetic = noise(keys[1], (2, 3, R, NP, NT), 1.0, 6.0, ((0, 2), (3, 32), (4, 8)), jnp.float32)
    pair_rows = draw_pair_rows(jax.random.fold_in(keys[6], 71), 0)
    send_cell = set_ends(jax.random.randint(keys[3], (2, LAT_BLOCKS, LON_BLOCKS, SEND), 0, CP * CT), jax.random.fold_in(keys[3], 1), 0, (CP * CT) - 1).astype(jnp.int32)
    send_weight = jnp.clip(0.25 + 0.75 * jax.random.uniform(keys[4], (2, LAT_BLOCKS, LON_BLOCKS, SEND), jnp.float32) ** block_scale(keys[4], (2, LAT_BLOCKS, LON_BLOCKS, SEND), ((0, 2), (1, 8), (2, 32)), -0.2, 0.2), 0.25, 1.0)
    cycle_slot = set_ends(jax.random.randint(keys[5], (2, LAT_BLOCKS, LON_BLOCKS, SEND), 0, CYCLE), jax.random.fold_in(keys[5], 1), 0, CYCLE - 1).astype(jnp.int32)
    return {"velocity": velocity, "magnetic": magnetic, "pair_rows": pair_rows, "send_cell": send_cell, "send_weight": send_weight, "cycle_slot": cycle_slot}


inner_radius = 0.6
smag_const = 0.2
aniso_weight = 0.8
turb_prandtl = 0.7
courant = 0.2
sym_index = ((0, 1, 2), (1, 3, 4), (2, 4, 5))
flux_pairs = ((0, 0), (0, 1), (0, 2), (1, 1), (1, 2), (2, 2))

def coefficients(theta_index, total_t, total_p, levels):
    theta_step = 0.5 * math.pi / total_t
    phi_step = 1.5 * math.pi / total_p
    spacing = inner_radius * theta_step
    radius = inner_radius + (jnp.arange(levels, dtype=jnp.float32) + 0.5) * spacing
    theta = 0.25 * math.pi + (theta_index.astype(jnp.float32) + 0.5) * theta_step
    coef_theta = (0.5 / (theta_step * radius))[:, None, None]
    coef_phi = 0.5 / (phi_step * radius[:, None, None] * jnp.sin(theta)[None, None, :])
    return (coef_theta, coef_phi, spacing, courant * spacing)

def radial(field, spacing):
    inner = (field[:, 2:] - field[:, :-2]) * (0.5 / spacing)
    lower = (field[:, 1:2] - field[:, :1]) * (1.0 / spacing)
    upper = (field[:, -1:] - field[:, -2:-1]) * (1.0 / spacing)
    return jnp.concatenate([lower, inner, upper], axis=1)

def derivatives(padded, coefs):
    coef_theta, coef_phi, spacing, time_step = coefs
    center = padded[:, :, 1:-1, 1:-1]
    along_theta = (padded[:, :, 1:-1, 2:] - padded[:, :, 1:-1, :-2]) * coef_theta
    along_phi = (padded[:, :, 2:, 1:-1] - padded[:, :, :-2, 1:-1]) * coef_phi
    return (center, (radial(center, spacing), along_theta, along_phi))

def fluxes(padded, coefs):
    spacing = coefs[2]
    center, grads = derivatives(padded, coefs)
    speed = center[0:3]
    field = center[3:6]
    grad_u = [[grads[col][row] for col in range(3)] for row in range(3)]
    grad_b = [[grads[col][row + 3] for col in range(3)] for row in range(3)]
    strain = [[0.5 * (grad_u[row][col] + grad_u[col][row]) for col in range(3)] for row in range(3)]
    magnitude = jnp.sqrt(2.0 * sum((strain[row][col] * strain[row][col] for row in range(3) for col in range(3))))
    viscous = (smag_const * spacing) ** 2 * magnitude
    field_sq = field[0] * field[0] + field[1] * field[1] + field[2] * field[2]
    scaling = 1.0 / jnp.sqrt(field_sq + 1.0)
    unit = [field[comp] * scaling for comp in range(3)]
    aligned = sum((unit[row] * strain[row][col] * unit[col] for row in range(3) for col in range(3)))
    parts = []
    for row, col in flux_pairs:
        value = speed[row] * speed[col] - field[row] * field[col]
        value = value - 2.0 * viscous * (strain[row][col] - aniso_weight * unit[row] * unit[col] * aligned)
        if row == col:
            value = value + 0.5 * field_sq
        parts.append(value)
    current = [grad_b[2][1] - grad_b[1][2], grad_b[0][2] - grad_b[2][0], grad_b[1][0] - grad_b[0][1]]
    cross = [speed[1] * field[2] - speed[2] * field[1], speed[2] * field[0] - speed[0] * field[2], speed[0] * field[1] - speed[1] * field[0]]
    for comp in range(3):
        parts.append(cross[comp] - viscous / turb_prandtl * current[comp])
    return jnp.stack(parts)

def advance(state, flux_pad, coefs):
    time_step = coefs[3]
    unused, grads = derivatives(flux_pad, coefs)
    result = []
    for row in range(3):
        spread = grads[0][sym_index[row][0]] + grads[1][sym_index[row][1]] + grads[2][sym_index[row][2]]
        result.append(state[row] - time_step * spread)
    curls = [grads[1][8] - grads[2][7], grads[2][6] - grads[0][8], grads[0][7] - grads[1][6]]
    for row in range(3):
        result.append(state[row + 3] + time_step * curls[row])
    return jnp.stack(result)

def reference(velocity, magnetic, pair_rows, send_cell, send_weight, cycle_slot):
    coefs = coefficients(jnp.arange(NT, dtype=jnp.int32), NT, NP, R)
    widths = ((0, 0), (0, 0), (1, 1), (1, 1))
    results = []
    for comp in range(2):
        state = jnp.concatenate([velocity[comp], magnetic[comp]], axis=0)
        flux = fluxes(jnp.pad(state, widths), coefs)
        results.append(advance(state, jnp.pad(flux, widths), coefs))
    new_state = jnp.stack(results)
    lat_block = jnp.arange(LAT_BLOCKS, dtype=jnp.int32)[None, :, None, None]
    lon_block = jnp.arange(LON_BLOCKS, dtype=jnp.int32)[None, None, :, None]
    row_p = lon_block * CP + send_cell // CT
    row_t = lat_block * CT + send_cell % CT
    flat_index = (row_p * NT + row_t).astype(jnp.int32)
    bucket_pos = jnp.arange(SEND, dtype=jnp.int32) % CAP
    live = bucket_pos[None, None, None, :] < jnp.repeat(pair_rows, CAP, axis=3)
    scale = jnp.where(live, send_weight, jnp.float32(0.0))
    donated = []
    for comp in range(2):
        flat = new_state[comp].reshape(6 * R, NP * NT)
        taken = jnp.take(flat, flat_index[comp].reshape(-1), axis=1)
        taken = taken.reshape(6 * R, LAT_BLOCKS, LON_BLOCKS, SEND) * scale[comp][None]
        taken = taken.reshape(6 * R, LAT_BLOCKS, LON_BLOCKS, LON_BLOCKS, CAP)
        onehot = (cycle_slot[comp][..., None] == jnp.arange(CYCLE, dtype=jnp.int32)).astype(jnp.float32)
        onehot = onehot.reshape(LAT_BLOCKS, LON_BLOCKS, LON_BLOCKS, CAP, CYCLE)
        donated.append(jnp.einsum('fijkc,ijkcm->ikfm', taken, onehot, precision=lax.Precision.HIGHEST))
    cycle_values = jnp.stack([donated[1], donated[0]])
    return (new_state[:, 0:3], new_state[:, 3:6], cycle_values)
```

```python
import math

import jax
import jax.numpy as jnp
from jax import lax
from jax.experimental import pallas as pl
from jax.experimental.pallas import tpu as pltpu
from jax.sharding import PartitionSpec as P

CAP = 16
CYCLE = 128
LEVELS = 8
CELLS_P = 32
CELLS_T = 128

inner_radius = 0.6
smag_const = 0.2
aniso_weight = 0.8
turb_prandtl = 0.7
courant = 0.2

ALONG_R = (0, 1, 2, 7, 8)
ALONG_T = (1, 3, 4, 6, 8)
ALONG_P = (2, 4, 5, 6, 7)
F32 = jnp.float32


def lanes_of(shape):
    return lax.broadcasted_iota(jnp.int32, shape, len(shape) - 1)


def rows_of(shape):
    return lax.broadcasted_iota(jnp.int32, shape, len(shape) - 2)


def pick(vel_ref, mag_ref, comp):
    return (vel_ref, comp) if comp < 3 else (mag_ref, comp - 3)


def edges_kernel(vel_ref, mag_ref, low_ref, high_ref, first_ref, last_ref):
    pair = lanes_of((CELLS_P, CELLS_T)) // 2
    low = jnp.zeros((CELLS_P, CELLS_T), F32)
    high = jnp.zeros((CELLS_P, CELLS_T), F32)
    for comp in range(6):
        ref, index = pick(vel_ref, mag_ref, comp)
        for level in range(LEVELS):
            place = 16 * comp + 2 * level
            block = ref[0, index, level]
            if place:
                block = pltpu.roll(block, place, 1)
            low = jnp.where(pair == place // 2, block, low)
            high = jnp.where(pair == (place // 2 - 1) % (CELLS_T // 2), block, high)
        first_ref[comp] = ref[0, index, :, 0, :]
        last_ref[comp] = ref[0, index, :, CELLS_P - 1, :]
        if comp < 5:
            first_ref[6 + comp] = ref[0, index, :, 1, :]
            last_ref[6 + comp] = ref[0, index, :, CELLS_P - 2, :]
    low_ref[...] = low
    high_ref[...] = pltpu.roll(high, 2, 1)
    first_ref[11] = jnp.zeros((LEVELS, CELLS_T), F32)
    last_ref[11] = jnp.zeros((LEVELS, CELLS_T), F32)


def strips_kernel(place_ref, below_ref, above_ref, first_ref, last_ref, far_ref, near_ref):
    odd = place_ref[1] % 2

    def corner(row):
        shape = (LEVELS, CELLS_T)
        below = jnp.broadcast_to(below_ref[row : row + 1, :], shape)
        above = jnp.broadcast_to(above_ref[row : row + 1, :], shape)
        return jnp.where(rows_of(shape) == 0, below, above)

    @pl.when(odd == 0)
    def _():
        far_ref[...] = first_ref[...]
        far_ref[11] = corner(0)
        near_ref[0:12] = last_ref[...]
        near_ref[11] = corner(CELLS_P - 1)

    @pl.when(odd == 1)
    def _():
        far_ref[...] = last_ref[...]
        far_ref[11] = corner(CELLS_P - 1)
        near_ref[0:12] = first_ref[...]
        near_ref[11] = corner(0)

    near_ref[12:24] = jnp.zeros((12, LEVELS, CELLS_T), F32)


def flux_of(center, grad_r, grad_t, grad_p, spacing, wanted):
    u0, u1, u2, b0, b1, b2 = center
    s00, s11, s22 = grad_r[0], grad_t[1], grad_p[2]
    d01 = grad_t[0] + grad_r[1]
    d02 = grad_p[0] + grad_r[2]
    d12 = grad_p[1] + grad_t[2]
    squares = 2.0 * (s00 * s00 + s11 * s11 + s22 * s22) + (d01 * d01 + d02 * d02 + d12 * d12)
    viscous = jnp.sqrt(squares) * ((smag_const * spacing) ** 2)
    q00, q11, q22 = b0 * b0, b1 * b1, b2 * b2
    field_sq = q00 + q11 + q22
    inverse = 1.0 / (field_sq + 1.0)
    q01, q02, q12 = b0 * b1, b0 * b2, b1 * b2
    aligned = q00 * s00 + q11 * s11 + q22 * s22 + (q01 * d01 + q02 * d02 + q12 * d12)
    weight = (2.0 * aniso_weight) * viscous * aligned * inverse * inverse - 1.0
    half = 0.5 * field_sq
    twice = viscous + viscous
    ratio = viscous * (1.0 / turb_prandtl)
    result = {}
    for chan in wanted:
        if chan == 0:
            result[0] = u0 * u0 + q00 * weight - twice * s00 + half
        elif chan == 1:
            result[1] = u0 * u1 + q01 * weight - viscous * d01
        elif chan == 2:
            result[2] = u0 * u2 + q02 * weight - viscous * d02
        elif chan == 3:
            result[3] = u1 * u1 + q11 * weight - twice * s11 + half
        elif chan == 4:
            result[4] = u1 * u2 + q12 * weight - viscous * d12
        elif chan == 5:
            result[5] = u2 * u2 + q22 * weight - twice * s22 + half
        elif chan == 6:
            result[6] = u1 * b2 - u2 * b1 - ratio * (grad_t[5] - grad_p[4])
        elif chan == 7:
            result[7] = u2 * b0 - u0 * b2 - ratio * (grad_p[3] - grad_r[5])
        else:
            result[8] = u0 * b1 - u1 * b0 - ratio * (grad_r[4] - grad_t[3])
    return result


def section_kernel(
    spacing,
    theta_step,
    phi_step,
    lat_blocks,
    lon_blocks,
    place_ref,
    vel_ref,
    mag_ref,
    low_ref,
    high_ref,
    below_ref,
    above_ref,
    first_ref,
    last_ref,
    side_ref,
    rows_ref,
    cell_ref,
    weight_ref,
    slot_ref,
    new_vel_ref,
    new_mag_ref,
    send_ref,
    flux_ref,
    edge_t_ref,
    edge_p_ref,
    taken_ref,
):
    lat = place_ref[0]
    lon = place_ref[1]
    odd_block = lon % 2
    time_step = courant * spacing
    wide = (CELLS_P, CELLS_T)
    flat = (LEVELS, CELLS_T)
    lane = lanes_of(wide)
    row = rows_of(wide)
    lane_flat = lanes_of(flat)
    row_flat = rows_of(flat)
    first_lane, last_lane = lane == 0, lane == CELLS_T - 1
    first_row, last_row = row == 0, row == CELLS_P - 1

    def radius(level):
        return inner_radius + (level.astype(F32) + 0.5) * spacing

    def inverse_sine(index):
        return 1.0 / jnp.sin(0.25 * math.pi + (index.astype(F32) + 0.5) * theta_step)

    first_t = lat * CELLS_T
    own_sine = inverse_sine(first_t + lanes_of((8, CELLS_T)))

    base = (12 * (1 - odd_block), 12 * odd_block)

    is_below = lane % 2 == 1
    level_of = (lane % 16) // 2
    below, above = below_ref[...], above_ref[...]
    beside = jnp.where(is_below, below, above)

    def swapped(block):
        return jnp.where(is_below, pltpu.roll(block, 1, 1), pltpu.roll(block, CELLS_T - 1, 1))

    def corner(side):
        tile = side_ref[base[side] + 11]
        return jnp.where(lane_flat[0:1] % 2 == 1, tile[0:1], tile[1:2])

    corners = (corner(0), corner(1))
    inverse_r = 1.0 / radius(level_of)
    own_step = jnp.where((level_of == 0) | (level_of == LEVELS - 1), 1.0 / spacing, 0.5 / spacing)
    up = jnp.where(level_of == LEVELS - 1, beside, pltpu.roll(beside, CELLS_T - 2, 1))
    down = jnp.where(level_of == 0, beside, pltpu.roll(beside, 2, 1))
    pack_r = (up - down) * own_step
    inner = jnp.where(is_below, high_ref[...], low_ref[...])
    outer = jnp.where(is_below, above, below)
    pack_t = swapped(inner - outer) * (
        jnp.where(is_below, 0.5 / theta_step, -0.5 / theta_step) * inverse_r
    )
    t_index = first_t + jnp.where(is_below, -1, CELLS_T)
    up = jnp.where(last_row, corners[1], pltpu.roll(beside, CELLS_P - 1, 0))
    down = jnp.where(first_row, corners[0], pltpu.roll(beside, 1, 0))
    pack_p = (up - down) * (inverse_sine(t_index) * inverse_r * (0.5 / phi_step))

    def spread(block):
        return [block if comp == 0 else pltpu.roll(block, CELLS_T - 16 * comp, 1) for comp in range(6)]

    edge = flux_of(
        spread(beside), spread(pack_r), spread(pack_t), spread(pack_p), spacing, ALONG_T
    )
    outside = (is_below & (lat == 0)) | ((lane % 2 == 0) & (lat == lat_blocks - 1))
    for slot, chan in enumerate(ALONG_T):
        edge_t_ref[slot] = jnp.where(outside, 0.0, edge[chan])

    level_step = jnp.where(
        (row_flat == 0) | (row_flat == LEVELS - 1), 1.0 / spacing, 0.5 / spacing
    )
    inverse_flat = 1.0 / radius(row_flat)
    for side in range(2):
        inner_ref = first_ref if side == 0 else last_ref
        sign = 1.0 if side == 0 else -1.0
        center = [side_ref[base[side] + comp] for comp in range(6)]
        corner_row = jnp.broadcast_to(corners[side], flat)
        grad_r, grad_t, grad_p = [], [], []
        for comp in range(6):
            block = center[comp]
            up = jnp.where(row_flat == LEVELS - 1, block, pltpu.roll(block, LEVELS - 1, 0))
            down = jnp.where(row_flat == 0, block, pltpu.roll(block, 1, 0))
            grad_r.append((up - down) * level_step)
            spot = 16 * comp + 2 * row_flat
            before = jnp.sum(
                jnp.where(lane_flat == spot + 1, corner_row, 0.0), axis=1, keepdims=True
            )
            after = jnp.sum(jnp.where(lane_flat == spot, corner_row, 0.0), axis=1, keepdims=True)
            up = jnp.where(lane_flat == CELLS_T - 1, after, pltpu.roll(block, CELLS_T - 1, 1))
            down = jnp.where(lane_flat == 0, before, pltpu.roll(block, 1, 1))
            grad_t.append((up - down) * (inverse_flat * (0.5 / theta_step)))
            if comp < 5:
                gap = inner_ref[comp] - side_ref[base[side] + 6 + comp]
                grad_p.append(gap * (own_sine * inverse_flat * (sign * 0.5 / phi_step)))
            else:
                grad_p.append(None)
        edge = flux_of(center, grad_r, grad_t, grad_p, spacing, ALONG_P)
        outside = lon == (0 if side == 0 else lon_blocks - 1)
        for slot, chan in enumerate(ALONG_P):
            edge_p_ref[side, slot] = jnp.where(outside, 0.0, edge[chan])

    def shifts(level, scale):
        low_level = jnp.maximum(level - 1, 0)
        high_level = jnp.minimum(level + 1, LEVELS - 1)
        ends = (level == 0) | (level == LEVELS - 1)
        step_r = jnp.where(ends, scale / spacing, 0.5 * scale / spacing)
        inverse = 1.0 / radius(jnp.full((8, CELLS_T), level, jnp.int32))
        step_t = (inverse * (0.5 * scale / theta_step))[0:1]
        step_p = (own_sine * inverse * (0.5 * scale / phi_step))[0:1]
        return low_level, high_level, step_r, step_t, step_p

    def along_t(block, ends, step):
        up = jnp.where(last_lane, ends, pltpu.roll(block, CELLS_T - 1, 1))
        down = jnp.where(first_lane, ends, pltpu.roll(block, 1, 1))
        return (up - down) * step

    def along_p(block, before, after, step):
        up = jnp.where(last_row, after, pltpu.roll(block, CELLS_P - 1, 0))
        down = jnp.where(first_row, before, pltpu.roll(block, 1, 0))
        return (up - down) * step

    def make_flux(level, carry):
        low_level, high_level, step_r, step_t, step_p = shifts(level, 1.0)
        center, grad_r, grad_t, grad_p = [], [], [], []
        for comp in range(6):
            ref, index = pick(vel_ref, mag_ref, comp)
            block = ref[0, index, level]
            center.append(block)
            grad_r.append((ref[0, index, high_level] - ref[0, index, low_level]) * step_r)
            ends = pltpu.roll(beside, 2 * CELLS_T - 1 - 16 * comp - 2 * level, 1)
            grad_t.append(along_t(block, ends, step_t))
            before = side_ref[base[0] + comp, pl.ds(level, 1), :]
            after = side_ref[base[1] + comp, pl.ds(level, 1), :]
            grad_p.append(along_p(block, before, after, step_p))
        flux = flux_of(center, grad_r, grad_t, grad_p, spacing, range(9))
        for chan in range(9):
            flux_ref[chan, level] = flux[chan]
        return carry

    lax.fori_loop(0, LEVELS, make_flux, 0)

    def advance(level, carry):
        low_level, high_level, step_r, step_t, step_p = shifts(level, time_step)

        def d_r(chan):
            return (flux_ref[chan, high_level] - flux_ref[chan, low_level]) * step_r

        def d_t(chan):
            slot = ALONG_T.index(chan)
            ends = pltpu.roll(edge_t_ref[slot], CELLS_T - 1 - 2 * level, 1)
            return along_t(flux_ref[chan, level], ends, step_t)

        def d_p(chan):
            slot = ALONG_P.index(chan)
            before = edge_p_ref[0, slot, pl.ds(level, 1), :]
            after = edge_p_ref[1, slot, pl.ds(level, 1), :]
            return along_p(flux_ref[chan, level], before, after, step_p)

        new_vel_ref[0, 0, level] = vel_ref[0, 0, level] - (d_r(0) + d_t(1) + d_p(2))
        new_vel_ref[0, 1, level] = vel_ref[0, 1, level] - (d_r(1) + d_t(3) + d_p(4))
        new_vel_ref[0, 2, level] = vel_ref[0, 2, level] - (d_r(2) + d_t(4) + d_p(5))
        new_mag_ref[0, 0, level] = mag_ref[0, 0, level] + (d_t(8) - d_p(7))
        new_mag_ref[0, 1, level] = mag_ref[0, 1, level] + (d_p(6) - d_r(8))
        new_mag_ref[0, 2, level] = mag_ref[0, 2, level] + (d_r(7) - d_t(6))
        return carry

    lax.fori_loop(0, LEVELS, advance, 0)

    slots_total = cell_ref.shape[-1]
    chunks = slots_total // CELLS_T
    rows_wide = jnp.broadcast_to(rows_ref[0, 0].astype(F32), (8, lon_blocks))
    owner = lanes_of((lon_blocks, slots_total)) // CAP == rows_of((lon_blocks, slots_total))
    counts = jnp.dot(rows_wide, owner.astype(F32), preferred_element_type=F32)
    bucket = lanes_of((8, slots_total)) % CAP
    live = bucket < (counts + 0.5).astype(jnp.int32)
    scale = jnp.where(live, jnp.broadcast_to(weight_ref[0, 0], (8, slots_total)), 0.0)
    cells = jnp.broadcast_to(cell_ref[0, 0], (8, slots_total))
    cell_t = cells % CELLS_T
    cell_p = cells // CELLS_T
    scale = jnp.where(cell_p % 8 == rows_of(cells.shape), scale, 0.0)
    group = cell_p // 8
    taken_ref[6:8] = jnp.zeros((2, LEVELS, slots_total), F32)
    taken_ref[6, 0:1] = slot_ref[0, 0].astype(F32)
    for start, ref in ((0, new_vel_ref), (3, new_mag_ref)):

        def take(comp, carry, start=start, ref=ref):
            for level in range(LEVELS):
                block = ref[0, comp, level]
                for chunk in range(chunks):
                    part = slice(chunk * CELLS_T, (chunk + 1) * CELLS_T)
                    where_t = cell_t[:, part]
                    total = jnp.zeros((8, CELLS_T), F32)
                    for step in range(CELLS_P // 8):
                        got = jnp.take_along_axis(
                            block[8 * step : 8 * step + 8],
                            where_t,
                            axis=1,
                            mode="promise_in_bounds",
                        )
                        total = jnp.where(group[:, part] == step, got, total)
                    total = jnp.sum(total * scale[:, part], axis=0, keepdims=True)
                    taken_ref[start + comp, level : level + 1, part] = total
            return carry

        lax.fori_loop(0, 3, take, 0)

    for chunk in range(chunks):
        part = taken_ref[:, :, chunk * CELLS_T : (chunk + 1) * CELLS_T].reshape(64, CELLS_T)
        both = jnp.concatenate([part, pltpu.roll(part, CELLS_T - 8, 1)], axis=0)
        turned = jnp.transpose(both)
        for block in range(8):
            send_ref[chunk * 8 + block] = turned[16 * block : 16 * block + 8]


def collect_kernel(got_ref, out_ref):
    rows = got_ref.shape[0] * got_ref.shape[1]
    got = got_ref[...].reshape(rows, CELLS_T)
    total = jnp.zeros((48, CYCLE), F32)
    for start in (0, 64):
        slot = got[:, start + 48 : start + 49].astype(jnp.int32)
        onehot = (slot == lanes_of((rows, CYCLE))).astype(F32)
        part = lax.dot_general(
            got,
            onehot,
            (((0,), (0,)), ((), ())),
            precision=lax.Precision.HIGHEST,
            preferred_element_type=F32,
        )
        total = total + part[start : start + 48]
    out_ref[0, 0, 0] = total


VMEM = pl.BlockSpec(memory_space=pltpu.VMEM)
SMEM = pl.BlockSpec(memory_space=pltpu.SMEM)
LIMIT = pltpu.CompilerParams(vmem_limit_bytes=32 * 1024 * 1024)


def tiles(*shape):
    return jax.ShapeDtypeStruct(shape, F32)


def edges(velocity, magnetic):
    pack = tiles(CELLS_P, CELLS_T)
    strip = tiles(12, LEVELS, CELLS_T)
    return pl.pallas_call(
        edges_kernel,
        in_specs=[VMEM] * 2,
        out_specs=[VMEM] * 4,
        out_shape=[pack, pack, strip, strip],
        compiler_params=LIMIT,
        name="edges",
    )(velocity, magnetic)


def local(velocity, magnetic, pair_rows, send_cell, send_weight, cycle_slot):
    lat_blocks, lon_blocks = lax.axis_size("lat"), lax.axis_size("lon")
    theta_step = 0.5 * math.pi / (lat_blocks * CELLS_T)
    phi_step = 1.5 * math.pi / (lon_blocks * CELLS_P)
    spacing = inner_radius * theta_step
    place = jnp.stack([lax.axis_index("lat"), lax.axis_index("lon")]).astype(jnp.int32)
    low, high, first, last = edges(velocity, magnetic)
    below = lax.ppermute(high, "lat", [(i, i + 1) for i in range(lat_blocks - 1)])
    above = lax.ppermute(low, "lat", [(i + 1, i) for i in range(lat_blocks - 1)])
    far, near = pl.pallas_call(
        strips_kernel,
        in_specs=[SMEM] + [VMEM] * 4,
        out_specs=[VMEM] * 2,
        out_shape=[tiles(12, LEVELS, CELLS_T), tiles(24, LEVELS, CELLS_T)],
        name="strips",
    )(place, below, above, first, last)
    hop = [(i, i - 2 if i % 2 == 0 else i + 2) for i in range(lon_blocks)]
    hop = [(i, j) for i, j in hop if 0 <= j < lon_blocks]
    relayed = lax.ppermute(far, "lon", hop)
    sides = lax.dynamic_update_slice(near, relayed, (12, 0, 0))
    sides = lax.ppermute(sides, "lon", [(i, i ^ 1) for i in range(lon_blocks)])
    slots_total = send_cell.shape[-1]

    def section(*refs):
        section_kernel(spacing, theta_step, phi_step, lat_blocks, lon_blocks, *refs)

    new_velocity, new_magnetic, payload = pl.pallas_call(
        section,
        in_specs=[SMEM] + [VMEM] * 13,
        out_specs=[VMEM] * 3,
        out_shape=[
            tiles(*velocity.shape),
            tiles(*magnetic.shape),
            tiles(lon_blocks, 8, CELLS_T),
        ],
        scratch_shapes=[
            pltpu.VMEM((9, LEVELS, CELLS_P, CELLS_T), F32),
            pltpu.VMEM((5, CELLS_P, CELLS_T), F32),
            pltpu.VMEM((2, 5, LEVELS, CELLS_T), F32),
            pltpu.VMEM((8, LEVELS, slots_total), F32),
        ],
        compiler_params=LIMIT,
        name="section",
    )(
        place,
        velocity,
        magnetic,
        low,
        high,
        below,
        above,
        first,
        last,
        sides,
        pair_rows,
        send_cell,
        send_weight,
        cycle_slot,
    )
    payload = lax.all_to_all(payload, "lon", split_axis=0, concat_axis=0, tiled=True)
    payload = lax.ppermute(payload, "grid", [(0, 1), (1, 0)])
    cycle = pl.pallas_call(
        collect_kernel,
        in_specs=[VMEM],
        out_specs=VMEM,
        out_shape=tiles(1, 1, 1, 48, CYCLE),
        name="collect",
    )(payload)
    return (new_velocity, new_magnetic, cycle)


def solution(mesh):
    state = P("grid", None, None, "lon", "lat")
    rows = P("grid", "lat", "lon", None)
    return jax.shard_map(
        local,
        mesh=mesh,
        in_specs=(state, state, rows, rows, rows, rows),
        out_specs=(state, state, P("grid", "lat", "lon", None, None)),
        check_vma=False,
    )
```

```python
import math

import jax
import jax.numpy as jnp
from jax import lax
from jax.experimental import pallas as pl
from jax.experimental.pallas import tpu as pltpu
from jax.sharding import PartitionSpec as P

CAP = 16
CYCLE = 128
LEVELS = 8
CELLS_P = 32
CELLS_T = 128

inner_radius = 0.6
smag_const = 0.2
aniso_weight = 0.8
turb_prandtl = 0.7
courant = 0.2

ALONG_R = (0, 1, 2, 7, 8)
ALONG_T = (1, 3, 4, 6, 8)
ALONG_P = (2, 4, 5, 6, 7)
F32 = jnp.float32


def lanes_of(shape):
    return lax.broadcasted_iota(jnp.int32, shape, len(shape) - 1)


def rows_of(shape):
    return lax.broadcasted_iota(jnp.int32, shape, len(shape) - 2)


def pick(vel_ref, mag_ref, comp):
    return (vel_ref, comp) if comp < 3 else (mag_ref, comp - 3)


def edges_kernel(vel_ref, mag_ref, low_ref, high_ref, first_ref, last_ref):
    pair = lanes_of((CELLS_P, CELLS_T)) // 2
    low = jnp.zeros((CELLS_P, CELLS_T), F32)
    high = jnp.zeros((CELLS_P, CELLS_T), F32)
    for comp in range(6):
        ref, index = pick(vel_ref, mag_ref, comp)
        for level in range(LEVELS):
            place = 16 * comp + 2 * level
            block = ref[0, index, level]
            if place:
                block = pltpu.roll(block, place, 1)
            low = jnp.where(pair == place // 2, block, low)
            high = jnp.where(pair == (place // 2 - 1) % (CELLS_T // 2), block, high)
        first_ref[comp] = ref[0, index, :, 0, :]
        last_ref[comp] = ref[0, index, :, CELLS_P - 1, :]
        if comp < 5:
            first_ref[6 + comp] = ref[0, index, :, 1, :]
            last_ref[6 + comp] = ref[0, index, :, CELLS_P - 2, :]
    low_ref[...] = low
    high_ref[...] = pltpu.roll(high, 2, 1)
    first_ref[11] = jnp.zeros((LEVELS, CELLS_T), F32)
    last_ref[11] = jnp.zeros((LEVELS, CELLS_T), F32)


def corners_kernel(
    below_ref, above_ref, first_ref, last_ref, before_ref, after_ref, first_out_ref, last_out_ref
):
    shape = (LEVELS, CELLS_T)
    for row, source, target in ((0, first_ref, first_out_ref), (CELLS_P - 1, last_ref, last_out_ref)):
        below = jnp.broadcast_to(below_ref[row : row + 1, :], shape)
        above = jnp.broadcast_to(above_ref[row : row + 1, :], shape)
        target[0:11] = source[0:11]
        target[11] = jnp.where(rows_of(shape) == 0, below, above)


def second_kernel(place_ref, before_ref, after_ref, low_ref, high_ref, low_out_ref, high_out_ref):
    @pl.when(place_ref[1] % 2 == 1)
    def _():
        low_out_ref[...] = low_ref[...]
        high_out_ref[...] = high_ref[...]

    @pl.when(place_ref[1] % 2 == 0)
    def _():
        lane = lanes_of((LEVELS, CELLS_T))
        low = jnp.zeros((LEVELS, CELLS_T), F32)
        high = jnp.zeros((LEVELS, CELLS_T), F32)
        for side, ref in ((0, before_ref), (1, after_ref)):
            for comp in range(6):
                spot = 6 * side + comp
                block = ref[comp]
                low = jnp.where(lane == spot, pltpu.roll(block, spot, 1) if spot else block, low)
                high = jnp.where(lane == spot, pltpu.roll(block, spot + 1, 1), high)
        low_out_ref[0:LEVELS] = low
        high_out_ref[0:LEVELS] = high
        low_out_ref[LEVELS:] = jnp.zeros((CELLS_P - LEVELS, CELLS_T), F32)
        high_out_ref[LEVELS:] = jnp.zeros((CELLS_P - LEVELS, CELLS_T), F32)


def flux_of(center, grad_r, grad_t, grad_p, spacing, wanted):
    u0, u1, u2, b0, b1, b2 = center
    s00, s11, s22 = grad_r[0], grad_t[1], grad_p[2]
    d01 = grad_t[0] + grad_r[1]
    d02 = grad_p[0] + grad_r[2]
    d12 = grad_p[1] + grad_t[2]
    squares = 2.0 * (s00 * s00 + s11 * s11 + s22 * s22) + (d01 * d01 + d02 * d02 + d12 * d12)
    viscous = jnp.sqrt(squares) * ((smag_const * spacing) ** 2)
    q00, q11, q22 = b0 * b0, b1 * b1, b2 * b2
    field_sq = q00 + q11 + q22
    inverse = 1.0 / (field_sq + 1.0)
    q01, q02, q12 = b0 * b1, b0 * b2, b1 * b2
    aligned = q00 * s00 + q11 * s11 + q22 * s22 + (q01 * d01 + q02 * d02 + q12 * d12)
    weight = (2.0 * aniso_weight) * viscous * aligned * inverse * inverse - 1.0
    half = 0.5 * field_sq
    twice = viscous + viscous
    ratio = viscous * (1.0 / turb_prandtl)
    result = {}
    for chan in wanted:
        if chan == 0:
            result[0] = u0 * u0 + q00 * weight - twice * s00 + half
        elif chan == 1:
            result[1] = u0 * u1 + q01 * weight - viscous * d01
        elif chan == 2:
            result[2] = u0 * u2 + q02 * weight - viscous * d02
        elif chan == 3:
            result[3] = u1 * u1 + q11 * weight - twice * s11 + half
        elif chan == 4:
            result[4] = u1 * u2 + q12 * weight - viscous * d12
        elif chan == 5:
            result[5] = u2 * u2 + q22 * weight - twice * s22 + half
        elif chan == 6:
            result[6] = u1 * b2 - u2 * b1 - ratio * (grad_t[5] - grad_p[4])
        elif chan == 7:
            result[7] = u2 * b0 - u0 * b2 - ratio * (grad_p[3] - grad_r[5])
        else:
            result[8] = u0 * b1 - u1 * b0 - ratio * (grad_r[4] - grad_t[3])
    return result


def radius(level, spacing):
    return inner_radius + (level.astype(F32) + 0.5) * spacing


def inverse_sine(index, theta_step):
    return 1.0 / jnp.sin(0.25 * math.pi + (index.astype(F32) + 0.5) * theta_step)


def level_steps(level, sine, steps, scale):
    spacing, theta_step, phi_step = steps
    low_level = jnp.maximum(level - 1, 0)
    high_level = jnp.minimum(level + 1, LEVELS - 1)
    ends = (level == 0) | (level == LEVELS - 1)
    step_r = jnp.where(ends, scale / spacing, 0.5 * scale / spacing)
    inverse = 1.0 / radius(jnp.full((8, CELLS_T), level, jnp.int32), spacing)
    step_t = (inverse * (0.5 * scale / theta_step))[0:1]
    step_p = (sine * inverse * (0.5 * scale / phi_step))[0:1]
    return low_level, high_level, step_r, step_t, step_p


def along_t(block, ends, step):
    lane = lanes_of(block.shape)
    up = jnp.where(lane == CELLS_T - 1, ends, pltpu.roll(block, CELLS_T - 1, 1))
    down = jnp.where(lane == 0, ends, pltpu.roll(block, 1, 1))
    return (up - down) * step


def flux_kernel(steps, parity, place_ref, vel_ref, mag_ref, below_ref, above_ref, *rest):
    flux_ref = rest[-1]
    wide = (CELLS_P, CELLS_T)

    @pl.when(place_ref[1] % 2 == parity)
    def _():
        is_below = lanes_of(wide) % 2 == 1
        beside = jnp.where(is_below, below_ref[...], above_ref[...])
        own_sine = inverse_sine(place_ref[0] * CELLS_T + lanes_of((8, CELLS_T)), steps[1])

        def make_flux(level, carry):
            low_level, high_level, step_r, step_t, step_p = level_steps(level, own_sine, steps, 1.0)
            center, grad_r, grad_t, grad_p = [], [], [], []
            for comp in range(6):
                ref, index = pick(vel_ref, mag_ref, comp)
                block = ref[0, index, level]
                center.append(block)
                grad_r.append((ref[0, index, high_level] - ref[0, index, low_level]) * step_r)
                ends = pltpu.roll(beside, 2 * CELLS_T - 1 - 16 * comp - 2 * level, 1)
                grad_t.append(along_t(block, ends, step_t))
                gap = pltpu.roll(block, CELLS_P - 1, 0) - pltpu.roll(block, 1, 0)
                grad_p.append(gap * step_p)
            flux = flux_of(center, grad_r, grad_t, grad_p, steps[0], range(9))
            for chan in range(9):
                flux_ref[chan, level] = flux[chan]
            return carry

        lax.fori_loop(0, LEVELS, make_flux, 0)


def section_kernel(
    steps,
    lat_blocks,
    lon_blocks,
    place_ref,
    vel_ref,
    mag_ref,
    low_ref,
    high_ref,
    below_even_ref,
    above_even_ref,
    below_odd_ref,
    above_odd_ref,
    first_ref,
    last_ref,
    before_even_ref,
    after_even_ref,
    before_odd_ref,
    after_odd_ref,
    rows_ref,
    cell_ref,
    weight_ref,
    slot_ref,
    flux_in_ref,
    out_vel_ref,
    out_mag_ref,
    send_ref,
    flux_ref,
    edge_t_ref,
    edge_p_ref,
    taken_ref,
    side_ref,
    new_vel_ref,
    new_mag_ref,
    sem_ref,
):
    spacing, theta_step, phi_step = steps
    lat = place_ref[0]
    lon = place_ref[1]
    odd_block = lon % 2 == 1
    time_step = courant * spacing
    wide = (CELLS_P, CELLS_T)
    flat = (LEVELS, CELLS_T)
    lane = lanes_of(wide)
    row = rows_of(wide)
    lane_flat = lanes_of(flat)
    row_flat = rows_of(flat)
    first_row, last_row = row == 0, row == CELLS_P - 1
    first_t = lat * CELLS_T
    own_sine = inverse_sine(first_t + lanes_of((8, CELLS_T)), theta_step)

    @pl.when(odd_block)
    def _():
        side_ref[0] = before_odd_ref[...]
        side_ref[1] = after_odd_ref[...]

    @pl.when(jnp.logical_not(odd_block))
    def _():
        side_ref[0] = before_even_ref[...]
        side_ref[1] = after_even_ref[...]

    is_below = lane % 2 == 1
    level_of = (lane % 16) // 2
    below = jnp.where(odd_block, below_odd_ref[...], below_even_ref[...])
    above = jnp.where(odd_block, above_odd_ref[...], above_even_ref[...])
    beside = jnp.where(is_below, below, above)

    def swapped(block):
        return jnp.where(is_below, pltpu.roll(block, 1, 1), pltpu.roll(block, CELLS_T - 1, 1))

    def corner(side):
        tile = side_ref[side, 11]
        held = jnp.where(lane_flat[0:1] % 2 == 1, tile[0:1], tile[1:2])
        spot = 2 * row_flat
        total = jnp.zeros(flat, F32)
        for comp in range(6):
            start = 6 * side + comp
            for ref, shift in ((below_odd_ref, 1), (above_odd_ref, 0)):
                column = ref[0:LEVELS, start : start + 1]
                total = jnp.where(lane_flat == spot + (16 * comp + shift), column, total)
        return jnp.where(odd_block, held, jnp.sum(total, axis=0, keepdims=True))

    corners = (corner(0), corner(1))
    inverse_r = 1.0 / radius(level_of, spacing)
    own_step = jnp.where((level_of == 0) | (level_of == LEVELS - 1), 1.0 / spacing, 0.5 / spacing)
    up = jnp.where(level_of == LEVELS - 1, beside, pltpu.roll(beside, CELLS_T - 2, 1))
    down = jnp.where(level_of == 0, beside, pltpu.roll(beside, 2, 1))
    pack_r = (up - down) * own_step
    inner = jnp.where(is_below, high_ref[...], low_ref[...])
    outer = jnp.where(is_below, above, below)
    pack_t = swapped(inner - outer) * (
        jnp.where(is_below, 0.5 / theta_step, -0.5 / theta_step) * inverse_r
    )
    t_index = first_t + jnp.where(is_below[0:8], -1, CELLS_T)
    edge_sine = inverse_sine(t_index, theta_step)[0:1]
    up = jnp.where(last_row, corners[1], pltpu.roll(beside, CELLS_P - 1, 0))
    down = jnp.where(first_row, corners[0], pltpu.roll(beside, 1, 0))
    pack_p = (up - down) * (edge_sine * inverse_r * (0.5 / phi_step))

    def spread(block):
        return [block if comp == 0 else pltpu.roll(block, CELLS_T - 16 * comp, 1) for comp in range(6)]

    edge = flux_of(
        spread(beside), spread(pack_r), spread(pack_t), spread(pack_p), spacing, ALONG_T
    )
    outside = (is_below & (lat == 0)) | ((lane % 2 == 0) & (lat == lat_blocks - 1))
    for slot, chan in enumerate(ALONG_T):
        edge_t_ref[slot] = jnp.where(outside, 0.0, edge[chan])

    level_step = jnp.where(
        (row_flat == 0) | (row_flat == LEVELS - 1), 1.0 / spacing, 0.5 / spacing
    )
    inverse_flat = 1.0 / radius(row_flat, spacing)
    step_t = inverse_flat * (0.5 / theta_step)
    step_p = own_sine * inverse_flat * (0.5 / phi_step)
    for kind in range(4):
        side, own = kind % 2, kind // 2 == 1
        edge_row_ref = first_ref if side == 0 else last_ref
        if own:
            center = [edge_row_ref[comp] for comp in range(6)]
            near = [side_ref[side, comp] for comp in range(5)]
            away = [edge_row_ref[6 + comp] for comp in range(5)]
            start = 0 if side == 0 else CELLS_P - 1
            ends = beside[start : start + 1]
        else:
            center = [side_ref[side, comp] for comp in range(6)]
            near = [side_ref[side, 6 + comp] for comp in range(5)]
            away = [edge_row_ref[comp] for comp in range(5)]
            ends = corners[side]
        ends = jnp.broadcast_to(ends, flat)
        grad_r, grad_t, grad_p = [], [], []
        for comp in range(6):
            block = center[comp]
            up = jnp.where(row_flat == LEVELS - 1, block, pltpu.roll(block, LEVELS - 1, 0))
            down = jnp.where(row_flat == 0, block, pltpu.roll(block, 1, 0))
            grad_r.append((up - down) * level_step)
            spot = 16 * comp + 2 * row_flat
            before = jnp.sum(jnp.where(lane_flat == spot + 1, ends, 0.0), axis=1, keepdims=True)
            after = jnp.sum(jnp.where(lane_flat == spot, ends, 0.0), axis=1, keepdims=True)
            up = jnp.where(lane_flat == CELLS_T - 1, after, pltpu.roll(block, CELLS_T - 1, 1))
            down = jnp.where(lane_flat == 0, before, pltpu.roll(block, 1, 1))
            grad_t.append((up - down) * step_t)
            if comp < 5:
                gap = away[comp] - near[comp] if side == 0 else near[comp] - away[comp]
                grad_p.append(gap * step_p)
            else:
                grad_p.append(None)
        if own:
            edge = flux_of(center, grad_r, grad_t, grad_p, spacing, range(9))
            for chan in range(9):
                flux_ref[chan, :, 0 if side == 0 else CELLS_P - 1, :] = edge[chan]
        else:
            edge = flux_of(center, grad_r, grad_t, grad_p, spacing, ALONG_P)
            outside = lon == (0 if side == 0 else lon_blocks - 1)
            for slot, chan in enumerate(ALONG_P):
                edge_p_ref[side, slot] = jnp.where(outside, 0.0, edge[chan])

    def along_p(block, before, after, step):
        up = jnp.where(last_row, after, pltpu.roll(block, CELLS_P - 1, 0))
        down = jnp.where(first_row, before, pltpu.roll(block, 1, 0))
        return (up - down) * step

    def advance(level, carry):
        low_level, high_level, step_r, step_t, step_p = level_steps(
            level, own_sine, steps, time_step
        )

        def d_r(chan):
            return (flux_ref[chan, high_level] - flux_ref[chan, low_level]) * step_r

        def d_t(chan):
            slot = ALONG_T.index(chan)
            ends = pltpu.roll(edge_t_ref[slot], CELLS_T - 1 - 2 * level, 1)
            return along_t(flux_ref[chan, level], ends, step_t)

        def d_p(chan):
            slot = ALONG_P.index(chan)
            before = edge_p_ref[0, slot, pl.ds(level, 1), :]
            after = edge_p_ref[1, slot, pl.ds(level, 1), :]
            return along_p(flux_ref[chan, level], before, after, step_p)

        new_vel_ref[0, 0, level] = vel_ref[0, 0, level] - (d_r(0) + d_t(1) + d_p(2))
        new_vel_ref[0, 1, level] = vel_ref[0, 1, level] - (d_r(1) + d_t(3) + d_p(4))
        new_vel_ref[0, 2, level] = vel_ref[0, 2, level] - (d_r(2) + d_t(4) + d_p(5))
        new_mag_ref[0, 0, level] = mag_ref[0, 0, level] + (d_t(8) - d_p(7))
        new_mag_ref[0, 1, level] = mag_ref[0, 1, level] + (d_p(6) - d_r(8))
        new_mag_ref[0, 2, level] = mag_ref[0, 2, level] + (d_r(7) - d_t(6))
        for copy in out_copies(level):
            copy.start()
        return carry

    def out_copies(level):
        return [
            pltpu.make_async_copy(new.at[0, :, level], out.at[0, :, level], sem_ref.at[which, level])
            for which, new, out in ((0, new_vel_ref, out_vel_ref), (1, new_mag_ref, out_mag_ref))
        ]

    lax.fori_loop(0, LEVELS, advance, 0)

    slots_total = cell_ref.shape[-1]
    chunks = slots_total // CELLS_T
    rows_wide = jnp.broadcast_to(rows_ref[0, 0].astype(F32), (8, lon_blocks))
    owner = lanes_of((lon_blocks, slots_total)) // CAP == rows_of((lon_blocks, slots_total))
    counts = jnp.dot(rows_wide, owner.astype(F32), preferred_element_type=F32)
    bucket = lanes_of((8, slots_total)) % CAP
    live = bucket < (counts + 0.5).astype(jnp.int32)
    scale = jnp.where(live, jnp.broadcast_to(weight_ref[0, 0], (8, slots_total)), 0.0)
    cells = jnp.broadcast_to(cell_ref[0, 0], (8, slots_total))
    cell_t = cells % CELLS_T
    cell_p = cells // CELLS_T
    scale = jnp.where(cell_p % 8 == rows_of(cells.shape), scale, 0.0)
    group = cell_p // 8
    taken_ref[6:8] = jnp.zeros((2, LEVELS, slots_total), F32)
    taken_ref[6, 0:1] = slot_ref[0, 0].astype(F32)
    for start, ref in ((0, new_vel_ref), (3, new_mag_ref)):

        def take(comp, carry, start=start, ref=ref):
            for level in range(LEVELS):
                block = ref[0, comp, level]
                for chunk in range(chunks):
                    part = slice(chunk * CELLS_T, (chunk + 1) * CELLS_T)
                    where_t = cell_t[:, part]
                    total = jnp.zeros((8, CELLS_T), F32)
                    for step in range(CELLS_P // 8):
                        got = jnp.take_along_axis(
                            block[8 * step : 8 * step + 8],
                            where_t,
                            axis=1,
                            mode="promise_in_bounds",
                        )
                        total = jnp.where(group[:, part] == step, got, total)
                    total = jnp.sum(total * scale[:, part], axis=0, keepdims=True)
                    taken_ref[start + comp, level : level + 1, part] = total
            return carry

        lax.fori_loop(0, 3, take, 0)

    for chunk in range(chunks):
        part = taken_ref[:, :, chunk * CELLS_T : (chunk + 1) * CELLS_T].reshape(64, CELLS_T)
        both = jnp.concatenate([part, pltpu.roll(part, CELLS_T - 8, 1)], axis=0)
        turned = jnp.transpose(both)
        for block in range(8):
            send_ref[chunk * 8 + block] = turned[16 * block : 16 * block + 8]

    def finish(level, carry):
        for copy in out_copies(level):
            copy.wait()
        return carry

    lax.fori_loop(0, LEVELS, finish, 0)


def collect_kernel(got_ref, out_ref):
    rows = got_ref.shape[0] * got_ref.shape[1]
    got = got_ref[...].reshape(rows, CELLS_T)
    total = jnp.zeros((48, CYCLE), F32)
    for start in (0, 64):
        slot = got[:, start + 48 : start + 49].astype(jnp.int32)
        onehot = (slot == lanes_of((rows, CYCLE))).astype(F32)
        part = lax.dot_general(
            got,
            onehot,
            (((0,), (0,)), ((), ())),
            precision=lax.Precision.HIGHEST,
            preferred_element_type=F32,
        )
        total = total + part[start : start + 48]
    out_ref[0, 0, 0] = total


VMEM = pl.BlockSpec(memory_space=pltpu.VMEM)
SMEM = pl.BlockSpec(memory_space=pltpu.SMEM)
HBM = pl.BlockSpec(memory_space=pltpu.HBM)


def limit(mebibytes):
    return pltpu.CompilerParams(vmem_limit_bytes=mebibytes * 1024 * 1024)


def tiles(*shape):
    return jax.ShapeDtypeStruct(shape, F32)


def local(velocity, magnetic, pair_rows, send_cell, send_weight, cycle_slot):
    lat_blocks, lon_blocks = lax.axis_size("lat"), lax.axis_size("lon")
    theta_step = 0.5 * math.pi / (lat_blocks * CELLS_T)
    phi_step = 1.5 * math.pi / (lon_blocks * CELLS_P)
    spacing = inner_radius * theta_step
    place = jnp.stack([lax.axis_index("lat"), lax.axis_index("lon")]).astype(jnp.int32)
    pack = tiles(CELLS_P, CELLS_T)
    strip = tiles(12, LEVELS, CELLS_T)
    evens, odds = range(0, lon_blocks, 2), range(1, lon_blocks, 2)

    def along_lat(block, step, lons):
        pairs = [
            (lat * lon_blocks + lon, (lat + step) * lon_blocks + lon)
            for lat in range(lat_blocks)
            for lon in lons
            if 0 <= lat + step < lat_blocks
        ]
        return lax.ppermute(block, ("lat", "lon"), pairs)

    def along_lon(block, step, lons):
        pairs = [(lon, lon + step) for lon in lons if 0 <= lon + step < lon_blocks]
        return lax.ppermute(block, "lon", pairs)

    low, high, first, last = pl.pallas_call(
        edges_kernel,
        in_specs=[VMEM] * 2,
        out_specs=[VMEM] * 4,
        out_shape=[pack, pack, strip, strip],
        compiler_params=limit(4),
        name="edges",
    )(velocity, magnetic)
    below_even = along_lat(high, 1, evens)
    above_even = along_lat(low, -1, evens)
    before_even = along_lon(last, 1, odds)
    after_even = along_lon(first, -1, odds)
    first_full, last_full = pl.pallas_call(
        corners_kernel,
        in_specs=[VMEM] * 6,
        out_specs=[VMEM] * 2,
        out_shape=[strip, strip],
        compiler_params=limit(4),
        name="corners",
    )(below_even, above_even, first, last, before_even, after_even)
    before_odd = along_lon(last_full, 1, evens)
    after_odd = along_lon(first_full, -1, evens)
    second_low, second_high = pl.pallas_call(
        second_kernel,
        in_specs=[SMEM] + [VMEM] * 4,
        out_specs=[VMEM] * 2,
        out_shape=[pack, pack],
        compiler_params=limit(4),
        name="second",
    )(place, before_even, after_even, low, high)
    every = range(lon_blocks)
    below_odd = along_lat(second_high, 1, every)
    above_odd = along_lat(second_low, -1, every)
    slots_total = send_cell.shape[-1]
    steps = (spacing, theta_step, phi_step)

    def section(*refs):
        section_kernel(steps, lat_blocks, lon_blocks, *refs)

    def flux_of_cells(parity, below, above, *given):
        def kernel(*refs):
            flux_kernel(steps, parity, *refs)

        return pl.pallas_call(
            kernel,
            in_specs=[SMEM] + [VMEM] * (4 + len(given)),
            out_specs=VMEM,
            out_shape=tiles(9, LEVELS, CELLS_P, CELLS_T),
            input_output_aliases={5: 0} if given else {},
            compiler_params=limit(8),
            name="flux",
        )(place, velocity, magnetic, below, above, *given)

    flux = flux_of_cells(0, below_even, above_even)
    flux = flux_of_cells(1, below_odd, above_odd, flux)
    new_velocity, new_magnetic, payload, _ = pl.pallas_call(
        section,
        in_specs=[SMEM] + [VMEM] * 19,
        out_specs=[HBM] * 2 + [VMEM, VMEM],
        out_shape=[
            tiles(*velocity.shape),
            tiles(*magnetic.shape),
            tiles(lon_blocks, 8, CELLS_T),
            tiles(9, LEVELS, CELLS_P, CELLS_T),
        ],
        input_output_aliases={19: 3},
        scratch_shapes=[
            pltpu.VMEM((5, CELLS_P, CELLS_T), F32),
            pltpu.VMEM((2, 5, LEVELS, CELLS_T), F32),
            pltpu.VMEM((8, LEVELS, slots_total), F32),
            pltpu.VMEM((2, 12, LEVELS, CELLS_T), F32),
            pltpu.VMEM(velocity.shape, F32),
            pltpu.VMEM(magnetic.shape, F32),
            pltpu.SemaphoreType.DMA((2, LEVELS)),
        ],
        compiler_params=limit(16),
        name="section",
    )(
        place,
        velocity,
        magnetic,
        low,
        high,
        below_even,
        above_even,
        below_odd,
        above_odd,
        first,
        last,
        before_even,
        after_even,
        before_odd,
        after_odd,
        pair_rows,
        send_cell,
        send_weight,
        cycle_slot,
        flux,
    )
    payload = lax.all_to_all(payload, "lon", split_axis=0, concat_axis=0, tiled=True)
    cycle = pl.pallas_call(
        collect_kernel,
        in_specs=[VMEM],
        out_specs=VMEM,
        out_shape=tiles(1, 1, 1, 48, CYCLE),
        compiler_params=limit(4),
        name="collect",
    )(payload)
    cycle = lax.ppermute(cycle, "grid", [(0, 1), (1, 0)])
    return (new_velocity, new_magnetic, cycle)


def solution(mesh):
    state = P("grid", None, None, "lon", "lat")
    rows = P("grid", "lat", "lon", None)
    return jax.shard_map(
        local,
        mesh=mesh,
        in_specs=(state, state, rows, rows, rows, rows),
        out_specs=(state, state, P("grid", "lat", "lon", None, None)),
        check_vma=False,
    )
```

```python
import math

import jax
import jax.numpy as jnp
from jax import lax
from jax.experimental import pallas as pl
from jax.experimental.pallas import tpu as pltpu
from jax.sharding import PartitionSpec as P

CAP = 16
CYCLE = 128
LEVELS = 8
CELLS_P = 32
CELLS_T = 128

inner_radius = 0.6
smag_const = 0.2
aniso_weight = 0.8
turb_prandtl = 0.7
courant = 0.2

ALONG_R = (0, 1, 2, 7, 8)
ALONG_T = (1, 3, 4, 6, 8)
ALONG_P = (2, 4, 5, 6, 7)
F32 = jnp.float32


def lanes_of(shape):
    return lax.broadcasted_iota(jnp.int32, shape, len(shape) - 1)


def rows_of(shape):
    return lax.broadcasted_iota(jnp.int32, shape, len(shape) - 2)


def pick(vel_ref, mag_ref, comp):
    return (vel_ref, comp) if comp < 3 else (mag_ref, comp - 3)


def edges_kernel(vel_ref, mag_ref, low_ref, high_ref, first_ref, last_ref):
    pair = lanes_of((CELLS_P, CELLS_T)) // 2
    low = jnp.zeros((CELLS_P, CELLS_T), F32)
    high = jnp.zeros((CELLS_P, CELLS_T), F32)
    for comp in range(6):
        ref, index = pick(vel_ref, mag_ref, comp)
        for level in range(LEVELS):
            place = 16 * comp + 2 * level
            block = ref[0, index, level]
            if place:
                block = pltpu.roll(block, place, 1)
            low = jnp.where(pair == place // 2, block, low)
            high = jnp.where(pair == (place // 2 - 1) % (CELLS_T // 2), block, high)
        first_ref[comp] = ref[0, index, :, 0, :]
        last_ref[comp] = ref[0, index, :, CELLS_P - 1, :]
        if comp < 5:
            first_ref[6 + comp] = ref[0, index, :, 1, :]
            last_ref[6 + comp] = ref[0, index, :, CELLS_P - 2, :]
    low_ref[...] = low
    high_ref[...] = pltpu.roll(high, 2, 1)
    first_ref[11] = jnp.zeros((LEVELS, CELLS_T), F32)
    last_ref[11] = jnp.zeros((LEVELS, CELLS_T), F32)


def corners_kernel(
    below_ref, above_ref, first_ref, last_ref, before_ref, after_ref, first_out_ref, last_out_ref
):
    shape = (LEVELS, CELLS_T)
    for row, source, target in ((0, first_ref, first_out_ref), (CELLS_P - 1, last_ref, last_out_ref)):
        below = jnp.broadcast_to(below_ref[row : row + 1, :], shape)
        above = jnp.broadcast_to(above_ref[row : row + 1, :], shape)
        target[0:11] = source[0:11]
        target[11] = jnp.where(rows_of(shape) == 0, below, above)


def second_kernel(place_ref, before_ref, after_ref, low_ref, high_ref, low_out_ref, high_out_ref):
    @pl.when(place_ref[1] % 2 == 1)
    def _():
        low_out_ref[...] = low_ref[...]
        high_out_ref[...] = high_ref[...]

    @pl.when(place_ref[1] % 2 == 0)
    def _():
        lane = lanes_of((LEVELS, CELLS_T))
        low = jnp.zeros((LEVELS, CELLS_T), F32)
        high = jnp.zeros((LEVELS, CELLS_T), F32)
        for side, ref in ((0, before_ref), (1, after_ref)):
            for comp in range(6):
                spot = 6 * side + comp
                block = ref[comp]
                low = jnp.where(lane == spot, pltpu.roll(block, spot, 1) if spot else block, low)
                high = jnp.where(lane == spot, pltpu.roll(block, spot + 1, 1), high)
        low_out_ref[0:LEVELS] = low
        high_out_ref[0:LEVELS] = high
        low_out_ref[LEVELS:] = jnp.zeros((CELLS_P - LEVELS, CELLS_T), F32)
        high_out_ref[LEVELS:] = jnp.zeros((CELLS_P - LEVELS, CELLS_T), F32)


def flux_of(center, grad_r, grad_t, grad_p, spacing, wanted):
    u0, u1, u2, b0, b1, b2 = center
    s00, s11, s22 = grad_r[0], grad_t[1], grad_p[2]
    d01 = grad_t[0] + grad_r[1]
    d02 = grad_p[0] + grad_r[2]
    d12 = grad_p[1] + grad_t[2]
    squares = 2.0 * (s00 * s00 + s11 * s11 + s22 * s22) + (d01 * d01 + d02 * d02 + d12 * d12)
    viscous = jnp.sqrt(squares) * ((smag_const * spacing) ** 2)
    q00, q11, q22 = b0 * b0, b1 * b1, b2 * b2
    field_sq = q00 + q11 + q22
    inverse = 1.0 / (field_sq + 1.0)
    q01, q02, q12 = b0 * b1, b0 * b2, b1 * b2
    aligned = q00 * s00 + q11 * s11 + q22 * s22 + (q01 * d01 + q02 * d02 + q12 * d12)
    weight = (2.0 * aniso_weight) * viscous * aligned * inverse * inverse - 1.0
    half = 0.5 * field_sq
    twice = viscous + viscous
    ratio = viscous * (1.0 / turb_prandtl)
    result = {}
    for chan in wanted:
        if chan == 0:
            result[0] = u0 * u0 + q00 * weight - twice * s00 + half
        elif chan == 1:
            result[1] = u0 * u1 + q01 * weight - viscous * d01
        elif chan == 2:
            result[2] = u0 * u2 + q02 * weight - viscous * d02
        elif chan == 3:
            result[3] = u1 * u1 + q11 * weight - twice * s11 + half
        elif chan == 4:
            result[4] = u1 * u2 + q12 * weight - viscous * d12
        elif chan == 5:
            result[5] = u2 * u2 + q22 * weight - twice * s22 + half
        elif chan == 6:
            result[6] = u1 * b2 - u2 * b1 - ratio * (grad_t[5] - grad_p[4])
        elif chan == 7:
            result[7] = u2 * b0 - u0 * b2 - ratio * (grad_p[3] - grad_r[5])
        else:
            result[8] = u0 * b1 - u1 * b0 - ratio * (grad_r[4] - grad_t[3])
    return result


def radius(level, spacing):
    return inner_radius + (level.astype(F32) + 0.5) * spacing


def inverse_sine(index, theta_step):
    return 1.0 / jnp.sin(0.25 * math.pi + (index.astype(F32) + 0.5) * theta_step)


def level_steps(level, sine, steps, scale):
    spacing, theta_step, phi_step = steps
    low_level = jnp.maximum(level - 1, 0)
    high_level = jnp.minimum(level + 1, LEVELS - 1)
    ends = (level == 0) | (level == LEVELS - 1)
    step_r = jnp.where(ends, scale / spacing, 0.5 * scale / spacing)
    inverse = 1.0 / radius(jnp.full((8, CELLS_T), level, jnp.int32), spacing)
    step_t = (inverse * (0.5 * scale / theta_step))[0:1]
    step_p = (sine * inverse * (0.5 * scale / phi_step))[0:1]
    return low_level, high_level, step_r, step_t, step_p


def along_t(block, ends, step):
    lane = lanes_of(block.shape)
    up = jnp.where(lane == CELLS_T - 1, ends, pltpu.roll(block, CELLS_T - 1, 1))
    down = jnp.where(lane == 0, ends, pltpu.roll(block, 1, 1))
    return (up - down) * step


def flux_kernel(steps, parity, place_ref, vel_ref, mag_ref, below_ref, above_ref, *rest):
    flux_ref = rest[-1]
    wide = (CELLS_P, CELLS_T)

    @pl.when(place_ref[1] % 2 == parity)
    def _():
        is_below = lanes_of(wide) % 2 == 1
        beside = jnp.where(is_below, below_ref[...], above_ref[...])
        own_sine = inverse_sine(place_ref[0] * CELLS_T + lanes_of((8, CELLS_T)), steps[1])

        def make_flux(level, carry):
            low_level, high_level, step_r, step_t, step_p = level_steps(level, own_sine, steps, 1.0)
            center, grad_r, grad_t, grad_p = [], [], [], []
            for comp in range(6):
                ref, index = pick(vel_ref, mag_ref, comp)
                block = ref[0, index, level]
                center.append(block)
                grad_r.append((ref[0, index, high_level] - ref[0, index, low_level]) * step_r)
                ends = pltpu.roll(beside, 2 * CELLS_T - 1 - 16 * comp - 2 * level, 1)
                grad_t.append(along_t(block, ends, step_t))
                gap = pltpu.roll(block, CELLS_P - 1, 0) - pltpu.roll(block, 1, 0)
                grad_p.append(gap * step_p)
            flux = flux_of(center, grad_r, grad_t, grad_p, steps[0], range(9))
            for chan in range(9):
                flux_ref[chan, level] = flux[chan]
            return carry

        lax.fori_loop(0, LEVELS, make_flux, 0, unroll=8)


def section_kernel(
    steps,
    lat_blocks,
    lon_blocks,
    place_ref,
    vel_ref,
    mag_ref,
    low_ref,
    high_ref,
    below_even_ref,
    above_even_ref,
    below_odd_ref,
    above_odd_ref,
    first_ref,
    last_ref,
    before_even_ref,
    after_even_ref,
    before_odd_ref,
    after_odd_ref,
    rows_ref,
    cell_ref,
    weight_ref,
    slot_ref,
    flux_in_ref,
    out_vel_ref,
    out_mag_ref,
    send_ref,
    flux_ref,
    edge_t_ref,
    edge_p_ref,
    taken_ref,
    side_ref,
    new_vel_ref,
    new_mag_ref,
    sem_ref,
):
    spacing, theta_step, phi_step = steps
    lat = place_ref[0]
    lon = place_ref[1]
    odd_block = lon % 2 == 1
    time_step = courant * spacing
    wide = (CELLS_P, CELLS_T)
    flat = (LEVELS, CELLS_T)
    lane = lanes_of(wide)
    row = rows_of(wide)
    lane_flat = lanes_of(flat)
    row_flat = rows_of(flat)
    first_row, last_row = row == 0, row == CELLS_P - 1
    first_t = lat * CELLS_T
    own_sine = inverse_sine(first_t + lanes_of((8, CELLS_T)), theta_step)

    @pl.when(odd_block)
    def _():
        side_ref[0] = before_odd_ref[...]
        side_ref[1] = after_odd_ref[...]

    @pl.when(jnp.logical_not(odd_block))
    def _():
        side_ref[0] = before_even_ref[...]
        side_ref[1] = after_even_ref[...]

    is_below = lane % 2 == 1
    level_of = (lane % 16) // 2
    below = jnp.where(odd_block, below_odd_ref[...], below_even_ref[...])
    above = jnp.where(odd_block, above_odd_ref[...], above_even_ref[...])
    beside = jnp.where(is_below, below, above)

    def swapped(block):
        return jnp.where(is_below, pltpu.roll(block, 1, 1), pltpu.roll(block, CELLS_T - 1, 1))

    def corner(side):
        tile = side_ref[side, 11]
        held = jnp.where(lane_flat[0:1] % 2 == 1, tile[0:1], tile[1:2])
        spot = 2 * row_flat
        total = jnp.zeros(flat, F32)
        for comp in range(6):
            start = 6 * side + comp
            for ref, shift in ((below_odd_ref, 1), (above_odd_ref, 0)):
                column = ref[0:LEVELS, start : start + 1]
                total = jnp.where(lane_flat == spot + (16 * comp + shift), column, total)
        return jnp.where(odd_block, held, jnp.sum(total, axis=0, keepdims=True))

    corners = (corner(0), corner(1))
    inverse_r = 1.0 / radius(level_of, spacing)
    own_step = jnp.where((level_of == 0) | (level_of == LEVELS - 1), 1.0 / spacing, 0.5 / spacing)
    up = jnp.where(level_of == LEVELS - 1, beside, pltpu.roll(beside, CELLS_T - 2, 1))
    down = jnp.where(level_of == 0, beside, pltpu.roll(beside, 2, 1))
    pack_r = (up - down) * own_step
    inner = jnp.where(is_below, high_ref[...], low_ref[...])
    outer = jnp.where(is_below, above, below)
    pack_t = swapped(inner - outer) * (
        jnp.where(is_below, 0.5 / theta_step, -0.5 / theta_step) * inverse_r
    )
    t_index = first_t + jnp.where(is_below[0:8], -1, CELLS_T)
    edge_sine = inverse_sine(t_index, theta_step)[0:1]
    up = jnp.where(last_row, corners[1], pltpu.roll(beside, CELLS_P - 1, 0))
    down = jnp.where(first_row, corners[0], pltpu.roll(beside, 1, 0))
    pack_p = (up - down) * (edge_sine * inverse_r * (0.5 / phi_step))

    def spread(block):
        return [block if comp == 0 else pltpu.roll(block, CELLS_T - 16 * comp, 1) for comp in range(6)]

    edge = flux_of(
        spread(beside), spread(pack_r), spread(pack_t), spread(pack_p), spacing, ALONG_T
    )
    outside = (is_below & (lat == 0)) | ((lane % 2 == 0) & (lat == lat_blocks - 1))
    for slot, chan in enumerate(ALONG_T):
        edge_t_ref[slot] = jnp.where(outside, 0.0, edge[chan])

    level_step = jnp.where(
        (row_flat == 0) | (row_flat == LEVELS - 1), 1.0 / spacing, 0.5 / spacing
    )
    inverse_flat = 1.0 / radius(row_flat, spacing)
    step_t = inverse_flat * (0.5 / theta_step)
    step_p = own_sine * inverse_flat * (0.5 / phi_step)
    for kind in range(4):
        side, own = kind % 2, kind // 2 == 1
        edge_row_ref = first_ref if side == 0 else last_ref
        if own:
            center = [edge_row_ref[comp] for comp in range(6)]
            near = [side_ref[side, comp] for comp in range(5)]
            away = [edge_row_ref[6 + comp] for comp in range(5)]
            start = 0 if side == 0 else CELLS_P - 1
            ends = beside[start : start + 1]
        else:
            center = [side_ref[side, comp] for comp in range(6)]
            near = [side_ref[side, 6 + comp] for comp in range(5)]
            away = [edge_row_ref[comp] for comp in range(5)]
            ends = corners[side]
        ends = jnp.broadcast_to(ends, flat)
        grad_r, grad_t, grad_p = [], [], []
        for comp in range(6):
            block = center[comp]
            up = jnp.where(row_flat == LEVELS - 1, block, pltpu.roll(block, LEVELS - 1, 0))
            down = jnp.where(row_flat == 0, block, pltpu.roll(block, 1, 0))
            grad_r.append((up - down) * level_step)
            spot = 16 * comp + 2 * row_flat
            before = jnp.sum(jnp.where(lane_flat == spot + 1, ends, 0.0), axis=1, keepdims=True)
            after = jnp.sum(jnp.where(lane_flat == spot, ends, 0.0), axis=1, keepdims=True)
            up = jnp.where(lane_flat == CELLS_T - 1, after, pltpu.roll(block, CELLS_T - 1, 1))
            down = jnp.where(lane_flat == 0, before, pltpu.roll(block, 1, 1))
            grad_t.append((up - down) * step_t)
            if comp < 5:
                gap = away[comp] - near[comp] if side == 0 else near[comp] - away[comp]
                grad_p.append(gap * step_p)
            else:
                grad_p.append(None)
        if own:
            edge = flux_of(center, grad_r, grad_t, grad_p, spacing, range(9))
            for chan in range(9):
                flux_ref[chan, :, 0 if side == 0 else CELLS_P - 1, :] = edge[chan]
        else:
            edge = flux_of(center, grad_r, grad_t, grad_p, spacing, ALONG_P)
            outside = lon == (0 if side == 0 else lon_blocks - 1)
            for slot, chan in enumerate(ALONG_P):
                edge_p_ref[side, slot] = jnp.where(outside, 0.0, edge[chan])

    def along_p(block, before, after, step):
        up = jnp.where(last_row, after, pltpu.roll(block, CELLS_P - 1, 0))
        down = jnp.where(first_row, before, pltpu.roll(block, 1, 0))
        return (up - down) * step

    def advance(level, carry):
        low_level, high_level, step_r, step_t, step_p = level_steps(
            level, own_sine, steps, time_step
        )

        def d_r(chan):
            return (flux_ref[chan, high_level] - flux_ref[chan, low_level]) * step_r

        def d_t(chan):
            slot = ALONG_T.index(chan)
            ends = pltpu.roll(edge_t_ref[slot], CELLS_T - 1 - 2 * level, 1)
            return along_t(flux_ref[chan, level], ends, step_t)

        def d_p(chan):
            slot = ALONG_P.index(chan)
            before = edge_p_ref[0, slot, pl.ds(level, 1), :]
            after = edge_p_ref[1, slot, pl.ds(level, 1), :]
            return along_p(flux_ref[chan, level], before, after, step_p)

        new_vel_ref[0, 0, level] = vel_ref[0, 0, level] - (d_r(0) + d_t(1) + d_p(2))
        new_vel_ref[0, 1, level] = vel_ref[0, 1, level] - (d_r(1) + d_t(3) + d_p(4))
        new_vel_ref[0, 2, level] = vel_ref[0, 2, level] - (d_r(2) + d_t(4) + d_p(5))
        new_mag_ref[0, 0, level] = mag_ref[0, 0, level] + (d_t(8) - d_p(7))
        new_mag_ref[0, 1, level] = mag_ref[0, 1, level] + (d_p(6) - d_r(8))
        new_mag_ref[0, 2, level] = mag_ref[0, 2, level] + (d_r(7) - d_t(6))
        for copy in out_copies(level):
            copy.start()
        return carry

    def out_copies(level):
        return [
            pltpu.make_async_copy(new.at[0, :, level], out.at[0, :, level], sem_ref.at[which, level])
            for which, new, out in ((0, new_vel_ref, out_vel_ref), (1, new_mag_ref, out_mag_ref))
        ]

    lax.fori_loop(0, LEVELS, advance, 0, unroll=8)

    slots_total = cell_ref.shape[-1]
    chunks = slots_total // CELLS_T
    rows_wide = jnp.broadcast_to(rows_ref[0, 0].astype(F32), (8, lon_blocks))
    owner = lanes_of((lon_blocks, slots_total)) // CAP == rows_of((lon_blocks, slots_total))
    counts = jnp.dot(rows_wide, owner.astype(F32), preferred_element_type=F32)
    bucket = lanes_of((8, slots_total)) % CAP
    live = bucket < (counts + 0.5).astype(jnp.int32)
    scale = jnp.where(live, jnp.broadcast_to(weight_ref[0, 0], (8, slots_total)), 0.0)
    cells = jnp.broadcast_to(cell_ref[0, 0], (8, slots_total))
    cell_t = cells % CELLS_T
    cell_p = cells // CELLS_T
    scale = jnp.where(cell_p % 8 == rows_of(cells.shape), scale, 0.0)
    group = cell_p // 8
    taken_ref[6:8] = jnp.zeros((2, LEVELS, slots_total), F32)
    taken_ref[6, 0:1] = slot_ref[0, 0].astype(F32)
    sub = rows_of((8, CELLS_T))

    def fold(blocks):
        for width in (4, 2, 1):
            keep = sub % (2 * width) < width
            half = len(blocks) // 2
            merged = []
            for one, two in zip(blocks[:half], blocks[half:]):
                mine, other = jnp.where(keep, one, two), jnp.where(keep, two, one)
                moved = pltpu.roll(other, width, 0)
                if width < 4:
                    moved = jnp.where(keep, pltpu.roll(other, 8 - width, 0), moved)
                merged.append(mine + moved)
            blocks = merged
        return blocks[0]

    for chunk in range(chunks):
        part = slice(chunk * CELLS_T, (chunk + 1) * CELLS_T)
        where_t = cell_t[:, part]
        weights = [jnp.where(group[:, part] == step, scale[:, part], 0.0) for step in range(4)]
        for start, ref in ((0, new_vel_ref), (3, new_mag_ref)):

            def take(comp, carry, start=start, ref=ref, part=part, where_t=where_t, weights=weights):
                sums = []
                for level in range(LEVELS):
                    block = ref[0, comp, level]
                    total = 0.0
                    for step in range(CELLS_P // 8):
                        got = jnp.take_along_axis(
                            block[8 * step : 8 * step + 8],
                            where_t,
                            axis=1,
                            mode="promise_in_bounds",
                        )
                        total = total + got * weights[step]
                    sums.append(total)
                taken_ref[start + comp, :, part] = fold(sums)

            for comp in range(3):
                take(comp, 0)

    for chunk in range(chunks):
        part = taken_ref[:, :, chunk * CELLS_T : (chunk + 1) * CELLS_T].reshape(64, CELLS_T)
        both = jnp.concatenate([part, pltpu.roll(part, CELLS_T - 8, 1)], axis=0)
        turned = jnp.transpose(both)
        for block in range(8):
            send_ref[chunk * 8 + block] = turned[16 * block : 16 * block + 8]

    def finish(level, carry):
        for copy in out_copies(level):
            copy.wait()
        return carry

    lax.fori_loop(0, LEVELS, finish, 0)


def collect_kernel(got_ref, out_ref):
    rows = got_ref.shape[0] * got_ref.shape[1]
    got = got_ref[...].reshape(rows, CELLS_T)
    total = jnp.zeros((48, CYCLE), F32)
    for start in (0, 64):
        slot = got[:, start + 48 : start + 49].astype(jnp.int32)
        onehot = (slot == lanes_of((rows, CYCLE))).astype(F32)
        part = lax.dot_general(
            got,
            onehot,
            (((0,), (0,)), ((), ())),
            precision=lax.Precision.HIGHEST,
            preferred_element_type=F32,
        )
        total = total + part[start : start + 48]
    out_ref[0, 0, 0] = total


VMEM = pl.BlockSpec(memory_space=pltpu.VMEM)
SMEM = pl.BlockSpec(memory_space=pltpu.SMEM)
HBM = pl.BlockSpec(memory_space=pltpu.HBM)


def limit(mebibytes):
    return pltpu.CompilerParams(vmem_limit_bytes=mebibytes * 1024 * 1024)


def tiles(*shape):
    return jax.ShapeDtypeStruct(shape, F32)


def local(velocity, magnetic, pair_rows, send_cell, send_weight, cycle_slot):
    lat_blocks, lon_blocks = lax.axis_size("lat"), lax.axis_size("lon")
    theta_step = 0.5 * math.pi / (lat_blocks * CELLS_T)
    phi_step = 1.5 * math.pi / (lon_blocks * CELLS_P)
    spacing = inner_radius * theta_step
    place = jnp.stack([lax.axis_index("lat"), lax.axis_index("lon")]).astype(jnp.int32)
    pack = tiles(CELLS_P, CELLS_T)
    strip = tiles(12, LEVELS, CELLS_T)
    evens, odds = range(0, lon_blocks, 2), range(1, lon_blocks, 2)

    def along_lat(block, step, lons):
        pairs = [
            (lat * lon_blocks + lon, (lat + step) * lon_blocks + lon)
            for lat in range(lat_blocks)
            for lon in lons
            if 0 <= lat + step < lat_blocks
        ]
        return lax.ppermute(block, ("lat", "lon"), pairs)

    def along_lon(block, step, lons):
        pairs = [(lon, lon + step) for lon in lons if 0 <= lon + step < lon_blocks]
        return lax.ppermute(block, "lon", pairs)

    low, high, first, last = pl.pallas_call(
        edges_kernel,
        in_specs=[VMEM] * 2,
        out_specs=[VMEM] * 4,
        out_shape=[pack, pack, strip, strip],
        compiler_params=limit(4),
        name="edges",
    )(velocity, magnetic)
    below_even = along_lat(high, 1, evens)
    above_even = along_lat(low, -1, evens)
    before_even = along_lon(last, 1, odds)
    after_even = along_lon(first, -1, odds)
    first_full, last_full = pl.pallas_call(
        corners_kernel,
        in_specs=[VMEM] * 6,
        out_specs=[VMEM] * 2,
        out_shape=[strip, strip],
        compiler_params=limit(4),
        name="corners",
    )(below_even, above_even, first, last, before_even, after_even)
    before_odd = along_lon(last_full, 1, evens)
    after_odd = along_lon(first_full, -1, evens)
    second_low, second_high = pl.pallas_call(
        second_kernel,
        in_specs=[SMEM] + [VMEM] * 4,
        out_specs=[VMEM] * 2,
        out_shape=[pack, pack],
        compiler_params=limit(4),
        name="second",
    )(place, before_even, after_even, low, high)
    every = range(lon_blocks)
    below_odd = along_lat(second_high, 1, every)
    above_odd = along_lat(second_low, -1, every)
    slots_total = send_cell.shape[-1]
    steps = (spacing, theta_step, phi_step)

    def section(*refs):
        section_kernel(steps, lat_blocks, lon_blocks, *refs)

    def flux_of_cells(parity, below, above, *given):
        def kernel(*refs):
            flux_kernel(steps, parity, *refs)

        return pl.pallas_call(
            kernel,
            in_specs=[SMEM] + [VMEM] * (4 + len(given)),
            out_specs=VMEM,
            out_shape=tiles(9, LEVELS, CELLS_P, CELLS_T),
            input_output_aliases={5: 0} if given else {},
            compiler_params=limit(8),
            name="flux",
        )(place, velocity, magnetic, below, above, *given)

    flux = flux_of_cells(0, below_even, above_even)
    flux = flux_of_cells(1, below_odd, above_odd, flux)
    new_velocity, new_magnetic, payload, _ = pl.pallas_call(
        section,
        in_specs=[SMEM] + [VMEM] * 19,
        out_specs=[HBM] * 2 + [VMEM, VMEM],
        out_shape=[
            tiles(*velocity.shape),
            tiles(*magnetic.shape),
            tiles(lon_blocks, 8, CELLS_T),
            tiles(9, LEVELS, CELLS_P, CELLS_T),
        ],
        input_output_aliases={19: 3},
        scratch_shapes=[
            pltpu.VMEM((5, CELLS_P, CELLS_T), F32),
            pltpu.VMEM((2, 5, LEVELS, CELLS_T), F32),
            pltpu.VMEM((8, LEVELS, slots_total), F32),
            pltpu.VMEM((2, 12, LEVELS, CELLS_T), F32),
            pltpu.VMEM(velocity.shape, F32),
            pltpu.VMEM(magnetic.shape, F32),
            pltpu.SemaphoreType.DMA((2, LEVELS)),
        ],
        compiler_params=limit(16),
        name="section",
    )(
        place,
        velocity,
        magnetic,
        low,
        high,
        below_even,
        above_even,
        below_odd,
        above_odd,
        first,
        last,
        before_even,
        after_even,
        before_odd,
        after_odd,
        pair_rows,
        send_cell,
        send_weight,
        cycle_slot,
        flux,
    )
    payload = lax.all_to_all(payload, "lon", split_axis=0, concat_axis=0, tiled=True)
    cycle = pl.pallas_call(
        collect_kernel,
        in_specs=[VMEM],
        out_specs=VMEM,
        out_shape=tiles(1, 1, 1, 48, CYCLE),
        compiler_params=limit(4),
        name="collect",
    )(payload)
    cycle = lax.ppermute(cycle, "grid", [(0, 1), (1, 0)])
    return (new_velocity, new_magnetic, cycle)


def solution(mesh):
    state = P("grid", None, None, "lon", "lat")
    rows = P("grid", "lat", "lon", None)
    return jax.shard_map(
        local,
        mesh=mesh,
        in_specs=(state, state, rows, rows, rows, rows),
        out_specs=(state, state, P("grid", "lat", "lon", None, None)),
        check_vma=False,
    )
```

```python
import math

import jax
import jax.numpy as jnp
from jax import lax
from jax.experimental import pallas as pl
from jax.experimental.pallas import tpu as pltpu
from jax.sharding import PartitionSpec as P

CAP = 16
CYCLE = 128
LEVELS = 8
CELLS_P = 32
CELLS_T = 128

inner_radius = 0.6
smag_const = 0.2
aniso_weight = 0.8
turb_prandtl = 0.7
courant = 0.2

ALONG_R = (0, 1, 2, 7, 8)
ALONG_T = (1, 3, 4, 6, 8)
ALONG_P = (2, 4, 5, 6, 7)
F32 = jnp.float32


def lanes_of(shape):
    return lax.broadcasted_iota(jnp.int32, shape, len(shape) - 1)


def rows_of(shape):
    return lax.broadcasted_iota(jnp.int32, shape, len(shape) - 2)


def pick(vel_ref, mag_ref, comp):
    return (vel_ref, comp) if comp < 3 else (mag_ref, comp - 3)


def edges_kernel(vel_ref, mag_ref, low_ref, high_ref, first_ref, last_ref):
    pair = lanes_of((CELLS_P, CELLS_T)) // 2
    low = jnp.zeros((CELLS_P, CELLS_T), F32)
    high = jnp.zeros((CELLS_P, CELLS_T), F32)
    for comp in range(6):
        ref, index = pick(vel_ref, mag_ref, comp)
        for level in range(LEVELS):
            place = 16 * comp + 2 * level
            block = ref[0, index, level]
            if place:
                block = pltpu.roll(block, place, 1)
            low = jnp.where(pair == place // 2, block, low)
            high = jnp.where(pair == (place // 2 - 1) % (CELLS_T // 2), block, high)
        first_ref[comp] = ref[0, index, :, 0, :]
        last_ref[comp] = ref[0, index, :, CELLS_P - 1, :]
        if comp < 5:
            first_ref[6 + comp] = ref[0, index, :, 1, :]
            last_ref[6 + comp] = ref[0, index, :, CELLS_P - 2, :]
    low_ref[...] = low
    high_ref[...] = pltpu.roll(high, 2, 1)


def corners_kernel(
    below_ref, above_ref, first_ref, last_ref, before_ref, after_ref, first_out_ref, last_out_ref
):
    shape = (LEVELS, CELLS_T)
    for row, source, target in ((0, first_ref, first_out_ref), (CELLS_P - 1, last_ref, last_out_ref)):
        below = jnp.broadcast_to(below_ref[row : row + 1, :], shape)
        above = jnp.broadcast_to(above_ref[row : row + 1, :], shape)
        target[0:11] = source[...]
        target[11] = jnp.where(rows_of(shape) == 0, below, above)


def second_kernel(before_ref, after_ref, low_ref, high_ref, low_out_ref, high_out_ref):
    odd = lax.axis_index("lon") % 2

    @pl.when(odd == 1)
    def _():
        low_out_ref[...] = low_ref[...]
        high_out_ref[...] = high_ref[...]

    @pl.when(odd == 0)
    def _():
        lane = lanes_of((LEVELS, CELLS_T))
        low = jnp.zeros((LEVELS, CELLS_T), F32)
        high = jnp.zeros((LEVELS, CELLS_T), F32)
        for side, ref in ((0, before_ref), (1, after_ref)):
            for comp in range(6):
                spot = 6 * side + comp
                block = ref[comp]
                low = jnp.where(lane == spot, pltpu.roll(block, spot, 1) if spot else block, low)
                high = jnp.where(lane == spot, pltpu.roll(block, spot + 1, 1), high)
        low_out_ref[0:LEVELS] = low
        high_out_ref[0:LEVELS] = high
        low_out_ref[LEVELS:] = jnp.zeros((CELLS_P - LEVELS, CELLS_T), F32)
        high_out_ref[LEVELS:] = jnp.zeros((CELLS_P - LEVELS, CELLS_T), F32)


def flux_of(center, grad_r, grad_t, grad_p, spacing, wanted):
    u0, u1, u2, b0, b1, b2 = center
    s00, s11, s22 = grad_r[0], grad_t[1], grad_p[2]
    d01 = grad_t[0] + grad_r[1]
    d02 = grad_p[0] + grad_r[2]
    d12 = grad_p[1] + grad_t[2]
    squares = 2.0 * (s00 * s00 + s11 * s11 + s22 * s22) + (d01 * d01 + d02 * d02 + d12 * d12)
    viscous = jnp.sqrt(squares) * ((smag_const * spacing) ** 2)
    q00, q11, q22 = b0 * b0, b1 * b1, b2 * b2
    field_sq = q00 + q11 + q22
    inverse = 1.0 / (field_sq + 1.0)
    q01, q02, q12 = b0 * b1, b0 * b2, b1 * b2
    aligned = q00 * s00 + q11 * s11 + q22 * s22 + (q01 * d01 + q02 * d02 + q12 * d12)
    weight = (2.0 * aniso_weight) * viscous * aligned * inverse * inverse - 1.0
    half = 0.5 * field_sq
    twice = viscous + viscous
    ratio = viscous * (1.0 / turb_prandtl)
    result = {}
    for chan in wanted:
        if chan == 0:
            result[0] = u0 * u0 + q00 * weight - twice * s00 + half
        elif chan == 1:
            result[1] = u0 * u1 + q01 * weight - viscous * d01
        elif chan == 2:
            result[2] = u0 * u2 + q02 * weight - viscous * d02
        elif chan == 3:
            result[3] = u1 * u1 + q11 * weight - twice * s11 + half
        elif chan == 4:
            result[4] = u1 * u2 + q12 * weight - viscous * d12
        elif chan == 5:
            result[5] = u2 * u2 + q22 * weight - twice * s22 + half
        elif chan == 6:
            result[6] = u1 * b2 - u2 * b1 - ratio * (grad_t[5] - grad_p[4])
        elif chan == 7:
            result[7] = u2 * b0 - u0 * b2 - ratio * (grad_p[3] - grad_r[5])
        else:
            result[8] = u0 * b1 - u1 * b0 - ratio * (grad_r[4] - grad_t[3])
    return result


def radius(level, spacing):
    return inner_radius + (level.astype(F32) + 0.5) * spacing


def inverse_sine(index, theta_step):
    return 1.0 / jnp.sin(0.25 * math.pi + (index.astype(F32) + 0.5) * theta_step)


def level_steps(level, sine, steps, scale):
    spacing, theta_step, phi_step = steps
    low_level = jnp.maximum(level - 1, 0)
    high_level = jnp.minimum(level + 1, LEVELS - 1)
    ends = (level == 0) | (level == LEVELS - 1)
    step_r = jnp.where(ends, scale / spacing, 0.5 * scale / spacing)
    inverse = 1.0 / radius(jnp.full((8, CELLS_T), level, jnp.int32), spacing)
    step_t = (inverse * (0.5 * scale / theta_step))[0:1]
    step_p = (sine * inverse * (0.5 * scale / phi_step))[0:1]
    return low_level, high_level, step_r, step_t, step_p


def along_t(block, ends, step):
    lane = lanes_of(block.shape)
    up = jnp.where(lane == CELLS_T - 1, ends, pltpu.roll(block, CELLS_T - 1, 1))
    down = jnp.where(lane == 0, ends, pltpu.roll(block, 1, 1))
    return (up - down) * step


def flux_kernel(steps, parity, vel_ref, mag_ref, below_ref, above_ref, *rest):
    flux_ref = rest[-1]
    wide = (CELLS_P, CELLS_T)

    @pl.when(lax.axis_index("lon") % 2 == parity)
    def _():
        is_below = lanes_of(wide) % 2 == 1
        beside = jnp.where(is_below, below_ref[...], above_ref[...])
        own_sine = inverse_sine(lax.axis_index("lat") * CELLS_T + lanes_of((8, CELLS_T)), steps[1])

        def make_flux(level, carry):
            low_level, high_level, step_r, step_t, step_p = level_steps(level, own_sine, steps, 1.0)
            center, grad_r, grad_t, grad_p = [], [], [], []
            for comp in range(6):
                ref, index = pick(vel_ref, mag_ref, comp)
                block = ref[0, index, level]
                center.append(block)
                grad_r.append((ref[0, index, high_level] - ref[0, index, low_level]) * step_r)
                ends = pltpu.roll(beside, 2 * CELLS_T - 1 - 16 * comp - 2 * level, 1)
                grad_t.append(along_t(block, ends, step_t))
                gap = pltpu.roll(block, CELLS_P - 1, 0) - pltpu.roll(block, 1, 0)
                grad_p.append(gap * step_p)
            flux = flux_of(center, grad_r, grad_t, grad_p, steps[0], range(9))
            for chan in range(9):
                flux_ref[chan, level] = flux[chan]
            return carry

        lax.fori_loop(0, LEVELS, make_flux, 0, unroll=8)


def section_kernel(
    steps,
    lat_blocks,
    lon_blocks,
    vel_ref,
    mag_ref,
    low_ref,
    high_ref,
    below_even_ref,
    above_even_ref,
    below_odd_ref,
    above_odd_ref,
    first_ref,
    last_ref,
    before_even_ref,
    after_even_ref,
    before_odd_ref,
    after_odd_ref,
    rows_ref,
    cell_ref,
    weight_ref,
    slot_ref,
    flux_in_ref,
    new_vel_ref,
    new_mag_ref,
    send_ref,
    flux_ref,
    edge_t_ref,
    edge_p_ref,
    taken_ref,
    side_ref,
):
    spacing, theta_step, phi_step = steps
    lat = lax.axis_index("lat")
    lon = lax.axis_index("lon")
    odd_block = lon % 2 == 1
    time_step = courant * spacing
    wide = (CELLS_P, CELLS_T)
    flat = (LEVELS, CELLS_T)
    lane = lanes_of(wide)
    row = rows_of(wide)
    lane_flat = lanes_of(flat)
    row_flat = rows_of(flat)
    first_row, last_row = row == 0, row == CELLS_P - 1
    first_t = lat * CELLS_T
    own_sine = inverse_sine(first_t + lanes_of((8, CELLS_T)), theta_step)

    @pl.when(odd_block)
    def _():
        side_ref[0] = before_odd_ref[...]
        side_ref[1] = after_odd_ref[...]

    @pl.when(jnp.logical_not(odd_block))
    def _():
        side_ref[0, 0:11] = before_even_ref[...]
        side_ref[1, 0:11] = after_even_ref[...]
        side_ref[:, 11] = jnp.zeros((2, LEVELS, CELLS_T), F32)

    is_below = lane % 2 == 1
    level_of = (lane % 16) // 2
    below = jnp.where(odd_block, below_odd_ref[...], below_even_ref[...])
    above = jnp.where(odd_block, above_odd_ref[...], above_even_ref[...])
    beside = jnp.where(is_below, below, above)

    def swapped(block):
        return jnp.where(is_below, pltpu.roll(block, 1, 1), pltpu.roll(block, CELLS_T - 1, 1))

    def corner(side):
        tile = side_ref[side, 11]
        held = jnp.where(lane_flat[0:1] % 2 == 1, tile[0:1], tile[1:2])
        spot = 2 * row_flat
        total = jnp.zeros(flat, F32)
        for comp in range(6):
            start = 6 * side + comp
            for ref, shift in ((below_odd_ref, 1), (above_odd_ref, 0)):
                column = ref[0:LEVELS, start : start + 1]
                total = jnp.where(lane_flat == spot + (16 * comp + shift), column, total)
        return jnp.where(odd_block, held, jnp.sum(total, axis=0, keepdims=True))

    corners = (corner(0), corner(1))
    inverse_r = 1.0 / radius(level_of, spacing)
    own_step = jnp.where((level_of == 0) | (level_of == LEVELS - 1), 1.0 / spacing, 0.5 / spacing)
    up = jnp.where(level_of == LEVELS - 1, beside, pltpu.roll(beside, CELLS_T - 2, 1))
    down = jnp.where(level_of == 0, beside, pltpu.roll(beside, 2, 1))
    pack_r = (up - down) * own_step
    inner = jnp.where(is_below, high_ref[...], low_ref[...])
    outer = jnp.where(is_below, above, below)
    pack_t = swapped(inner - outer) * (
        jnp.where(is_below, 0.5 / theta_step, -0.5 / theta_step) * inverse_r
    )
    t_index = first_t + jnp.where(is_below[0:8], -1, CELLS_T)
    edge_sine = inverse_sine(t_index, theta_step)[0:1]
    up = jnp.where(last_row, corners[1], pltpu.roll(beside, CELLS_P - 1, 0))
    down = jnp.where(first_row, corners[0], pltpu.roll(beside, 1, 0))
    pack_p = (up - down) * (edge_sine * inverse_r * (0.5 / phi_step))

    def spread(block):
        return [block if comp == 0 else pltpu.roll(block, CELLS_T - 16 * comp, 1) for comp in range(6)]

    edge = flux_of(
        spread(beside), spread(pack_r), spread(pack_t), spread(pack_p), spacing, ALONG_T
    )
    outside = (is_below & (lat == 0)) | ((lane % 2 == 0) & (lat == lat_blocks - 1))
    for slot, chan in enumerate(ALONG_T):
        edge_t_ref[slot] = jnp.where(outside, 0.0, edge[chan])

    level_step = jnp.where(
        (row_flat == 0) | (row_flat == LEVELS - 1), 1.0 / spacing, 0.5 / spacing
    )
    inverse_flat = 1.0 / radius(row_flat, spacing)
    step_t = inverse_flat * (0.5 / theta_step)
    step_p = own_sine * inverse_flat * (0.5 / phi_step)
    for kind in range(4):
        side, own = kind % 2, kind // 2 == 1
        edge_row_ref = first_ref if side == 0 else last_ref
        if own:
            center = [edge_row_ref[comp] for comp in range(6)]
            near = [side_ref[side, comp] for comp in range(5)]
            away = [edge_row_ref[6 + comp] for comp in range(5)]
            start = 0 if side == 0 else CELLS_P - 1
            ends = beside[start : start + 1]
        else:
            center = [side_ref[side, comp] for comp in range(6)]
            near = [side_ref[side, 6 + comp] for comp in range(5)]
            away = [edge_row_ref[comp] for comp in range(5)]
            ends = corners[side]
        ends = jnp.broadcast_to(ends, flat)
        grad_r, grad_t, grad_p = [], [], []
        for comp in range(6):
            block = center[comp]
            up = jnp.where(row_flat == LEVELS - 1, block, pltpu.roll(block, LEVELS - 1, 0))
            down = jnp.where(row_flat == 0, block, pltpu.roll(block, 1, 0))
            grad_r.append((up - down) * level_step)
            spot = 16 * comp + 2 * row_flat
            before = jnp.sum(jnp.where(lane_flat == spot + 1, ends, 0.0), axis=1, keepdims=True)
            after = jnp.sum(jnp.where(lane_flat == spot, ends, 0.0), axis=1, keepdims=True)
            up = jnp.where(lane_flat == CELLS_T - 1, after, pltpu.roll(block, CELLS_T - 1, 1))
            down = jnp.where(lane_flat == 0, before, pltpu.roll(block, 1, 1))
            grad_t.append((up - down) * step_t)
            if comp < 5:
                gap = away[comp] - near[comp] if side == 0 else near[comp] - away[comp]
                grad_p.append(gap * step_p)
            else:
                grad_p.append(None)
        if own:
            edge = flux_of(center, grad_r, grad_t, grad_p, spacing, range(9))
            for chan in range(9):
                flux_ref[chan, :, 0 if side == 0 else CELLS_P - 1, :] = edge[chan]
        else:
            edge = flux_of(center, grad_r, grad_t, grad_p, spacing, ALONG_P)
            outside = lon == (0 if side == 0 else lon_blocks - 1)
            for slot, chan in enumerate(ALONG_P):
                edge_p_ref[side, slot] = jnp.where(outside, 0.0, edge[chan])

    def along_p(block, before, after, step):
        up = jnp.where(last_row, after, pltpu.roll(block, CELLS_P - 1, 0))
        down = jnp.where(first_row, before, pltpu.roll(block, 1, 0))
        return (up - down) * step

    def advance(level, carry):
        low_level, high_level, step_r, step_t, step_p = level_steps(
            level, own_sine, steps, time_step
        )

        def d_r(chan):
            return (flux_ref[chan, high_level] - flux_ref[chan, low_level]) * step_r

        def d_t(chan):
            slot = ALONG_T.index(chan)
            ends = pltpu.roll(edge_t_ref[slot], CELLS_T - 1 - 2 * level, 1)
            return along_t(flux_ref[chan, level], ends, step_t)

        def d_p(chan):
            slot = ALONG_P.index(chan)
            before = edge_p_ref[0, slot, pl.ds(level, 1), :]
            after = edge_p_ref[1, slot, pl.ds(level, 1), :]
            return along_p(flux_ref[chan, level], before, after, step_p)

        new_vel_ref[0, 0, level] = vel_ref[0, 0, level] - (d_r(0) + d_t(1) + d_p(2))
        new_vel_ref[0, 1, level] = vel_ref[0, 1, level] - (d_r(1) + d_t(3) + d_p(4))
        new_vel_ref[0, 2, level] = vel_ref[0, 2, level] - (d_r(2) + d_t(4) + d_p(5))
        new_mag_ref[0, 0, level] = mag_ref[0, 0, level] + (d_t(8) - d_p(7))
        new_mag_ref[0, 1, level] = mag_ref[0, 1, level] + (d_p(6) - d_r(8))
        new_mag_ref[0, 2, level] = mag_ref[0, 2, level] + (d_r(7) - d_t(6))
        return carry

    lax.fori_loop(0, LEVELS, advance, 0, unroll=8)

    slots_total = cell_ref.shape[-1]
    chunks = slots_total // CELLS_T
    rows_wide = jnp.broadcast_to(rows_ref[0, 0].astype(F32), (8, lon_blocks))
    owner = lanes_of((lon_blocks, slots_total)) // CAP == rows_of((lon_blocks, slots_total))
    counts = jnp.dot(rows_wide, owner.astype(F32), preferred_element_type=F32)
    bucket = lanes_of((8, slots_total)) % CAP
    live = bucket < (counts + 0.5).astype(jnp.int32)
    scale = jnp.where(live, jnp.broadcast_to(weight_ref[0, 0], (8, slots_total)), 0.0)
    cells = jnp.broadcast_to(cell_ref[0, 0], (8, slots_total))
    cell_t = cells % CELLS_T
    cell_p = cells // CELLS_T
    scale = jnp.where(cell_p % 8 == rows_of(cells.shape), scale, 0.0)
    group = cell_p // 8
    taken_ref[6:8] = jnp.zeros((2, LEVELS, slots_total), F32)
    taken_ref[6, 0:1] = slot_ref[0, 0].astype(F32)
    sub = rows_of((8, CELLS_T))

    def fold(blocks):
        for width in (4, 2, 1):
            keep = sub % (2 * width) < width
            half = len(blocks) // 2
            merged = []
            for one, two in zip(blocks[:half], blocks[half:]):
                mine, other = jnp.where(keep, one, two), jnp.where(keep, two, one)
                moved = pltpu.roll(other, width, 0)
                if width < 4:
                    moved = jnp.where(keep, pltpu.roll(other, 8 - width, 0), moved)
                merged.append(mine + moved)
            blocks = merged
        return blocks[0]

    for chunk in range(chunks):
        part = slice(chunk * CELLS_T, (chunk + 1) * CELLS_T)
        where_t = cell_t[:, part]
        weights = [jnp.where(group[:, part] == step, scale[:, part], 0.0) for step in range(4)]
        for start, ref in ((0, new_vel_ref), (3, new_mag_ref)):

            def take(comp, carry, start=start, ref=ref, part=part, where_t=where_t, weights=weights):
                sums = []
                for level in range(LEVELS):
                    block = ref[0, comp, level]
                    total = 0.0
                    for step in range(CELLS_P // 8):
                        got = jnp.take_along_axis(
                            block[8 * step : 8 * step + 8],
                            where_t,
                            axis=1,
                            mode="promise_in_bounds",
                        )
                        total = total + got * weights[step]
                    sums.append(total)
                taken_ref[start + comp, :, part] = fold(sums)

            for comp in range(3):
                take(comp, 0)

    for chunk in range(chunks):
        part = taken_ref[:, :, chunk * CELLS_T : (chunk + 1) * CELLS_T].reshape(64, CELLS_T)
        both = jnp.concatenate([part, pltpu.roll(part, CELLS_T - 8, 1)], axis=0)
        turned = jnp.transpose(both)
        for block in range(8):
            send_ref[chunk * 8 + block] = turned[16 * block : 16 * block + 8]


def store_kernel(vel_ref, mag_ref, out_vel_ref, out_mag_ref, sem_ref):
    copies = [
        pltpu.make_async_copy(vel_ref, out_vel_ref, sem_ref.at[0]),
        pltpu.make_async_copy(mag_ref, out_mag_ref, sem_ref.at[1]),
    ]
    for copy in copies:
        copy.start()
    for copy in copies:
        copy.wait()


def collect_kernel(got_ref, near_ref, far_ref):
    sources = got_ref.shape[0]
    rows = sources * 8
    totals = []
    for half in range(2):
        got = got_ref[:, 8 * half : 8 * half + 8].reshape(rows, CELLS_T)
        total = jnp.zeros((48, CYCLE), F32)
        for start in (0, 64):
            slot = got[:, start + 48 : start + 49].astype(jnp.int32)
            onehot = (slot == lanes_of((rows, CYCLE))).astype(F32)
            part = lax.dot_general(
                got,
                onehot,
                (((0,), (0,)), ((), ())),
                precision=lax.Precision.HIGHEST,
                preferred_element_type=F32,
            )
            total = total + part[start : start + 48]
        totals.append(total)
    odd = lax.axis_index("lon") % 2 == 1
    near_ref[0, 0, 0] = jnp.where(odd, totals[1], totals[0])
    far_ref[0, 0, 0] = jnp.where(odd, totals[0], totals[1])


VMEM = pl.BlockSpec(memory_space=pltpu.VMEM)
HBM = pl.BlockSpec(memory_space=pltpu.HBM)


def limit(mebibytes):
    return pltpu.CompilerParams(vmem_limit_bytes=mebibytes * 1024 * 1024)


def tiles(*shape):
    return jax.ShapeDtypeStruct(shape, F32)


def local(velocity, magnetic, pair_rows, send_cell, send_weight, cycle_slot):
    lat_blocks, lon_blocks = lax.axis_size("lat"), lax.axis_size("lon")
    theta_step = 0.5 * math.pi / (lat_blocks * CELLS_T)
    phi_step = 1.5 * math.pi / (lon_blocks * CELLS_P)
    spacing = inner_radius * theta_step
    pack = tiles(CELLS_P, CELLS_T)
    strip = tiles(11, LEVELS, CELLS_T)
    strip_full = tiles(12, LEVELS, CELLS_T)
    evens, odds = range(0, lon_blocks, 2), range(1, lon_blocks, 2)

    def along_lat(block, step, lons):
        pairs = [
            (lat * lon_blocks + lon, (lat + step) * lon_blocks + lon)
            for lat in range(lat_blocks)
            for lon in lons
            if 0 <= lat + step < lat_blocks
        ]
        return lax.ppermute(block, ("lat", "lon"), pairs)

    def along_lon(block, step, lons):
        pairs = [(lon, lon + step) for lon in lons if 0 <= lon + step < lon_blocks]
        return lax.ppermute(block, "lon", pairs)

    low, high, first, last = pl.pallas_call(
        edges_kernel,
        in_specs=[VMEM] * 2,
        out_specs=[VMEM] * 4,
        out_shape=[pack, pack, strip, strip],
        compiler_params=limit(4),
        name="edges",
    )(velocity, magnetic)
    below_even = along_lat(high, 1, evens)
    above_even = along_lat(low, -1, evens)
    before_even = along_lon(last, 1, odds)
    after_even = along_lon(first, -1, odds)
    first_full, last_full = pl.pallas_call(
        corners_kernel,
        in_specs=[VMEM] * 6,
        out_specs=[VMEM] * 2,
        out_shape=[strip_full, strip_full],
        compiler_params=limit(4),
        name="corners",
    )(below_even, above_even, first, last, before_even, after_even)
    before_odd = along_lon(last_full, 1, evens)
    after_odd = along_lon(first_full, -1, evens)
    second_low, second_high = pl.pallas_call(
        second_kernel,
        in_specs=[VMEM] * 4,
        out_specs=[VMEM] * 2,
        out_shape=[pack, pack],
        compiler_params=limit(4),
        name="second",
    )(before_even, after_even, low, high)
    every = range(lon_blocks)
    below_odd = along_lat(second_high, 1, every)
    above_odd = along_lat(second_low, -1, every)
    slots_total = send_cell.shape[-1]
    steps = (spacing, theta_step, phi_step)

    def section(*refs):
        section_kernel(steps, lat_blocks, lon_blocks, *refs)

    def flux_of_cells(parity, below, above, *given):
        def kernel(*refs):
            flux_kernel(steps, parity, *refs)

        return pl.pallas_call(
            kernel,
            in_specs=[VMEM] * (4 + len(given)),
            out_specs=VMEM,
            out_shape=tiles(9, LEVELS, CELLS_P, CELLS_T),
            input_output_aliases={4: 0} if given else {},
            compiler_params=limit(8),
            name="flux",
        )(velocity, magnetic, below, above, *given)

    flux = flux_of_cells(0, below_even, above_even)
    flux = flux_of_cells(1, below_odd, above_odd, flux)
    new_velocity, new_magnetic, payload, _ = pl.pallas_call(
        section,
        in_specs=[VMEM] * 19,
        out_specs=[VMEM] * 4,
        out_shape=[
            tiles(*velocity.shape),
            tiles(*magnetic.shape),
            tiles(lon_blocks, 8, CELLS_T),
            tiles(9, LEVELS, CELLS_P, CELLS_T),
        ],
        input_output_aliases={18: 3},
        scratch_shapes=[
            pltpu.VMEM((5, CELLS_P, CELLS_T), F32),
            pltpu.VMEM((2, 5, LEVELS, CELLS_T), F32),
            pltpu.VMEM((8, LEVELS, slots_total), F32),
            pltpu.VMEM((2, 12, LEVELS, CELLS_T), F32),
        ],
        compiler_params=limit(16),
        name="section",
    )(
        velocity,
        magnetic,
        low,
        high,
        below_even,
        above_even,
        below_odd,
        above_odd,
        first,
        last,
        before_even,
        after_even,
        before_odd,
        after_odd,
        pair_rows,
        send_cell,
        send_weight,
        cycle_slot,
        flux,
    )
    new_velocity, new_magnetic = pl.pallas_call(
        store_kernel,
        in_specs=[VMEM] * 2,
        out_specs=[HBM] * 2,
        out_shape=[tiles(*velocity.shape), tiles(*magnetic.shape)],
        scratch_shapes=[pltpu.SemaphoreType.DMA((2,))],
        compiler_params=limit(4),
        name="store",
    )(new_velocity, new_magnetic)
    pairs = lon_blocks // 2
    groups = [[2 * pair + parity for pair in range(pairs)] for parity in range(2)]
    payload = lax.all_to_all(
        payload.reshape(pairs, 16, CELLS_T),
        "lon",
        split_axis=0,
        concat_axis=0,
        axis_index_groups=groups,
        tiled=True,
    )
    near, far = pl.pallas_call(
        collect_kernel,
        in_specs=[VMEM],
        out_specs=[VMEM] * 2,
        out_shape=[tiles(1, 1, 1, 48, CYCLE)] * 2,
        compiler_params=limit(4),
        name="collect",
    )(payload)
    across = [
        (grid * lon_blocks + lon, (1 - grid) * lon_blocks + (lon ^ 1))
        for grid in range(2)
        for lon in range(lon_blocks)
    ]
    far = lax.ppermute(far, ("grid", "lon"), across)
    near = lax.ppermute(near, "grid", [(0, 1), (1, 0)])
    cycle = far + near
    return (new_velocity, new_magnetic, cycle)


def solution(mesh):
    state = P("grid", None, None, "lon", "lat")
    rows = P("grid", "lat", "lon", None)
    return jax.shard_map(
        local,
        mesh=mesh,
        in_specs=(state, state, rows, rows, rows, rows),
        out_specs=(state, state, P("grid", "lat", "lon", None, None)),
        check_vma=False,
    )
```

```python
import math

import jax
import jax.numpy as jnp
from jax import lax
from jax.experimental import pallas as pl
from jax.experimental.pallas import tpu as pltpu
from jax.sharding import PartitionSpec as P

CAP = 16
CYCLE = 128
LEVELS = 8
CELLS_P = 32
CELLS_T = 128

inner_radius = 0.6
smag_const = 0.2
aniso_weight = 0.8
turb_prandtl = 0.7
courant = 0.2

ALONG_R = (0, 1, 2, 7, 8)
ALONG_T = (1, 3, 4, 6, 8)
ALONG_P = (2, 4, 5, 6, 7)
F32 = jnp.float32


def lanes_of(shape):
    return lax.broadcasted_iota(jnp.int32, shape, len(shape) - 1)


def rows_of(shape):
    return lax.broadcasted_iota(jnp.int32, shape, len(shape) - 2)


def pick(vel_ref, mag_ref, comp):
    return (vel_ref, comp) if comp < 3 else (mag_ref, comp - 3)


def edges_kernel(vel_ref, mag_ref, low_ref, high_ref, first_ref, last_ref, one_ref, two_ref):
    pair = lanes_of((CELLS_P, CELLS_T)) // 2
    low = jnp.zeros((CELLS_P, CELLS_T), F32)
    high = jnp.zeros((CELLS_P, CELLS_T), F32)
    for comp in range(6):
        ref, index = pick(vel_ref, mag_ref, comp)
        for level in range(LEVELS):
            place = 16 * comp + 2 * level
            block = ref[0, index, level]
            if place:
                block = pltpu.roll(block, place, 1)
            low = jnp.where(pair == place // 2, block, low)
            high = jnp.where(pair == (place // 2 - 1) % (CELLS_T // 2), block, high)
        first_ref[comp] = ref[0, index, :, 0, :]
        last_ref[comp] = ref[0, index, :, CELLS_P - 1, :]
        if comp < 5:
            first_ref[6 + comp] = ref[0, index, :, 1, :]
            last_ref[6 + comp] = ref[0, index, :, CELLS_P - 2, :]
    high = pltpu.roll(high, 2, 1)
    low_ref[...] = low
    high_ref[...] = high
    upward = lax.axis_index("lat") % 2 == 0
    one_ref[...] = jnp.where(upward, high, low)
    two_ref[...] = jnp.where(upward, low, high)


def below_above(one, two):
    upward = lax.axis_index("lat") % 2 == 0
    return jnp.where(upward, two, one), jnp.where(upward, one, two)


def corners_kernel(
    one_ref, two_ref, first_ref, last_ref, before_ref, after_ref, first_out_ref, last_out_ref
):
    shape = (LEVELS, CELLS_T)
    for row, source, target in ((0, first_ref, first_out_ref), (CELLS_P - 1, last_ref, last_out_ref)):
        below, above = below_above(one_ref[row : row + 1, :], two_ref[row : row + 1, :])
        below = jnp.broadcast_to(below, shape)
        above = jnp.broadcast_to(above, shape)
        target[0:11] = source[...]
        target[11] = jnp.where(rows_of(shape) == 0, below, above)


def second_kernel(before_ref, after_ref, low_ref, high_ref, one_ref, two_ref):
    upward = lax.axis_index("lat") % 2 == 0

    odd = lax.axis_index("lon") % 2

    @pl.when(odd == 1)
    def _():
        one_ref[...] = jnp.where(upward, high_ref[...], low_ref[...])
        two_ref[...] = jnp.where(upward, low_ref[...], high_ref[...])

    @pl.when(odd == 0)
    def _():
        lane = lanes_of((LEVELS, CELLS_T))
        low = jnp.zeros((LEVELS, CELLS_T), F32)
        high = jnp.zeros((LEVELS, CELLS_T), F32)
        for side, ref in ((0, before_ref), (1, after_ref)):
            for comp in range(6):
                spot = 6 * side + comp
                block = ref[comp]
                low = jnp.where(lane == spot, pltpu.roll(block, spot, 1) if spot else block, low)
                high = jnp.where(lane == spot, pltpu.roll(block, spot + 1, 1), high)
        one_ref[0:LEVELS] = jnp.where(upward, high, low)
        two_ref[0:LEVELS] = jnp.where(upward, low, high)
        one_ref[LEVELS:] = jnp.zeros((CELLS_P - LEVELS, CELLS_T), F32)
        two_ref[LEVELS:] = jnp.zeros((CELLS_P - LEVELS, CELLS_T), F32)


def flux_of(center, grad_r, grad_t, grad_p, spacing, wanted):
    u0, u1, u2, b0, b1, b2 = center
    s00, s11, s22 = grad_r[0], grad_t[1], grad_p[2]
    d01 = grad_t[0] + grad_r[1]
    d02 = grad_p[0] + grad_r[2]
    d12 = grad_p[1] + grad_t[2]
    squares = 2.0 * (s00 * s00 + s11 * s11 + s22 * s22) + (d01 * d01 + d02 * d02 + d12 * d12)
    viscous = jnp.sqrt(squares) * ((smag_const * spacing) ** 2)
    q00, q11, q22 = b0 * b0, b1 * b1, b2 * b2
    field_sq = q00 + q11 + q22
    inverse = 1.0 / (field_sq + 1.0)
    q01, q02, q12 = b0 * b1, b0 * b2, b1 * b2
    aligned = q00 * s00 + q11 * s11 + q22 * s22 + (q01 * d01 + q02 * d02 + q12 * d12)
    weight = (2.0 * aniso_weight) * viscous * aligned * inverse * inverse - 1.0
    half = 0.5 * field_sq
    twice = viscous + viscous
    ratio = viscous * (1.0 / turb_prandtl)
    result = {}
    for chan in wanted:
        if chan == 0:
            result[0] = u0 * u0 + q00 * weight - twice * s00 + half
        elif chan == 1:
            result[1] = u0 * u1 + q01 * weight - viscous * d01
        elif chan == 2:
            result[2] = u0 * u2 + q02 * weight - viscous * d02
        elif chan == 3:
            result[3] = u1 * u1 + q11 * weight - twice * s11 + half
        elif chan == 4:
            result[4] = u1 * u2 + q12 * weight - viscous * d12
        elif chan == 5:
            result[5] = u2 * u2 + q22 * weight - twice * s22 + half
        elif chan == 6:
            result[6] = u1 * b2 - u2 * b1 - ratio * (grad_t[5] - grad_p[4])
        elif chan == 7:
            result[7] = u2 * b0 - u0 * b2 - ratio * (grad_p[3] - grad_r[5])
        else:
            result[8] = u0 * b1 - u1 * b0 - ratio * (grad_r[4] - grad_t[3])
    return result


def radius(level, spacing):
    return inner_radius + (level.astype(F32) + 0.5) * spacing


def inverse_sine(index, theta_step):
    return 1.0 / jnp.sin(0.25 * math.pi + (index.astype(F32) + 0.5) * theta_step)


def level_steps(level, sine, steps, scale):
    spacing, theta_step, phi_step = steps
    low_level = jnp.maximum(level - 1, 0)
    high_level = jnp.minimum(level + 1, LEVELS - 1)
    ends = (level == 0) | (level == LEVELS - 1)
    step_r = jnp.where(ends, scale / spacing, 0.5 * scale / spacing)
    inverse = 1.0 / radius(jnp.full((8, CELLS_T), level, jnp.int32), spacing)
    step_t = (inverse * (0.5 * scale / theta_step))[0:1]
    step_p = (sine * inverse * (0.5 * scale / phi_step))[0:1]
    return low_level, high_level, step_r, step_t, step_p


def along_t(block, ends, step):
    lane = lanes_of(block.shape)
    up = jnp.where(lane == CELLS_T - 1, ends, pltpu.roll(block, CELLS_T - 1, 1))
    down = jnp.where(lane == 0, ends, pltpu.roll(block, 1, 1))
    return (up - down) * step


def flux_kernel(steps, parity, vel_ref, mag_ref, one_ref, two_ref, *rest):
    flux_ref = rest[-1]
    wide = (CELLS_P, CELLS_T)

    @pl.when(lax.axis_index("lon") % 2 == parity)
    def _():
        is_below = lanes_of(wide) % 2 == 1
        below, above = below_above(one_ref[...], two_ref[...])
        beside = jnp.where(is_below, below, above)
        own_sine = inverse_sine(lax.axis_index("lat") * CELLS_T + lanes_of((8, CELLS_T)), steps[1])

        def make_flux(level, carry):
            low_level, high_level, step_r, step_t, step_p = level_steps(level, own_sine, steps, 1.0)
            center, grad_r, grad_t, grad_p = [], [], [], []
            for comp in range(6):
                ref, index = pick(vel_ref, mag_ref, comp)
                block = ref[0, index, level]
                center.append(block)
                grad_r.append((ref[0, index, high_level] - ref[0, index, low_level]) * step_r)
                ends = pltpu.roll(beside, 2 * CELLS_T - 1 - 16 * comp - 2 * level, 1)
                grad_t.append(along_t(block, ends, step_t))
                gap = pltpu.roll(block, CELLS_P - 1, 0) - pltpu.roll(block, 1, 0)
                grad_p.append(gap * step_p)
            flux = flux_of(center, grad_r, grad_t, grad_p, steps[0], range(9))
            for chan in range(9):
                flux_ref[chan, level] = flux[chan]
            return carry

        lax.fori_loop(0, LEVELS, make_flux, 0, unroll=8)


def section_kernel(
    steps,
    lat_blocks,
    lon_blocks,
    vel_ref,
    mag_ref,
    low_ref,
    high_ref,
    one_even_ref,
    two_even_ref,
    one_odd_ref,
    two_odd_ref,
    first_ref,
    last_ref,
    before_even_ref,
    after_even_ref,
    before_odd_ref,
    after_odd_ref,
    spot_ref,
    factor_ref,
    slot_ref,
    flux_in_ref,
    new_vel_ref,
    new_mag_ref,
    send_ref,
    flux_ref,
    edge_t_ref,
    edge_p_ref,
    taken_ref,
    side_ref,
):
    spacing, theta_step, phi_step = steps
    lat = lax.axis_index("lat")
    lon = lax.axis_index("lon")
    odd_block = lon % 2 == 1
    time_step = courant * spacing
    wide = (CELLS_P, CELLS_T)
    flat = (LEVELS, CELLS_T)
    lane = lanes_of(wide)
    row = rows_of(wide)
    lane_flat = lanes_of(flat)
    row_flat = rows_of(flat)
    first_row, last_row = row == 0, row == CELLS_P - 1
    first_t = lat * CELLS_T
    own_sine = inverse_sine(first_t + lanes_of((8, CELLS_T)), theta_step)

    @pl.when(odd_block)
    def _():
        side_ref[0] = before_odd_ref[...]
        side_ref[1] = after_odd_ref[...]

    @pl.when(jnp.logical_not(odd_block))
    def _():
        side_ref[0, 0:11] = before_even_ref[...]
        side_ref[1, 0:11] = after_even_ref[...]
        side_ref[:, 11] = jnp.zeros((2, LEVELS, CELLS_T), F32)

    is_below = lane % 2 == 1
    level_of = (lane % 16) // 2
    first_below, first_above = below_above(one_even_ref[...], two_even_ref[...])
    second_below, second_above = below_above(one_odd_ref[...], two_odd_ref[...])
    below = jnp.where(odd_block, second_below, first_below)
    above = jnp.where(odd_block, second_above, first_above)
    beside = jnp.where(is_below, below, above)

    def swapped(block):
        return jnp.where(is_below, pltpu.roll(block, 1, 1), pltpu.roll(block, CELLS_T - 1, 1))

    def corner(side):
        tile = side_ref[side, 11]
        held = jnp.where(lane_flat[0:1] % 2 == 1, tile[0:1], tile[1:2])
        spot = 2 * row_flat
        total = jnp.zeros(flat, F32)
        for comp in range(6):
            start = 6 * side + comp
            for block, shift in ((second_below, 1), (second_above, 0)):
                column = block[0:LEVELS, start : start + 1]
                total = jnp.where(lane_flat == spot + (16 * comp + shift), column, total)
        return jnp.where(odd_block, held, jnp.sum(total, axis=0, keepdims=True))

    corners = (corner(0), corner(1))
    inverse_r = 1.0 / radius(level_of, spacing)
    own_step = jnp.where((level_of == 0) | (level_of == LEVELS - 1), 1.0 / spacing, 0.5 / spacing)
    up = jnp.where(level_of == LEVELS - 1, beside, pltpu.roll(beside, CELLS_T - 2, 1))
    down = jnp.where(level_of == 0, beside, pltpu.roll(beside, 2, 1))
    pack_r = (up - down) * own_step
    inner = jnp.where(is_below, high_ref[...], low_ref[...])
    outer = jnp.where(is_below, above, below)
    pack_t = swapped(inner - outer) * (
        jnp.where(is_below, 0.5 / theta_step, -0.5 / theta_step) * inverse_r
    )
    t_index = first_t + jnp.where(is_below[0:8], -1, CELLS_T)
    edge_sine = inverse_sine(t_index, theta_step)[0:1]
    up = jnp.where(last_row, corners[1], pltpu.roll(beside, CELLS_P - 1, 0))
    down = jnp.where(first_row, corners[0], pltpu.roll(beside, 1, 0))
    pack_p = (up - down) * (edge_sine * inverse_r * (0.5 / phi_step))

    def spread(block):
        return [block if comp == 0 else pltpu.roll(block, CELLS_T - 16 * comp, 1) for comp in range(6)]

    edge = flux_of(
        spread(beside), spread(pack_r), spread(pack_t), spread(pack_p), spacing, ALONG_T
    )
    outside = (is_below & (lat == 0)) | ((lane % 2 == 0) & (lat == lat_blocks - 1))
    for slot, chan in enumerate(ALONG_T):
        edge_t_ref[slot] = jnp.where(outside, 0.0, edge[chan])

    level_step = jnp.where(
        (row_flat == 0) | (row_flat == LEVELS - 1), 1.0 / spacing, 0.5 / spacing
    )
    inverse_flat = 1.0 / radius(row_flat, spacing)
    step_t = inverse_flat * (0.5 / theta_step)
    step_p = own_sine * inverse_flat * (0.5 / phi_step)
    for kind in range(4):
        side, own = kind % 2, kind // 2 == 1
        edge_row_ref = first_ref if side == 0 else last_ref
        if own:
            center = [edge_row_ref[comp] for comp in range(6)]
            near = [side_ref[side, comp] for comp in range(5)]
            away = [edge_row_ref[6 + comp] for comp in range(5)]
            start = 0 if side == 0 else CELLS_P - 1
            ends = beside[start : start + 1]
        else:
            center = [side_ref[side, comp] for comp in range(6)]
            near = [side_ref[side, 6 + comp] for comp in range(5)]
            away = [edge_row_ref[comp] for comp in range(5)]
            ends = corners[side]
        ends = jnp.broadcast_to(ends, flat)
        grad_r, grad_t, grad_p = [], [], []
        for comp in range(6):
            block = center[comp]
            up = jnp.where(row_flat == LEVELS - 1, block, pltpu.roll(block, LEVELS - 1, 0))
            down = jnp.where(row_flat == 0, block, pltpu.roll(block, 1, 0))
            grad_r.append((up - down) * level_step)
            spot = 16 * comp + 2 * row_flat
            before = jnp.sum(jnp.where(lane_flat == spot + 1, ends, 0.0), axis=1, keepdims=True)
            after = jnp.sum(jnp.where(lane_flat == spot, ends, 0.0), axis=1, keepdims=True)
            up = jnp.where(lane_flat == CELLS_T - 1, after, pltpu.roll(block, CELLS_T - 1, 1))
            down = jnp.where(lane_flat == 0, before, pltpu.roll(block, 1, 1))
            grad_t.append((up - down) * step_t)
            if comp < 5:
                gap = away[comp] - near[comp] if side == 0 else near[comp] - away[comp]
                grad_p.append(gap * step_p)
            else:
                grad_p.append(None)
        if own:
            edge = flux_of(center, grad_r, grad_t, grad_p, spacing, range(9))
            for chan in range(9):
                flux_ref[chan, :, 0 if side == 0 else CELLS_P - 1, :] = edge[chan]
        else:
            edge = flux_of(center, grad_r, grad_t, grad_p, spacing, ALONG_P)
            outside = lon == (0 if side == 0 else lon_blocks - 1)
            for slot, chan in enumerate(ALONG_P):
                edge_p_ref[side, slot] = jnp.where(outside, 0.0, edge[chan])

    def along_p(block, before, after, step):
        up = jnp.where(last_row, after, pltpu.roll(block, CELLS_P - 1, 0))
        down = jnp.where(first_row, before, pltpu.roll(block, 1, 0))
        return (up - down) * step

    def advance(level, carry):
        low_level, high_level, step_r, step_t, step_p = level_steps(
            level, own_sine, steps, time_step
        )

        def d_r(chan):
            return (flux_ref[chan, high_level] - flux_ref[chan, low_level]) * step_r

        def d_t(chan):
            slot = ALONG_T.index(chan)
            ends = pltpu.roll(edge_t_ref[slot], CELLS_T - 1 - 2 * level, 1)
            return along_t(flux_ref[chan, level], ends, step_t)

        def d_p(chan):
            slot = ALONG_P.index(chan)
            before = edge_p_ref[0, slot, pl.ds(level, 1), :]
            after = edge_p_ref[1, slot, pl.ds(level, 1), :]
            return along_p(flux_ref[chan, level], before, after, step_p)

        new_vel_ref[0, 0, level] = vel_ref[0, 0, level] - (d_r(0) + d_t(1) + d_p(2))
        new_vel_ref[0, 1, level] = vel_ref[0, 1, level] - (d_r(1) + d_t(3) + d_p(4))
        new_vel_ref[0, 2, level] = vel_ref[0, 2, level] - (d_r(2) + d_t(4) + d_p(5))
        new_mag_ref[0, 0, level] = mag_ref[0, 0, level] + (d_t(8) - d_p(7))
        new_mag_ref[0, 1, level] = mag_ref[0, 1, level] + (d_p(6) - d_r(8))
        new_mag_ref[0, 2, level] = mag_ref[0, 2, level] + (d_r(7) - d_t(6))
        return carry

    lax.fori_loop(0, LEVELS, advance, 0, unroll=8)

    slots_total = spot_ref.shape[-1]
    chunks = slots_total // CELLS_T
    taken_ref[6:8] = jnp.zeros((2, LEVELS, slots_total), F32)
    taken_ref[6, 0:1] = slot_ref[0, 0].astype(F32)
    sub = rows_of((8, CELLS_T))

    def fold(blocks):
        for width in (4, 2, 1):
            keep = sub % (2 * width) < width
            half = len(blocks) // 2
            merged = []
            for one, two in zip(blocks[:half], blocks[half:]):
                mine, other = jnp.where(keep, one, two), jnp.where(keep, two, one)
                moved = pltpu.roll(other, width, 0)
                if width < 4:
                    moved = jnp.where(keep, pltpu.roll(other, 8 - width, 0), moved)
                merged.append(mine + moved)
            blocks = merged
        return blocks[0]

    for chunk in range(chunks):
        part = slice(chunk * CELLS_T, (chunk + 1) * CELLS_T)
        where_t = spot_ref[:, part]
        weights = [factor_ref[step, :, part] for step in range(CELLS_P // 8)]
        for start, ref in ((0, new_vel_ref), (3, new_mag_ref)):

            def take(comp, carry, start=start, ref=ref, part=part, where_t=where_t, weights=weights):
                sums = []
                for level in range(LEVELS):
                    block = ref[0, comp, level]
                    total = 0.0
                    for step in range(CELLS_P // 8):
                        got = jnp.take_along_axis(
                            block[8 * step : 8 * step + 8],
                            where_t,
                            axis=1,
                            mode="promise_in_bounds",
                        )
                        total = total + got * weights[step]
                    sums.append(total)
                taken_ref[start + comp, :, part] = fold(sums)

            for comp in range(3):
                take(comp, 0)

    for chunk in range(chunks):
        part = taken_ref[:, :, chunk * CELLS_T : (chunk + 1) * CELLS_T].reshape(64, CELLS_T)
        both = jnp.concatenate([part, pltpu.roll(part, CELLS_T - 8, 1)], axis=0)
        turned = jnp.transpose(both)
        for block in range(8):
            send_ref[chunk * 8 + block] = turned[16 * block : 16 * block + 8]


def store_kernel(vel_ref, mag_ref, out_vel_ref, out_mag_ref, sem_ref):
    copies = [
        pltpu.make_async_copy(vel_ref, out_vel_ref, sem_ref.at[0]),
        pltpu.make_async_copy(mag_ref, out_mag_ref, sem_ref.at[1]),
    ]
    for copy in copies:
        copy.start()
    for copy in copies:
        copy.wait()


def donors_kernel(lon_blocks, rows_ref, cell_ref, weight_ref, spot_ref, factor_ref):
    slots_total = cell_ref.shape[-1]
    rows_wide = jnp.broadcast_to(rows_ref[0, 0].astype(F32), (8, lon_blocks))
    owner = lanes_of((lon_blocks, slots_total)) // CAP == rows_of((lon_blocks, slots_total))
    counts = jnp.dot(rows_wide, owner.astype(F32), preferred_element_type=F32)
    bucket = lanes_of((8, slots_total)) % CAP
    live = bucket < (counts + 0.5).astype(jnp.int32)
    scale = jnp.where(live, jnp.broadcast_to(weight_ref[0, 0], (8, slots_total)), 0.0)
    cells = jnp.broadcast_to(cell_ref[0, 0], (8, slots_total))
    spot_ref[...] = cells % CELLS_T
    cell_p = cells // CELLS_T
    for step in range(CELLS_P // 8):
        factor_ref[step] = jnp.where(cell_p == 8 * step + rows_of(cells.shape), scale, 0.0)


def collect_kernel(got_ref, near_ref, far_ref):
    sources = got_ref.shape[0]
    rows = sources * 8
    totals = []
    for half in range(2):
        got = got_ref[:, 8 * half : 8 * half + 8].reshape(rows, CELLS_T)
        total = jnp.zeros((48, CYCLE), F32)
        for start in (0, 64):
            slot = got[:, start + 48 : start + 49].astype(jnp.int32)
            onehot = (slot == lanes_of((rows, CYCLE))).astype(F32)
            part = lax.dot_general(
                got,
                onehot,
                (((0,), (0,)), ((), ())),
                precision=lax.Precision.HIGHEST,
                preferred_element_type=F32,
            )
            total = total + part[start : start + 48]
        totals.append(total)
    odd = lax.axis_index("lon") % 2 == 1
    near_ref[0, 0, 0] = jnp.where(odd, totals[1], totals[0])
    far_ref[0, 0, 0] = jnp.where(odd, totals[0], totals[1])


VMEM = pl.BlockSpec(memory_space=pltpu.VMEM)
HBM = pl.BlockSpec(memory_space=pltpu.HBM)


def limit(mebibytes):
    return pltpu.CompilerParams(vmem_limit_bytes=mebibytes * 1024 * 1024)


def tiles(*shape):
    return jax.ShapeDtypeStruct(shape, F32)


def local(velocity, magnetic, pair_rows, send_cell, send_weight, cycle_slot):
    lat_blocks, lon_blocks = lax.axis_size("lat"), lax.axis_size("lon")
    theta_step = 0.5 * math.pi / (lat_blocks * CELLS_T)
    phi_step = 1.5 * math.pi / (lon_blocks * CELLS_P)
    spacing = inner_radius * theta_step
    pack = tiles(CELLS_P, CELLS_T)
    strip = tiles(11, LEVELS, CELLS_T)
    strip_full = tiles(12, LEVELS, CELLS_T)
    evens, odds = range(0, lon_blocks, 2), range(1, lon_blocks, 2)

    def along_lon(block, step, lons):
        pairs = [(lon, lon + step) for lon in lons if 0 <= lon + step < lon_blocks]
        return lax.ppermute(block, "lon", pairs)

    def between_lat(block, start, lons):
        pairs = [
            (lat * lon_blocks + lon, other * lon_blocks + lon)
            for first_lat in range(start, lat_blocks - 1, 2)
            for lat, other in ((first_lat, first_lat + 1), (first_lat + 1, first_lat))
            for lon in lons
        ]
        return lax.ppermute(block, ("lat", "lon"), pairs)

    low, high, first, last, one, two = pl.pallas_call(
        edges_kernel,
        in_specs=[VMEM] * 2,
        out_specs=[VMEM] * 6,
        out_shape=[pack, pack, strip, strip, pack, pack],
        compiler_params=limit(4),
        name="edges",
    )(velocity, magnetic)
    one_even = between_lat(one, 0, evens)
    two_even = between_lat(two, 1, evens)
    before_even = along_lon(last, 1, odds)
    after_even = along_lon(first, -1, odds)
    first_full, last_full = pl.pallas_call(
        corners_kernel,
        in_specs=[VMEM] * 6,
        out_specs=[VMEM] * 2,
        out_shape=[strip_full, strip_full],
        compiler_params=limit(4),
        name="corners",
    )(one_even, two_even, first, last, before_even, after_even)
    before_odd = along_lon(last_full, 1, evens)
    after_odd = along_lon(first_full, -1, evens)
    second_one, second_two = pl.pallas_call(
        second_kernel,
        in_specs=[VMEM] * 4,
        out_specs=[VMEM] * 2,
        out_shape=[pack, pack],
        compiler_params=limit(4),
        name="second",
    )(before_even, after_even, low, high)
    one_odd = between_lat(second_one, 0, range(lon_blocks))
    two_odd = between_lat(second_two, 1, range(lon_blocks))
    slots_total = send_cell.shape[-1]
    steps = (spacing, theta_step, phi_step)

    def donors(*refs):
        donors_kernel(lon_blocks, *refs)

    spots, factors = pl.pallas_call(
        donors,
        in_specs=[VMEM] * 3,
        out_specs=[VMEM] * 2,
        out_shape=[
            jax.ShapeDtypeStruct((8, slots_total), jnp.int32),
            tiles(CELLS_P // 8, 8, slots_total),
        ],
        compiler_params=limit(4),
        cost_estimate=pl.CostEstimate(flops=0, bytes_accessed=1, transcendentals=0),
        name="donors",
    )(pair_rows, send_cell, send_weight)

    def section(*refs):
        section_kernel(steps, lat_blocks, lon_blocks, *refs)

    def flux_of_cells(parity, one, two, *given):
        def kernel(*refs):
            flux_kernel(steps, parity, *refs)

        return pl.pallas_call(
            kernel,
            in_specs=[VMEM] * (4 + len(given)),
            out_specs=VMEM,
            out_shape=tiles(9, LEVELS, CELLS_P, CELLS_T),
            input_output_aliases={4: 0} if given else {},
            compiler_params=limit(8),
            name="flux",
        )(velocity, magnetic, one, two, *given)

    flux = flux_of_cells(0, one_even, two_even)
    flux = flux_of_cells(1, one_odd, two_odd, flux)
    new_velocity, new_magnetic, payload, _ = pl.pallas_call(
        section,
        in_specs=[VMEM] * 18,
        out_specs=[VMEM] * 4,
        out_shape=[
            tiles(*velocity.shape),
            tiles(*magnetic.shape),
            tiles(lon_blocks, 8, CELLS_T),
            tiles(9, LEVELS, CELLS_P, CELLS_T),
        ],
        input_output_aliases={17: 3},
        scratch_shapes=[
            pltpu.VMEM((5, CELLS_P, CELLS_T), F32),
            pltpu.VMEM((2, 5, LEVELS, CELLS_T), F32),
            pltpu.VMEM((8, LEVELS, slots_total), F32),
            pltpu.VMEM((2, 12, LEVELS, CELLS_T), F32),
        ],
        compiler_params=limit(16),
        name="section",
    )(
        velocity,
        magnetic,
        low,
        high,
        one_even,
        two_even,
        one_odd,
        two_odd,
        first,
        last,
        before_even,
        after_even,
        before_odd,
        after_odd,
        spots,
        factors,
        cycle_slot,
        flux,
    )
    new_velocity, new_magnetic = pl.pallas_call(
        store_kernel,
        in_specs=[VMEM] * 2,
        out_specs=[HBM] * 2,
        out_shape=[tiles(*velocity.shape), tiles(*magnetic.shape)],
        scratch_shapes=[pltpu.SemaphoreType.DMA((2,))],
        compiler_params=limit(4),
        name="store",
    )(new_velocity, new_magnetic)
    pairs = lon_blocks // 2
    groups = [[2 * pair + parity for pair in range(pairs)] for parity in range(2)]
    payload = lax.all_to_all(
        payload.reshape(pairs, 16, CELLS_T),
        "lon",
        split_axis=0,
        concat_axis=0,
        axis_index_groups=groups,
        tiled=True,
    )
    near, far = pl.pallas_call(
        collect_kernel,
        in_specs=[VMEM],
        out_specs=[VMEM] * 2,
        out_shape=[tiles(1, 1, 1, 48, CYCLE)] * 2,
        compiler_params=limit(4),
        name="collect",
    )(payload)
    across = [
        (grid * lon_blocks + lon, (1 - grid) * lon_blocks + (lon ^ 1))
        for grid in range(2)
        for lon in range(lon_blocks)
    ]
    far = lax.ppermute(far, ("grid", "lon"), across)
    near = lax.ppermute(near, "grid", [(0, 1), (1, 0)])
    cycle = far + near
    return (new_velocity, new_magnetic, cycle)


def solution(mesh):
    state = P("grid", None, None, "lon", "lat")
    rows = P("grid", "lat", "lon", None)
    return jax.shard_map(
        local,
        mesh=mesh,
        in_specs=(state, state, rows, rows, rows, rows),
        out_specs=(state, state, P("grid", "lat", "lon", None, None)),
        check_vma=False,
    )
```

```python
import math

import jax
import jax.numpy as jnp
from jax import lax
from jax.experimental import pallas as pl
from jax.experimental.pallas import tpu as pltpu
from jax.sharding import PartitionSpec as P

CAP = 16
CYCLE = 128
LEVELS = 8
CELLS_P = 32
CELLS_T = 128

inner_radius = 0.6
smag_const = 0.2
aniso_weight = 0.8
turb_prandtl = 0.7
courant = 0.2

ALONG_R = (0, 1, 2, 7, 8)
ALONG_T = (1, 3, 4, 6, 8)
ALONG_P = (2, 4, 5, 6, 7)
F32 = jnp.float32


def lanes_of(shape):
    return lax.broadcasted_iota(jnp.int32, shape, len(shape) - 1)


def rows_of(shape):
    return lax.broadcasted_iota(jnp.int32, shape, len(shape) - 2)


def pick(vel_ref, mag_ref, comp):
    return (vel_ref, comp) if comp < 3 else (mag_ref, comp - 3)


def edges_kernel(
    vel_ref,
    mag_ref,
    low_ref,
    high_ref,
    first_ref,
    last_ref,
    one_ref,
    two_ref,
    held_vel_ref,
    held_mag_ref,
    sem_ref,
):
    copies = []
    for comp in range(6):
        ref, index = pick(vel_ref, mag_ref, comp)
        held, _ = pick(held_vel_ref, held_mag_ref, comp)
        copies.append(
            pltpu.make_async_copy(ref.at[0, index], held.at[0, index], sem_ref.at[comp])
        )
    for copy in copies:
        copy.start()
    pair = lanes_of((CELLS_P, CELLS_T)) // 2
    low = jnp.zeros((CELLS_P, CELLS_T), F32)
    high = jnp.zeros((CELLS_P, CELLS_T), F32)
    for comp in range(6):
        copies[comp].wait()
        ref, index = pick(held_vel_ref, held_mag_ref, comp)
        for level in range(LEVELS):
            place = 16 * comp + 2 * level
            block = ref[0, index, level]
            if place:
                block = pltpu.roll(block, place, 1)
            low = jnp.where(pair == place // 2, block, low)
            high = jnp.where(pair == (place // 2 - 1) % (CELLS_T // 2), block, high)
        first_ref[comp] = ref[0, index, :, 0, :]
        last_ref[comp] = ref[0, index, :, CELLS_P - 1, :]
        if comp < 5:
            first_ref[6 + comp] = ref[0, index, :, 1, :]
            last_ref[6 + comp] = ref[0, index, :, CELLS_P - 2, :]
    high = pltpu.roll(high, 2, 1)
    low_ref[...] = low
    high_ref[...] = high
    upward = lax.axis_index("lat") % 2 == 0
    one_ref[...] = jnp.where(upward, high, low)
    two_ref[...] = jnp.where(upward, low, high)


def below_above(one, two):
    upward = lax.axis_index("lat") % 2 == 0
    return jnp.where(upward, two, one), jnp.where(upward, one, two)


def corners_kernel(
    one_ref,
    two_ref,
    first_ref,
    last_ref,
    before_ref,
    after_ref,
    flux_ref,
    first_out_ref,
    last_out_ref,
):
    shape = (LEVELS, CELLS_T)
    for row, source, target in ((0, first_ref, first_out_ref), (CELLS_P - 1, last_ref, last_out_ref)):
        below, above = below_above(one_ref[row : row + 1, :], two_ref[row : row + 1, :])
        below = jnp.broadcast_to(below, shape)
        above = jnp.broadcast_to(above, shape)
        target[0:11] = source[...]
        target[11] = jnp.where(rows_of(shape) == 0, below, above)


def second_kernel(before_ref, after_ref, low_ref, high_ref, one_ref, two_ref):
    upward = lax.axis_index("lat") % 2 == 0

    odd = lax.axis_index("lon") % 2

    @pl.when(odd == 1)
    def _():
        one_ref[...] = jnp.where(upward, high_ref[...], low_ref[...])
        two_ref[...] = jnp.where(upward, low_ref[...], high_ref[...])

    @pl.when(odd == 0)
    def _():
        lane = lanes_of((LEVELS, CELLS_T))
        low = jnp.zeros((LEVELS, CELLS_T), F32)
        high = jnp.zeros((LEVELS, CELLS_T), F32)
        for side, ref in ((0, before_ref), (1, after_ref)):
            for comp in range(6):
                spot = 6 * side + comp
                block = ref[comp]
                low = jnp.where(lane == spot, pltpu.roll(block, spot, 1) if spot else block, low)
                high = jnp.where(lane == spot, pltpu.roll(block, spot + 1, 1), high)
        one_ref[0:LEVELS] = jnp.where(upward, high, low)
        two_ref[0:LEVELS] = jnp.where(upward, low, high)
        one_ref[LEVELS:] = jnp.zeros((CELLS_P - LEVELS, CELLS_T), F32)
        two_ref[LEVELS:] = jnp.zeros((CELLS_P - LEVELS, CELLS_T), F32)


def flux_of(center, grad_r, grad_t, grad_p, spacing, wanted):
    u0, u1, u2, b0, b1, b2 = center
    s00, s11, s22 = grad_r[0], grad_t[1], grad_p[2]
    d01 = grad_t[0] + grad_r[1]
    d02 = grad_p[0] + grad_r[2]
    d12 = grad_p[1] + grad_t[2]
    squares = 2.0 * (s00 * s00 + s11 * s11 + s22 * s22) + (d01 * d01 + d02 * d02 + d12 * d12)
    viscous = jnp.sqrt(squares) * ((smag_const * spacing) ** 2)
    q00, q11, q22 = b0 * b0, b1 * b1, b2 * b2
    field_sq = q00 + q11 + q22
    inverse = 1.0 / (field_sq + 1.0)
    q01, q02, q12 = b0 * b1, b0 * b2, b1 * b2
    aligned = q00 * s00 + q11 * s11 + q22 * s22 + (q01 * d01 + q02 * d02 + q12 * d12)
    weight = (2.0 * aniso_weight) * viscous * aligned * inverse * inverse - 1.0
    half = 0.5 * field_sq
    twice = viscous + viscous
    ratio = viscous * (1.0 / turb_prandtl)
    result = {}
    for chan in wanted:
        if chan == 0:
            result[0] = u0 * u0 + q00 * weight - twice * s00 + half
        elif chan == 1:
            result[1] = u0 * u1 + q01 * weight - viscous * d01
        elif chan == 2:
            result[2] = u0 * u2 + q02 * weight - viscous * d02
        elif chan == 3:
            result[3] = u1 * u1 + q11 * weight - twice * s11 + half
        elif chan == 4:
            result[4] = u1 * u2 + q12 * weight - viscous * d12
        elif chan == 5:
            result[5] = u2 * u2 + q22 * weight - twice * s22 + half
        elif chan == 6:
            result[6] = u1 * b2 - u2 * b1 - ratio * (grad_t[5] - grad_p[4])
        elif chan == 7:
            result[7] = u2 * b0 - u0 * b2 - ratio * (grad_p[3] - grad_r[5])
        else:
            result[8] = u0 * b1 - u1 * b0 - ratio * (grad_r[4] - grad_t[3])
    return result


def radius(level, spacing):
    return inner_radius + (level.astype(F32) + 0.5) * spacing


def inverse_sine(index, theta_step):
    return 1.0 / jnp.sin(0.25 * math.pi + (index.astype(F32) + 0.5) * theta_step)


def level_steps(level, sine, steps, scale):
    spacing, theta_step, phi_step = steps
    low_level = jnp.maximum(level - 1, 0)
    high_level = jnp.minimum(level + 1, LEVELS - 1)
    ends = (level == 0) | (level == LEVELS - 1)
    step_r = jnp.where(ends, scale / spacing, 0.5 * scale / spacing)
    inverse = 1.0 / radius(jnp.full((8, CELLS_T), level, jnp.int32), spacing)
    step_t = (inverse * (0.5 * scale / theta_step))[0:1]
    step_p = (sine * inverse * (0.5 * scale / phi_step))[0:1]
    return low_level, high_level, step_r, step_t, step_p


def along_t(block, ends, step):
    lane = lanes_of(block.shape)
    up = jnp.where(lane == CELLS_T - 1, ends, pltpu.roll(block, CELLS_T - 1, 1))
    down = jnp.where(lane == 0, ends, pltpu.roll(block, 1, 1))
    return (up - down) * step


def flux_kernel(steps, parity, vel_ref, mag_ref, one_ref, two_ref, *rest):
    flux_ref = rest[-1]
    wide = (CELLS_P, CELLS_T)

    @pl.when(lax.axis_index("lon") % 2 == parity)
    def _():
        is_below = lanes_of(wide) % 2 == 1
        below, above = below_above(one_ref[...], two_ref[...])
        beside = jnp.where(is_below, below, above)
        own_sine = inverse_sine(lax.axis_index("lat") * CELLS_T + lanes_of((8, CELLS_T)), steps[1])

        def make_flux(level, carry):
            low_level, high_level, step_r, step_t, step_p = level_steps(level, own_sine, steps, 1.0)
            center, grad_r, grad_t, grad_p = [], [], [], []
            for comp in range(6):
                ref, index = pick(vel_ref, mag_ref, comp)
                block = ref[0, index, level]
                center.append(block)
                grad_r.append((ref[0, index, high_level] - ref[0, index, low_level]) * step_r)
                ends = pltpu.roll(beside, 2 * CELLS_T - 1 - 16 * comp - 2 * level, 1)
                grad_t.append(along_t(block, ends, step_t))
                gap = pltpu.roll(block, CELLS_P - 1, 0) - pltpu.roll(block, 1, 0)
                grad_p.append(gap * step_p)
            flux = flux_of(center, grad_r, grad_t, grad_p, steps[0], range(9))
            for chan in range(9):
                flux_ref[chan, level] = flux[chan]
            return carry

        lax.fori_loop(0, LEVELS, make_flux, 0, unroll=8)


def section_kernel(
    steps,
    lat_blocks,
    lon_blocks,
    vel_ref,
    mag_ref,
    low_ref,
    high_ref,
    one_even_ref,
    two_even_ref,
    one_odd_ref,
    two_odd_ref,
    first_ref,
    last_ref,
    before_even_ref,
    after_even_ref,
    before_odd_ref,
    after_odd_ref,
    spot_ref,
    factor_ref,
    slot_ref,
    flux_in_ref,
    new_vel_ref,
    new_mag_ref,
    send_ref,
    flux_ref,
    edge_t_ref,
    edge_p_ref,
    taken_ref,
    side_ref,
):
    spacing, theta_step, phi_step = steps
    lat = lax.axis_index("lat")
    lon = lax.axis_index("lon")
    odd_block = lon % 2 == 1
    time_step = courant * spacing
    wide = (CELLS_P, CELLS_T)
    flat = (LEVELS, CELLS_T)
    lane = lanes_of(wide)
    row = rows_of(wide)
    lane_flat = lanes_of(flat)
    row_flat = rows_of(flat)
    first_row, last_row = row == 0, row == CELLS_P - 1
    first_t = lat * CELLS_T
    own_sine = inverse_sine(first_t + lanes_of((8, CELLS_T)), theta_step)

    @pl.when(odd_block)
    def _():
        side_ref[0] = before_odd_ref[...]
        side_ref[1] = after_odd_ref[...]

    @pl.when(jnp.logical_not(odd_block))
    def _():
        side_ref[0, 0:11] = before_even_ref[...]
        side_ref[1, 0:11] = after_even_ref[...]
        side_ref[:, 11] = jnp.zeros((2, LEVELS, CELLS_T), F32)

    is_below = lane % 2 == 1
    level_of = (lane % 16) // 2
    first_below, first_above = below_above(one_even_ref[...], two_even_ref[...])
    second_below, second_above = below_above(one_odd_ref[...], two_odd_ref[...])
    below = jnp.where(odd_block, second_below, first_below)
    above = jnp.where(odd_block, second_above, first_above)
    beside = jnp.where(is_below, below, above)

    def swapped(block):
        return jnp.where(is_below, pltpu.roll(block, 1, 1), pltpu.roll(block, CELLS_T - 1, 1))

    def corner(side):
        tile = side_ref[side, 11]
        held = jnp.where(lane_flat[0:1] % 2 == 1, tile[0:1], tile[1:2])
        spot = 2 * row_flat
        total = jnp.zeros(flat, F32)
        for comp in range(6):
            start = 6 * side + comp
            for block, shift in ((second_below, 1), (second_above, 0)):
                column = block[0:LEVELS, start : start + 1]
                total = jnp.where(lane_flat == spot + (16 * comp + shift), column, total)
        return jnp.where(odd_block, held, jnp.sum(total, axis=0, keepdims=True))

    corners = (corner(0), corner(1))
    inverse_r = 1.0 / radius(level_of, spacing)
    own_step = jnp.where((level_of == 0) | (level_of == LEVELS - 1), 1.0 / spacing, 0.5 / spacing)
    up = jnp.where(level_of == LEVELS - 1, beside, pltpu.roll(beside, CELLS_T - 2, 1))
    down = jnp.where(level_of == 0, beside, pltpu.roll(beside, 2, 1))
    pack_r = (up - down) * own_step
    inner = jnp.where(is_below, high_ref[...], low_ref[...])
    outer = jnp.where(is_below, above, below)
    pack_t = swapped(inner - outer) * (
        jnp.where(is_below, 0.5 / theta_step, -0.5 / theta_step) * inverse_r
    )
    t_index = first_t + jnp.where(is_below[0:8], -1, CELLS_T)
    edge_sine = inverse_sine(t_index, theta_step)[0:1]
    up = jnp.where(last_row, corners[1], pltpu.roll(beside, CELLS_P - 1, 0))
    down = jnp.where(first_row, corners[0], pltpu.roll(beside, 1, 0))
    pack_p = (up - down) * (edge_sine * inverse_r * (0.5 / phi_step))

    def spread(block):
        return [block if comp == 0 else pltpu.roll(block, CELLS_T - 16 * comp, 1) for comp in range(6)]

    edge = flux_of(
        spread(beside), spread(pack_r), spread(pack_t), spread(pack_p), spacing, ALONG_T
    )
    outside = (is_below & (lat == 0)) | ((lane % 2 == 0) & (lat == lat_blocks - 1))
    for slot, chan in enumerate(ALONG_T):
        edge_t_ref[slot] = jnp.where(outside, 0.0, edge[chan])

    level_step = jnp.where(
        (row_flat == 0) | (row_flat == LEVELS - 1), 1.0 / spacing, 0.5 / spacing
    )
    inverse_flat = 1.0 / radius(row_flat, spacing)
    step_t = inverse_flat * (0.5 / theta_step)
    step_p = own_sine * inverse_flat * (0.5 / phi_step)
    for kind in range(4):
        side, own = kind % 2, kind // 2 == 1
        edge_row_ref = first_ref if side == 0 else last_ref
        if own:
            center = [edge_row_ref[comp] for comp in range(6)]
            near = [side_ref[side, comp] for comp in range(5)]
            away = [edge_row_ref[6 + comp] for comp in range(5)]
            start = 0 if side == 0 else CELLS_P - 1
            ends = beside[start : start + 1]
        else:
            center = [side_ref[side, comp] for comp in range(6)]
            near = [side_ref[side, 6 + comp] for comp in range(5)]
            away = [edge_row_ref[comp] for comp in range(5)]
            ends = corners[side]
        ends = jnp.broadcast_to(ends, flat)
        grad_r, grad_t, grad_p = [], [], []
        for comp in range(6):
            block = center[comp]
            up = jnp.where(row_flat == LEVELS - 1, block, pltpu.roll(block, LEVELS - 1, 0))
            down = jnp.where(row_flat == 0, block, pltpu.roll(block, 1, 0))
            grad_r.append((up - down) * level_step)
            spot = 16 * comp + 2 * row_flat
            before = jnp.sum(jnp.where(lane_flat == spot + 1, ends, 0.0), axis=1, keepdims=True)
            after = jnp.sum(jnp.where(lane_flat == spot, ends, 0.0), axis=1, keepdims=True)
            up = jnp.where(lane_flat == CELLS_T - 1, after, pltpu.roll(block, CELLS_T - 1, 1))
            down = jnp.where(lane_flat == 0, before, pltpu.roll(block, 1, 1))
            grad_t.append((up - down) * step_t)
            if comp < 5:
                gap = away[comp] - near[comp] if side == 0 else near[comp] - away[comp]
                grad_p.append(gap * step_p)
            else:
                grad_p.append(None)
        if own:
            edge = flux_of(center, grad_r, grad_t, grad_p, spacing, range(9))
            for chan in range(9):
                flux_ref[chan, :, 0 if side == 0 else CELLS_P - 1, :] = edge[chan]
        else:
            edge = flux_of(center, grad_r, grad_t, grad_p, spacing, ALONG_P)
            outside = lon == (0 if side == 0 else lon_blocks - 1)
            for slot, chan in enumerate(ALONG_P):
                edge_p_ref[side, slot] = jnp.where(outside, 0.0, edge[chan])

    def along_p(block, before, after, step):
        up = jnp.where(last_row, after, pltpu.roll(block, CELLS_P - 1, 0))
        down = jnp.where(first_row, before, pltpu.roll(block, 1, 0))
        return (up - down) * step

    def advance(level, carry):
        low_level, high_level, step_r, step_t, step_p = level_steps(
            level, own_sine, steps, time_step
        )

        def d_r(chan):
            return (flux_ref[chan, high_level] - flux_ref[chan, low_level]) * step_r

        def d_t(chan):
            slot = ALONG_T.index(chan)
            ends = pltpu.roll(edge_t_ref[slot], CELLS_T - 1 - 2 * level, 1)
            return along_t(flux_ref[chan, level], ends, step_t)

        def d_p(chan):
            slot = ALONG_P.index(chan)
            before = edge_p_ref[0, slot, pl.ds(level, 1), :]
            after = edge_p_ref[1, slot, pl.ds(level, 1), :]
            return along_p(flux_ref[chan, level], before, after, step_p)

        new_vel_ref[0, 0, level] = vel_ref[0, 0, level] - (d_r(0) + d_t(1) + d_p(2))
        new_vel_ref[0, 1, level] = vel_ref[0, 1, level] - (d_r(1) + d_t(3) + d_p(4))
        new_vel_ref[0, 2, level] = vel_ref[0, 2, level] - (d_r(2) + d_t(4) + d_p(5))
        new_mag_ref[0, 0, level] = mag_ref[0, 0, level] + (d_t(8) - d_p(7))
        new_mag_ref[0, 1, level] = mag_ref[0, 1, level] + (d_p(6) - d_r(8))
        new_mag_ref[0, 2, level] = mag_ref[0, 2, level] + (d_r(7) - d_t(6))
        return carry

    lax.fori_loop(0, LEVELS, advance, 0, unroll=8)

    slots_total = spot_ref.shape[-1]
    chunks = slots_total // CELLS_T
    taken_ref[6:8] = jnp.zeros((2, LEVELS, slots_total), F32)
    taken_ref[6, 0:1] = slot_ref[0, 0].astype(F32)
    sub = rows_of((8, CELLS_T))

    def fold(blocks):
        for width in (4, 2, 1):
            keep = sub % (2 * width) < width
            half = len(blocks) // 2
            merged = []
            for one, two in zip(blocks[:half], blocks[half:]):
                mine, other = jnp.where(keep, one, two), jnp.where(keep, two, one)
                moved = pltpu.roll(other, width, 0)
                if width < 4:
                    moved = jnp.where(keep, pltpu.roll(other, 8 - width, 0), moved)
                merged.append(mine + moved)
            blocks = merged
        return blocks[0]

    for chunk in range(chunks):
        part = slice(chunk * CELLS_T, (chunk + 1) * CELLS_T)
        where_t = spot_ref[:, part]
        weights = [factor_ref[step, :, part] for step in range(CELLS_P // 8)]
        for start, ref in ((0, new_vel_ref), (3, new_mag_ref)):

            def take(comp, carry, start=start, ref=ref, part=part, where_t=where_t, weights=weights):
                sums = []
                for level in range(LEVELS):
                    block = ref[0, comp, level]
                    total = 0.0
                    for step in range(CELLS_P // 8):
                        got = jnp.take_along_axis(
                            block[8 * step : 8 * step + 8],
                            where_t,
                            axis=1,
                            mode="promise_in_bounds",
                        )
                        total = total + got * weights[step]
                    sums.append(total)
                taken_ref[start + comp, :, part] = fold(sums)

            for comp in range(3):
                take(comp, 0)

    for chunk in range(chunks):
        part = taken_ref[:, :, chunk * CELLS_T : (chunk + 1) * CELLS_T].reshape(64, CELLS_T)
        both = jnp.concatenate([part, pltpu.roll(part, CELLS_T - 8, 1)], axis=0)
        turned = jnp.transpose(both)
        for block in range(8):
            send_ref[chunk * 8 + block] = turned[16 * block : 16 * block + 8]


def store_kernel(vel_ref, mag_ref, out_vel_ref, out_mag_ref, sem_ref):
    copies = [
        pltpu.make_async_copy(vel_ref, out_vel_ref, sem_ref.at[0]),
        pltpu.make_async_copy(mag_ref, out_mag_ref, sem_ref.at[1]),
    ]
    for copy in copies:
        copy.start()
    for copy in copies:
        copy.wait()


def donors_kernel(lon_blocks, rows_ref, cell_ref, weight_ref, spot_ref, factor_ref):
    slots_total = cell_ref.shape[-1]
    rows_wide = jnp.broadcast_to(rows_ref[0, 0].astype(F32), (8, lon_blocks))
    owner = lanes_of((lon_blocks, slots_total)) // CAP == rows_of((lon_blocks, slots_total))
    counts = jnp.dot(rows_wide, owner.astype(F32), preferred_element_type=F32)
    bucket = lanes_of((8, slots_total)) % CAP
    live = bucket < (counts + 0.5).astype(jnp.int32)
    scale = jnp.where(live, jnp.broadcast_to(weight_ref[0, 0], (8, slots_total)), 0.0)
    cells = jnp.broadcast_to(cell_ref[0, 0], (8, slots_total))
    spot_ref[...] = cells % CELLS_T
    cell_p = cells // CELLS_T
    for step in range(CELLS_P // 8):
        factor_ref[step] = jnp.where(cell_p == 8 * step + rows_of(cells.shape), scale, 0.0)


def collect_kernel(got_ref, near_ref, far_ref):
    sources = got_ref.shape[0]
    rows = sources * 8
    totals = []
    for half in range(2):
        got = got_ref[:, 8 * half : 8 * half + 8].reshape(rows, CELLS_T)
        total = jnp.zeros((48, CYCLE), F32)
        for start in (0, 64):
            slot = got[:, start + 48 : start + 49].astype(jnp.int32)
            onehot = (slot == lanes_of((rows, CYCLE))).astype(F32)
            part = lax.dot_general(
                got,
                onehot,
                (((0,), (0,)), ((), ())),
                precision=lax.Precision.HIGHEST,
                preferred_element_type=F32,
            )
            total = total + part[start : start + 48]
        totals.append(total)
    odd = lax.axis_index("lon") % 2 == 1
    near_ref[0, 0, 0] = jnp.where(odd, totals[1], totals[0])
    far_ref[0, 0, 0] = jnp.where(odd, totals[0], totals[1])


VMEM = pl.BlockSpec(memory_space=pltpu.VMEM)
HBM = pl.BlockSpec(memory_space=pltpu.HBM)


def limit(mebibytes):
    return pltpu.CompilerParams(vmem_limit_bytes=mebibytes * 1024 * 1024)


def tiles(*shape):
    return jax.ShapeDtypeStruct(shape, F32)


def local(velocity, magnetic, pair_rows, send_cell, send_weight, cycle_slot):
    lat_blocks, lon_blocks = lax.axis_size("lat"), lax.axis_size("lon")
    theta_step = 0.5 * math.pi / (lat_blocks * CELLS_T)
    phi_step = 1.5 * math.pi / (lon_blocks * CELLS_P)
    spacing = inner_radius * theta_step
    pack = tiles(CELLS_P, CELLS_T)
    strip = tiles(11, LEVELS, CELLS_T)
    strip_full = tiles(12, LEVELS, CELLS_T)
    evens, odds = range(0, lon_blocks, 2), range(1, lon_blocks, 2)

    def along_lon(block, step, lons):
        pairs = [(lon, lon + step) for lon in lons if 0 <= lon + step < lon_blocks]
        return lax.ppermute(block, "lon", pairs)

    def between_lat(block, start, lons):
        pairs = [
            (lat * lon_blocks + lon, other * lon_blocks + lon)
            for first_lat in range(start, lat_blocks - 1, 2)
            for lat, other in ((first_lat, first_lat + 1), (first_lat + 1, first_lat))
            for lon in lons
        ]
        return lax.ppermute(block, ("lat", "lon"), pairs)

    low, high, first, last, one, two, held_vel, held_mag = pl.pallas_call(
        edges_kernel,
        in_specs=[HBM] * 2,
        out_specs=[VMEM] * 8,
        out_shape=[
            pack,
            pack,
            strip,
            strip,
            pack,
            pack,
            tiles(*velocity.shape),
            tiles(*magnetic.shape),
        ],
        scratch_shapes=[
            pltpu.SemaphoreType.DMA((6,)),
        ],
        compiler_params=limit(4),
        name="edges",
    )(*(pltpu.with_memory_space_constraint(array, pltpu.HBM) for array in (velocity, magnetic)))
    one_even = between_lat(one, 0, evens)
    two_even = between_lat(two, 1, evens)
    before_even = along_lon(last, 1, odds)
    after_even = along_lon(first, -1, odds)
    steps = (spacing, theta_step, phi_step)

    def flux_of_cells(parity, one, two, *given):
        def kernel(*refs):
            flux_kernel(steps, parity, *refs)

        return pl.pallas_call(
            kernel,
            in_specs=[VMEM] * (4 + len(given)),
            out_specs=VMEM,
            out_shape=tiles(9, LEVELS, CELLS_P, CELLS_T),
            input_output_aliases={4: 0} if given else {},
            compiler_params=limit(8),
            name="flux",
        )(held_vel, held_mag, one, two, *given)

    flux = flux_of_cells(0, one_even, two_even)
    first_full, last_full = pl.pallas_call(
        corners_kernel,
        in_specs=[VMEM] * 7,
        out_specs=[VMEM] * 2,
        out_shape=[strip_full, strip_full],
        compiler_params=limit(4),
        name="corners",
    )(one_even, two_even, first, last, before_even, after_even, flux)
    before_odd = along_lon(last_full, 1, evens)
    after_odd = along_lon(first_full, -1, evens)
    second_one, second_two = pl.pallas_call(
        second_kernel,
        in_specs=[VMEM] * 4,
        out_specs=[VMEM] * 2,
        out_shape=[pack, pack],
        compiler_params=limit(4),
        name="second",
    )(before_even, after_even, low, high)
    one_odd = between_lat(second_one, 0, range(lon_blocks))
    two_odd = between_lat(second_two, 1, range(lon_blocks))
    slots_total = send_cell.shape[-1]

    def donors(*refs):
        donors_kernel(lon_blocks, *refs)

    spots, factors = pl.pallas_call(
        donors,
        in_specs=[VMEM] * 3,
        out_specs=[VMEM] * 2,
        out_shape=[
            jax.ShapeDtypeStruct((8, slots_total), jnp.int32),
            tiles(CELLS_P // 8, 8, slots_total),
        ],
        compiler_params=limit(4),
        cost_estimate=pl.CostEstimate(flops=0, bytes_accessed=1, transcendentals=0),
        name="donors",
    )(pair_rows, send_cell, send_weight)

    def section(*refs):
        section_kernel(steps, lat_blocks, lon_blocks, *refs)

    flux = flux_of_cells(1, one_odd, two_odd, flux)
    new_velocity, new_magnetic, payload, _ = pl.pallas_call(
        section,
        in_specs=[VMEM] * 18,
        out_specs=[VMEM] * 4,
        out_shape=[
            tiles(*velocity.shape),
            tiles(*magnetic.shape),
            tiles(lon_blocks, 8, CELLS_T),
            tiles(9, LEVELS, CELLS_P, CELLS_T),
        ],
        input_output_aliases={17: 3},
        scratch_shapes=[
            pltpu.VMEM((5, CELLS_P, CELLS_T), F32),
            pltpu.VMEM((2, 5, LEVELS, CELLS_T), F32),
            pltpu.VMEM((8, LEVELS, slots_total), F32),
            pltpu.VMEM((2, 12, LEVELS, CELLS_T), F32),
        ],
        compiler_params=limit(16),
        name="section",
    )(
        held_vel,
        held_mag,
        low,
        high,
        one_even,
        two_even,
        one_odd,
        two_odd,
        first,
        last,
        before_even,
        after_even,
        before_odd,
        after_odd,
        spots,
        factors,
        cycle_slot,
        flux,
    )
    new_velocity, new_magnetic = pl.pallas_call(
        store_kernel,
        in_specs=[VMEM] * 2,
        out_specs=[HBM] * 2,
        out_shape=[tiles(*velocity.shape), tiles(*magnetic.shape)],
        scratch_shapes=[pltpu.SemaphoreType.DMA((2,))],
        compiler_params=limit(4),
        name="store",
    )(new_velocity, new_magnetic)
    pairs = lon_blocks // 2
    groups = [[2 * pair + parity for pair in range(pairs)] for parity in range(2)]
    payload = lax.all_to_all(
        payload.reshape(pairs, 16, CELLS_T),
        "lon",
        split_axis=0,
        concat_axis=0,
        axis_index_groups=groups,
        tiled=True,
    )
    near, far = pl.pallas_call(
        collect_kernel,
        in_specs=[VMEM],
        out_specs=[VMEM] * 2,
        out_shape=[tiles(1, 1, 1, 48, CYCLE)] * 2,
        compiler_params=limit(4),
        name="collect",
    )(payload)
    across = [
        (grid * lon_blocks + lon, (1 - grid) * lon_blocks + (lon ^ 1))
        for grid in range(2)
        for lon in range(lon_blocks)
    ]
    far = lax.ppermute(far, ("grid", "lon"), across)
    near = lax.ppermute(near, "grid", [(0, 1), (1, 0)])
    cycle = far + near
    return (new_velocity, new_magnetic, cycle)


def solution(mesh):
    state = P("grid", None, None, "lon", "lat")
    rows = P("grid", "lat", "lon", None)
    return jax.shard_map(
        local,
        mesh=mesh,
        in_specs=(state, state, rows, rows, rows, rows),
        out_specs=(state, state, P("grid", "lat", "lon", None, None)),
        check_vma=False,
    )
```

```python
import math

import jax
import jax.numpy as jnp
from jax import lax
from jax.experimental import pallas as pl
from jax.experimental.pallas import tpu as pltpu
from jax.sharding import PartitionSpec as P

CAP = 16
CYCLE = 128
LEVELS = 8
CELLS_P = 32
CELLS_T = 128

inner_radius = 0.6
smag_const = 0.2
aniso_weight = 0.8
turb_prandtl = 0.7
courant = 0.2

ALONG_R = (0, 1, 2, 7, 8)
ALONG_T = (1, 3, 4, 6, 8)
ALONG_P = (2, 4, 5, 6, 7)
F32 = jnp.float32


def lanes_of(shape):
    return lax.broadcasted_iota(jnp.int32, shape, len(shape) - 1)


def rows_of(shape):
    return lax.broadcasted_iota(jnp.int32, shape, len(shape) - 2)


def pick(vel_ref, mag_ref, comp):
    return (vel_ref, comp) if comp < 3 else (mag_ref, comp - 3)


def edges_kernel(
    vel_ref,
    mag_ref,
    low_ref,
    high_ref,
    first_ref,
    last_ref,
    one_ref,
    two_ref,
    held_vel_ref,
    held_mag_ref,
    sem_ref,
):
    copies = []
    for comp in range(6):
        ref, index = pick(vel_ref, mag_ref, comp)
        held, _ = pick(held_vel_ref, held_mag_ref, comp)
        copies.append(
            pltpu.make_async_copy(ref.at[0, index], held.at[0, index], sem_ref.at[comp])
        )
    for copy in copies:
        copy.start()
    pair = lanes_of((CELLS_P, CELLS_T)) // 2
    low = jnp.zeros((CELLS_P, CELLS_T), F32)
    high = jnp.zeros((CELLS_P, CELLS_T), F32)
    for comp in range(6):
        copies[comp].wait()
        ref, index = pick(held_vel_ref, held_mag_ref, comp)
        for level in range(LEVELS):
            place = 16 * comp + 2 * level
            block = ref[0, index, level]
            if place:
                block = pltpu.roll(block, place, 1)
            low = jnp.where(pair == place // 2, block, low)
            high = jnp.where(pair == (place // 2 - 1) % (CELLS_T // 2), block, high)
        first_ref[comp] = ref[0, index, :, 0, :]
        last_ref[comp] = ref[0, index, :, CELLS_P - 1, :]
        if comp < 5:
            first_ref[6 + comp] = ref[0, index, :, 1, :]
            last_ref[6 + comp] = ref[0, index, :, CELLS_P - 2, :]
    high = pltpu.roll(high, 2, 1)
    low_ref[...] = low
    high_ref[...] = high
    upward = lax.axis_index("lat") % 2 == 0
    one_ref[...] = jnp.where(upward, high, low)
    two_ref[...] = jnp.where(upward, low, high)


def below_above(one, two):
    upward = lax.axis_index("lat") % 2 == 0
    return jnp.where(upward, two, one), jnp.where(upward, one, two)


def corners_kernel(
    one_ref,
    two_ref,
    first_ref,
    last_ref,
    before_ref,
    after_ref,
    flux_ref,
    first_out_ref,
    last_out_ref,
):
    shape = (LEVELS, CELLS_T)
    for row, source, target in ((0, first_ref, first_out_ref), (CELLS_P - 1, last_ref, last_out_ref)):
        below, above = below_above(one_ref[row : row + 1, :], two_ref[row : row + 1, :])
        below = jnp.broadcast_to(below, shape)
        above = jnp.broadcast_to(above, shape)
        target[0:11] = source[...]
        target[11] = jnp.where(rows_of(shape) == 0, below, above)


def second_kernel(before_ref, after_ref, low_ref, high_ref, one_ref, two_ref):
    upward = lax.axis_index("lat") % 2 == 0

    odd = lax.axis_index("lon") % 2

    @pl.when(odd == 1)
    def _():
        one_ref[...] = jnp.where(upward, high_ref[...], low_ref[...])
        two_ref[...] = jnp.where(upward, low_ref[...], high_ref[...])

    @pl.when(odd == 0)
    def _():
        lane = lanes_of((LEVELS, CELLS_T))
        low = jnp.zeros((LEVELS, CELLS_T), F32)
        high = jnp.zeros((LEVELS, CELLS_T), F32)
        for side, ref in ((0, before_ref), (1, after_ref)):
            for comp in range(6):
                spot = 6 * side + comp
                block = ref[comp]
                low = jnp.where(lane == spot, pltpu.roll(block, spot, 1) if spot else block, low)
                high = jnp.where(lane == spot, pltpu.roll(block, spot + 1, 1), high)
        one_ref[0:LEVELS] = jnp.where(upward, high, low)
        two_ref[0:LEVELS] = jnp.where(upward, low, high)
        one_ref[LEVELS:] = jnp.zeros((CELLS_P - LEVELS, CELLS_T), F32)
        two_ref[LEVELS:] = jnp.zeros((CELLS_P - LEVELS, CELLS_T), F32)


def flux_of(center, grad_r, grad_t, grad_p, spacing, wanted):
    u0, u1, u2, b0, b1, b2 = center
    s00, s11, s22 = grad_r[0], grad_t[1], grad_p[2]
    d01 = grad_t[0] + grad_r[1]
    d02 = grad_p[0] + grad_r[2]
    d12 = grad_p[1] + grad_t[2]
    squares = 2.0 * (s00 * s00 + s11 * s11 + s22 * s22) + (d01 * d01 + d02 * d02 + d12 * d12)
    viscous = jnp.sqrt(squares) * ((smag_const * spacing) ** 2)
    q00, q11, q22 = b0 * b0, b1 * b1, b2 * b2
    field_sq = q00 + q11 + q22
    inverse = 1.0 / (field_sq + 1.0)
    q01, q02, q12 = b0 * b1, b0 * b2, b1 * b2
    aligned = q00 * s00 + q11 * s11 + q22 * s22 + (q01 * d01 + q02 * d02 + q12 * d12)
    weight = (2.0 * aniso_weight) * viscous * aligned * inverse * inverse - 1.0
    half = 0.5 * field_sq
    twice = viscous + viscous
    ratio = viscous * (1.0 / turb_prandtl)
    result = {}
    for chan in wanted:
        if chan == 0:
            result[0] = u0 * u0 + q00 * weight - twice * s00 + half
        elif chan == 1:
            result[1] = u0 * u1 + q01 * weight - viscous * d01
        elif chan == 2:
            result[2] = u0 * u2 + q02 * weight - viscous * d02
        elif chan == 3:
            result[3] = u1 * u1 + q11 * weight - twice * s11 + half
        elif chan == 4:
            result[4] = u1 * u2 + q12 * weight - viscous * d12
        elif chan == 5:
            result[5] = u2 * u2 + q22 * weight - twice * s22 + half
        elif chan == 6:
            result[6] = u1 * b2 - u2 * b1 - ratio * (grad_t[5] - grad_p[4])
        elif chan == 7:
            result[7] = u2 * b0 - u0 * b2 - ratio * (grad_p[3] - grad_r[5])
        else:
            result[8] = u0 * b1 - u1 * b0 - ratio * (grad_r[4] - grad_t[3])
    return result


def radius(level, spacing):
    return inner_radius + (level.astype(F32) + 0.5) * spacing


def inverse_sine(index, theta_step):
    return 1.0 / jnp.sin(0.25 * math.pi + (index.astype(F32) + 0.5) * theta_step)


def level_steps(level, sine, steps, scale):
    spacing, theta_step, phi_step = steps
    low_level = jnp.maximum(level - 1, 0)
    high_level = jnp.minimum(level + 1, LEVELS - 1)
    ends = (level == 0) | (level == LEVELS - 1)
    step_r = jnp.where(ends, scale / spacing, 0.5 * scale / spacing)
    inverse = 1.0 / radius(jnp.full((8, CELLS_T), level, jnp.int32), spacing)
    step_t = (inverse * (0.5 * scale / theta_step))[0:1]
    step_p = (sine * inverse * (0.5 * scale / phi_step))[0:1]
    return low_level, high_level, step_r, step_t, step_p


def along_t(block, ends, step):
    lane = lanes_of(block.shape)
    up = jnp.where(lane == CELLS_T - 1, ends, pltpu.roll(block, CELLS_T - 1, 1))
    down = jnp.where(lane == 0, ends, pltpu.roll(block, 1, 1))
    return (up - down) * step


def flux_kernel(steps, parity, vel_ref, mag_ref, one_ref, two_ref, *rest):
    flux_ref = rest[-1]
    wide = (CELLS_P, CELLS_T)

    @pl.when(lax.axis_index("lon") % 2 == parity)
    def _():
        is_below = lanes_of(wide) % 2 == 1
        below, above = below_above(one_ref[...], two_ref[...])
        beside = jnp.where(is_below, below, above)
        own_sine = inverse_sine(lax.axis_index("lat") * CELLS_T + lanes_of((8, CELLS_T)), steps[1])

        def make_flux(level, carry):
            low_level, high_level, step_r, step_t, step_p = level_steps(level, own_sine, steps, 1.0)
            center, grad_r, grad_t, grad_p = [], [], [], []
            for comp in range(6):
                ref, index = pick(vel_ref, mag_ref, comp)
                block = ref[0, index, level]
                center.append(block)
                grad_r.append((ref[0, index, high_level] - ref[0, index, low_level]) * step_r)
                ends = pltpu.roll(beside, 2 * CELLS_T - 1 - 16 * comp - 2 * level, 1)
                grad_t.append(along_t(block, ends, step_t))
                gap = pltpu.roll(block, CELLS_P - 1, 0) - pltpu.roll(block, 1, 0)
                grad_p.append(gap * step_p)
            flux = flux_of(center, grad_r, grad_t, grad_p, steps[0], range(9))
            for chan in range(9):
                flux_ref[chan, level] = flux[chan]
            return carry

        lax.fori_loop(0, LEVELS, make_flux, 0, unroll=8)


def section_kernel(
    steps,
    lat_blocks,
    lon_blocks,
    vel_ref,
    mag_ref,
    low_ref,
    high_ref,
    one_even_ref,
    two_even_ref,
    one_odd_ref,
    two_odd_ref,
    first_ref,
    last_ref,
    before_even_ref,
    after_even_ref,
    before_odd_ref,
    after_odd_ref,
    spot_ref,
    factor_ref,
    slot_ref,
    flux_in_ref,
    new_vel_ref,
    new_mag_ref,
    send_ref,
    flux_ref,
    edge_t_ref,
    edge_p_ref,
    taken_ref,
    side_ref,
):
    spacing, theta_step, phi_step = steps
    lat = lax.axis_index("lat")
    lon = lax.axis_index("lon")
    odd_block = lon % 2 == 1
    time_step = courant * spacing
    wide = (CELLS_P, CELLS_T)
    flat = (LEVELS, CELLS_T)
    lane = lanes_of(wide)
    row = rows_of(wide)
    lane_flat = lanes_of(flat)
    row_flat = rows_of(flat)
    first_row, last_row = row == 0, row == CELLS_P - 1
    first_t = lat * CELLS_T
    own_sine = inverse_sine(first_t + lanes_of((8, CELLS_T)), theta_step)

    @pl.when(odd_block)
    def _():
        side_ref[0] = before_odd_ref[...]
        side_ref[1] = after_odd_ref[...]

    @pl.when(jnp.logical_not(odd_block))
    def _():
        side_ref[0, 0:11] = before_even_ref[...]
        side_ref[1, 0:11] = after_even_ref[...]
        side_ref[:, 11] = jnp.zeros((2, LEVELS, CELLS_T), F32)

    is_below = lane % 2 == 1
    level_of = (lane % 16) // 2
    first_below, first_above = below_above(one_even_ref[...], two_even_ref[...])
    second_below, second_above = below_above(one_odd_ref[...], two_odd_ref[...])
    below = jnp.where(odd_block, second_below, first_below)
    above = jnp.where(odd_block, second_above, first_above)
    beside = jnp.where(is_below, below, above)

    def swapped(block):
        return jnp.where(is_below, pltpu.roll(block, 1, 1), pltpu.roll(block, CELLS_T - 1, 1))

    def corner(side):
        tile = side_ref[side, 11]
        held = jnp.where(lane_flat[0:1] % 2 == 1, tile[0:1], tile[1:2])
        spot = 2 * row_flat
        total = jnp.zeros(flat, F32)
        for comp in range(6):
            start = 6 * side + comp
            for block, shift in ((second_below, 1), (second_above, 0)):
                column = block[0:LEVELS, start : start + 1]
                total = jnp.where(lane_flat == spot + (16 * comp + shift), column, total)
        return jnp.where(odd_block, held, jnp.sum(total, axis=0, keepdims=True))

    corners = (corner(0), corner(1))
    inverse_r = 1.0 / radius(level_of, spacing)
    own_step = jnp.where((level_of == 0) | (level_of == LEVELS - 1), 1.0 / spacing, 0.5 / spacing)
    up = jnp.where(level_of == LEVELS - 1, beside, pltpu.roll(beside, CELLS_T - 2, 1))
    down = jnp.where(level_of == 0, beside, pltpu.roll(beside, 2, 1))
    pack_r = (up - down) * own_step
    inner = jnp.where(is_below, high_ref[...], low_ref[...])
    outer = jnp.where(is_below, above, below)
    pack_t = swapped(inner - outer) * (
        jnp.where(is_below, 0.5 / theta_step, -0.5 / theta_step) * inverse_r
    )
    t_index = first_t + jnp.where(is_below[0:8], -1, CELLS_T)
    edge_sine = inverse_sine(t_index, theta_step)[0:1]
    up = jnp.where(last_row, corners[1], pltpu.roll(beside, CELLS_P - 1, 0))
    down = jnp.where(first_row, corners[0], pltpu.roll(beside, 1, 0))
    pack_p = (up - down) * (edge_sine * inverse_r * (0.5 / phi_step))

    def spread(block):
        return [block if comp == 0 else pltpu.roll(block, CELLS_T - 16 * comp, 1) for comp in range(6)]

    edge = flux_of(
        spread(beside), spread(pack_r), spread(pack_t), spread(pack_p), spacing, ALONG_T
    )
    outside = (is_below & (lat == 0)) | ((lane % 2 == 0) & (lat == lat_blocks - 1))
    for slot, chan in enumerate(ALONG_T):
        edge_t_ref[slot] = jnp.where(outside, 0.0, edge[chan])

    level_step = jnp.where(
        (row_flat == 0) | (row_flat == LEVELS - 1), 1.0 / spacing, 0.5 / spacing
    )
    inverse_flat = 1.0 / radius(row_flat, spacing)
    step_t = inverse_flat * (0.5 / theta_step)
    step_p = own_sine * inverse_flat * (0.5 / phi_step)
    for kind in range(4):
        side, own = kind % 2, kind // 2 == 1
        edge_row_ref = first_ref if side == 0 else last_ref
        if own:
            center = [edge_row_ref[comp] for comp in range(6)]
            near = [side_ref[side, comp] for comp in range(5)]
            away = [edge_row_ref[6 + comp] for comp in range(5)]
            start = 0 if side == 0 else CELLS_P - 1
            ends = beside[start : start + 1]
        else:
            center = [side_ref[side, comp] for comp in range(6)]
            near = [side_ref[side, 6 + comp] for comp in range(5)]
            away = [edge_row_ref[comp] for comp in range(5)]
            ends = corners[side]
        ends = jnp.broadcast_to(ends, flat)
        grad_r, grad_t, grad_p = [], [], []
        for comp in range(6):
            block = center[comp]
            up = jnp.where(row_flat == LEVELS - 1, block, pltpu.roll(block, LEVELS - 1, 0))
            down = jnp.where(row_flat == 0, block, pltpu.roll(block, 1, 0))
            grad_r.append((up - down) * level_step)
            spot = 16 * comp + 2 * row_flat
            before = jnp.sum(jnp.where(lane_flat == spot + 1, ends, 0.0), axis=1, keepdims=True)
            after = jnp.sum(jnp.where(lane_flat == spot, ends, 0.0), axis=1, keepdims=True)
            up = jnp.where(lane_flat == CELLS_T - 1, after, pltpu.roll(block, CELLS_T - 1, 1))
            down = jnp.where(lane_flat == 0, before, pltpu.roll(block, 1, 1))
            grad_t.append((up - down) * step_t)
            if comp < 5:
                gap = away[comp] - near[comp] if side == 0 else near[comp] - away[comp]
                grad_p.append(gap * step_p)
            else:
                grad_p.append(None)
        if own:
            edge = flux_of(center, grad_r, grad_t, grad_p, spacing, range(9))
            for chan in range(9):
                flux_ref[chan, :, 0 if side == 0 else CELLS_P - 1, :] = edge[chan]
        else:
            edge = flux_of(center, grad_r, grad_t, grad_p, spacing, ALONG_P)
            outside = lon == (0 if side == 0 else lon_blocks - 1)
            for slot, chan in enumerate(ALONG_P):
                edge_p_ref[side, slot] = jnp.where(outside, 0.0, edge[chan])

    def along_p(block, before, after, step):
        up = jnp.where(last_row, after, pltpu.roll(block, CELLS_P - 1, 0))
        down = jnp.where(first_row, before, pltpu.roll(block, 1, 0))
        return (up - down) * step

    def advance(level, carry):
        low_level, high_level, step_r, step_t, step_p = level_steps(
            level, own_sine, steps, time_step
        )

        def d_r(chan):
            return (flux_ref[chan, high_level] - flux_ref[chan, low_level]) * step_r

        def d_t(chan):
            slot = ALONG_T.index(chan)
            ends = pltpu.roll(edge_t_ref[slot], CELLS_T - 1 - 2 * level, 1)
            return along_t(flux_ref[chan, level], ends, step_t)

        def d_p(chan):
            slot = ALONG_P.index(chan)
            before = edge_p_ref[0, slot, pl.ds(level, 1), :]
            after = edge_p_ref[1, slot, pl.ds(level, 1), :]
            return along_p(flux_ref[chan, level], before, after, step_p)

        new_vel_ref[0, 0, level] = vel_ref[0, 0, level] - (d_r(0) + d_t(1) + d_p(2))
        new_vel_ref[0, 1, level] = vel_ref[0, 1, level] - (d_r(1) + d_t(3) + d_p(4))
        new_vel_ref[0, 2, level] = vel_ref[0, 2, level] - (d_r(2) + d_t(4) + d_p(5))
        new_mag_ref[0, 0, level] = mag_ref[0, 0, level] + (d_t(8) - d_p(7))
        new_mag_ref[0, 1, level] = mag_ref[0, 1, level] + (d_p(6) - d_r(8))
        new_mag_ref[0, 2, level] = mag_ref[0, 2, level] + (d_r(7) - d_t(6))
        return carry

    lax.fori_loop(0, LEVELS, advance, 0, unroll=8)

    slots_total = spot_ref.shape[-1]
    chunks = slots_total // CELLS_T
    taken_ref[6:8] = jnp.zeros((2, LEVELS, slots_total), F32)
    taken_ref[6, 0:1] = slot_ref[0, 0].astype(F32)
    sub = rows_of((8, CELLS_T))

    def fold(blocks):
        for width in (4, 2, 1):
            keep = sub % (2 * width) < width
            half = len(blocks) // 2
            merged = []
            for one, two in zip(blocks[:half], blocks[half:]):
                mine, other = jnp.where(keep, one, two), jnp.where(keep, two, one)
                moved = pltpu.roll(other, width, 0)
                if width < 4:
                    moved = jnp.where(keep, pltpu.roll(other, 8 - width, 0), moved)
                merged.append(mine + moved)
            blocks = merged
        return blocks[0]

    for chunk in range(chunks):
        part = slice(chunk * CELLS_T, (chunk + 1) * CELLS_T)
        where_t = spot_ref[:, part]
        weights = [factor_ref[step, :, part] for step in range(CELLS_P // 8)]
        for start, ref in ((0, new_vel_ref), (3, new_mag_ref)):

            def take(comp, carry, start=start, ref=ref, part=part, where_t=where_t, weights=weights):
                sums = []
                for level in range(LEVELS):
                    block = ref[0, comp, level]
                    total = 0.0
                    for step in range(CELLS_P // 8):
                        got = jnp.take_along_axis(
                            block[8 * step : 8 * step + 8],
                            where_t,
                            axis=1,
                            mode="promise_in_bounds",
                        )
                        total = total + got * weights[step]
                    sums.append(total)
                taken_ref[start + comp, :, part] = fold(sums)

            for comp in range(3):
                take(comp, 0)

    for chunk in range(chunks):
        part = taken_ref[:, :, chunk * CELLS_T : (chunk + 1) * CELLS_T].reshape(64, CELLS_T)
        both = jnp.concatenate([part, pltpu.roll(part, CELLS_T - 8, 1)], axis=0)
        turned = jnp.transpose(both)
        for block in range(8):
            send_ref[chunk * 8 + block] = turned[16 * block : 16 * block + 8]


def store_kernel(vel_ref, mag_ref, out_vel_ref, out_mag_ref, sem_ref):
    copies = [
        pltpu.make_async_copy(vel_ref, out_vel_ref, sem_ref.at[0]),
        pltpu.make_async_copy(mag_ref, out_mag_ref, sem_ref.at[1]),
    ]
    for copy in copies:
        copy.start()
    for copy in copies:
        copy.wait()


def donors_kernel(lon_blocks, rows_ref, cell_ref, weight_ref, spot_ref, factor_ref):
    slots_total = cell_ref.shape[-1]
    rows_wide = jnp.broadcast_to(rows_ref[0, 0].astype(F32), (8, lon_blocks))
    owner = lanes_of((lon_blocks, slots_total)) // CAP == rows_of((lon_blocks, slots_total))
    counts = jnp.dot(rows_wide, owner.astype(F32), preferred_element_type=F32)
    bucket = lanes_of((8, slots_total)) % CAP
    live = bucket < (counts + 0.5).astype(jnp.int32)
    scale = jnp.where(live, jnp.broadcast_to(weight_ref[0, 0], (8, slots_total)), 0.0)
    cells = jnp.broadcast_to(cell_ref[0, 0], (8, slots_total))
    spot_ref[...] = cells % CELLS_T
    cell_p = cells // CELLS_T
    for step in range(CELLS_P // 8):
        factor_ref[step] = jnp.where(cell_p == 8 * step + rows_of(cells.shape), scale, 0.0)


def collect_kernel(got_ref, near_ref, far_ref):
    sources = got_ref.shape[0]
    rows = sources * 8
    totals = []
    for half in range(2):
        got = got_ref[:, 8 * half : 8 * half + 8].reshape(rows, CELLS_T)
        onehots = []
        for start in (0, 64):
            slot = got[:, start + 48 : start + 49].astype(jnp.int32)
            onehots.append((slot == lanes_of((rows, CYCLE))).astype(F32))
        both = lax.dot_general(
            got,
            jnp.concatenate(onehots, axis=1),
            (((0,), (0,)), ((), ())),
            precision=lax.Precision.HIGHEST,
            preferred_element_type=F32,
        )
        total = both[0:48, 0:CYCLE] + both[64:112, CYCLE:]
        totals.append(total)
    odd = lax.axis_index("lon") % 2 == 1
    near_ref[0, 0, 0] = jnp.where(odd, totals[1], totals[0])
    far_ref[0, 0, 0] = jnp.where(odd, totals[0], totals[1])


VMEM = pl.BlockSpec(memory_space=pltpu.VMEM)
HBM = pl.BlockSpec(memory_space=pltpu.HBM)


def limit(mebibytes):
    return pltpu.CompilerParams(vmem_limit_bytes=mebibytes * 1024 * 1024)


def tiles(*shape):
    return jax.ShapeDtypeStruct(shape, F32)


def local(velocity, magnetic, pair_rows, send_cell, send_weight, cycle_slot):
    lat_blocks, lon_blocks = lax.axis_size("lat"), lax.axis_size("lon")
    theta_step = 0.5 * math.pi / (lat_blocks * CELLS_T)
    phi_step = 1.5 * math.pi / (lon_blocks * CELLS_P)
    spacing = inner_radius * theta_step
    pack = tiles(CELLS_P, CELLS_T)
    strip = tiles(11, LEVELS, CELLS_T)
    strip_full = tiles(12, LEVELS, CELLS_T)
    evens, odds = range(0, lon_blocks, 2), range(1, lon_blocks, 2)

    def along_lon(block, step, lons):
        pairs = [(lon, lon + step) for lon in lons if 0 <= lon + step < lon_blocks]
        return lax.ppermute(block, "lon", pairs)

    def between_lat(block, start, lons):
        pairs = [
            (lat * lon_blocks + lon, other * lon_blocks + lon)
            for first_lat in range(start, lat_blocks - 1, 2)
            for lat, other in ((first_lat, first_lat + 1), (first_lat + 1, first_lat))
            for lon in lons
        ]
        return lax.ppermute(block, ("lat", "lon"), pairs)

    low, high, first, last, one, two, held_vel, held_mag = pl.pallas_call(
        edges_kernel,
        in_specs=[HBM] * 2,
        out_specs=[VMEM] * 8,
        out_shape=[
            pack,
            pack,
            strip,
            strip,
            pack,
            pack,
            tiles(*velocity.shape),
            tiles(*magnetic.shape),
        ],
        scratch_shapes=[
            pltpu.SemaphoreType.DMA((6,)),
        ],
        compiler_params=limit(4),
        name="edges",
    )(*(pltpu.with_memory_space_constraint(array, pltpu.HBM) for array in (velocity, magnetic)))
    one_even = between_lat(one, 0, evens)
    two_even = between_lat(two, 1, evens)
    before_even = along_lon(last, 1, odds)
    after_even = along_lon(first, -1, odds)
    steps = (spacing, theta_step, phi_step)

    def flux_of_cells(parity, one, two, *given):
        def kernel(*refs):
            flux_kernel(steps, parity, *refs)

        return pl.pallas_call(
            kernel,
            in_specs=[VMEM] * (4 + len(given)),
            out_specs=VMEM,
            out_shape=tiles(9, LEVELS, CELLS_P, CELLS_T),
            input_output_aliases={4: 0} if given else {},
            compiler_params=limit(8),
            name="flux",
        )(held_vel, held_mag, one, two, *given)

    flux = flux_of_cells(0, one_even, two_even)
    first_full, last_full = pl.pallas_call(
        corners_kernel,
        in_specs=[VMEM] * 7,
        out_specs=[VMEM] * 2,
        out_shape=[strip_full, strip_full],
        compiler_params=limit(4),
        name="corners",
    )(one_even, two_even, first, last, before_even, after_even, flux)
    before_odd = along_lon(last_full, 1, evens)
    after_odd = along_lon(first_full, -1, evens)
    second_one, second_two = pl.pallas_call(
        second_kernel,
        in_specs=[VMEM] * 4,
        out_specs=[VMEM] * 2,
        out_shape=[pack, pack],
        compiler_params=limit(4),
        name="second",
    )(before_even, after_even, low, high)
    one_odd = between_lat(second_one, 0, range(lon_blocks))
    two_odd = between_lat(second_two, 1, range(lon_blocks))
    slots_total = send_cell.shape[-1]

    def donors(*refs):
        donors_kernel(lon_blocks, *refs)

    spots, factors = pl.pallas_call(
        donors,
        in_specs=[VMEM] * 3,
        out_specs=[VMEM] * 2,
        out_shape=[
            jax.ShapeDtypeStruct((8, slots_total), jnp.int32),
            tiles(CELLS_P // 8, 8, slots_total),
        ],
        compiler_params=limit(4),
        cost_estimate=pl.CostEstimate(flops=0, bytes_accessed=1, transcendentals=0),
        name="donors",
    )(pair_rows, send_cell, send_weight)

    def section(*refs):
        section_kernel(steps, lat_blocks, lon_blocks, *refs)

    flux = flux_of_cells(1, one_odd, two_odd, flux)
    new_velocity, new_magnetic, payload, _ = pl.pallas_call(
        section,
        in_specs=[VMEM] * 18,
        out_specs=[VMEM] * 4,
        out_shape=[
            tiles(*velocity.shape),
            tiles(*magnetic.shape),
            tiles(lon_blocks, 8, CELLS_T),
            tiles(9, LEVELS, CELLS_P, CELLS_T),
        ],
        input_output_aliases={17: 3},
        scratch_shapes=[
            pltpu.VMEM((5, CELLS_P, CELLS_T), F32),
            pltpu.VMEM((2, 5, LEVELS, CELLS_T), F32),
            pltpu.VMEM((8, LEVELS, slots_total), F32),
            pltpu.VMEM((2, 12, LEVELS, CELLS_T), F32),
        ],
        compiler_params=limit(16),
        name="section",
    )(
        held_vel,
        held_mag,
        low,
        high,
        one_even,
        two_even,
        one_odd,
        two_odd,
        first,
        last,
        before_even,
        after_even,
        before_odd,
        after_odd,
        spots,
        factors,
        cycle_slot,
        flux,
    )
    new_velocity, new_magnetic = pl.pallas_call(
        store_kernel,
        in_specs=[VMEM] * 2,
        out_specs=[HBM] * 2,
        out_shape=[tiles(*velocity.shape), tiles(*magnetic.shape)],
        scratch_shapes=[pltpu.SemaphoreType.DMA((2,))],
        compiler_params=limit(4),
        name="store",
    )(new_velocity, new_magnetic)
    pairs = lon_blocks // 2
    groups = [[2 * pair + parity for pair in range(pairs)] for parity in range(2)]
    payload = lax.all_to_all(
        payload.reshape(pairs, 16, CELLS_T),
        "lon",
        split_axis=0,
        concat_axis=0,
        axis_index_groups=groups,
        tiled=True,
    )
    near, far = pl.pallas_call(
        collect_kernel,
        in_specs=[VMEM],
        out_specs=[VMEM] * 2,
        out_shape=[tiles(1, 1, 1, 48, CYCLE)] * 2,
        compiler_params=limit(4),
        name="collect",
    )(payload)
    across = [
        (grid * lon_blocks + lon, (1 - grid) * lon_blocks + (lon ^ 1))
        for grid in range(2)
        for lon in range(lon_blocks)
    ]
    far = lax.ppermute(far, ("grid", "lon"), across)
    near = lax.ppermute(near, "grid", [(0, 1), (1, 0)])
    cycle = far + near
    return (new_velocity, new_magnetic, cycle)


def solution(mesh):
    state = P("grid", None, None, "lon", "lat")
    rows = P("grid", "lat", "lon", None)
    return jax.shard_map(
        local,
        mesh=mesh,
        in_specs=(state, state, rows, rows, rows, rows),
        out_specs=(state, state, P("grid", "lat", "lon", None, None)),
        check_vma=False,
    )
```
